256 devices in a mesh: dom: 16 (over z, core), tile: 16 (over x, y).
Axes of the slice: x: 4, y: 4, z: 8, core: 2. Of those that a mesh axis runs over, the one named last changes fastest.
Arguments:
- members: float32 [256, 4, 128, 384], P('dom', None, 'tile'), may hold values from -6 to 6
- noise: float32 [2, 256, 4, 128, 384], P(None, 'dom', None, 'tile'), may hold values from -4 to 4
- courant: float32 [2, 128, 384], P(None, 'tile'), may hold values from -0.35 to 0.35
- diffusion: float32 [4, 128, 384], P(None, 'tile'), may hold values from 0.02 to 0.07
- obs_loc: int32 [16, 64], P('tile'), may hold values from 0 to 3071
- observed: float32 [2, 16, 64], P(None, 'tile'), may hold values from -6 to 6
- obs_var: float32 [16, 64], P('tile'), may hold values from 0.1 to 1
- ancestors: int32 [2, 16, 256], P(None, 'tile'), may hold values from 0 to 255, as said below
Outputs:
- ensemble: float32 [256, 4, 128, 384], P('dom', None, 'tile')
- averages: float32 [2, 4, 128, 384], P(None, None, 'tile')
The draws below stay inside these ranges and needn't reach their ends.
Inputs may be any that keep to these rules, and one draw needn't show every extreme that they name: `ancestors`: for every cycle, tile and group of 16 consecutive new particles, at most 2 of them descend from particles of one group of 16 consecutive old particles, and some group of old particles gives exactly 2.
All inputs are finite; a program needn't handle non-finite values.
Results may differ from the reference program's by a relative error of at most 0.0003.
Values sent between devices are 32-bit elements; how exact they have to be, the bound alone decides.
A program may use at most 64 MiB of HBM per device.

```python
import math
import jax
import jax.numpy as jnp
from jax import lax

FIELDS = 4
P_DEV = 16
ROWS = 8
NY = 384
NOBS = 64
STEPS = 4
CYCLES = 2
CAP = 2
P_SIZE = 256
NT = 16
NX = 128


def draw_ancestors(key, part):
    key = jax.random.fold_in(key, 7)
    groups = P_SIZE // P_DEV
    slot_count = groups * CAP

    def one_list(list_key):
        key_ranks, key_forced, key_local, key_shuffle = jax.random.split(list_key, 4)
        ranks = jax.random.permutation(key_ranks, slot_count).astype(jnp.int32)
        slot_ids = jnp.arange(slot_count, dtype=jnp.int32)
        slot_owner = slot_ids // CAP
        forced_source = jax.random.randint(key_forced, (), 0, groups).astype(jnp.int32)
        slot_score = jnp.where(slot_owner == forced_source, slot_ids % CAP - CAP, ranks)
        chosen_slots = jnp.argsort(slot_score, stable=True)[:P_DEV]
        source = slot_owner[chosen_slots]
        member_local = jax.random.randint(key_local, (P_DEV,), 0, P_DEV).astype(jnp.int32)
        lineage = source * P_DEV + member_local
        return lineage[jax.random.permutation(key_shuffle, P_DEV)]
    key_list = jax.random.split(key, CYCLES * NT * groups)
    lineage = jax.vmap(one_list)(key_list)
    return lineage.reshape(CYCLES, NT, P_SIZE).astype(jnp.int32)


def plant(values, stream_key, least, high):
    spot = [jax.random.randint(jax.random.fold_in(stream_key, axis), (), 0, length) for axis, length in enumerate(values.shape)]
    widest = values.shape.index(max(values.shape))
    beside = spot[:widest] + [(spot[widest] + 1) % values.shape[widest]] + spot[widest + 1:]
    return values.at[tuple(spot)].set(least).at[tuple(beside)].set(high)


def steps_of(own_key, shape, cuts, low, largest):
    gain = 1.0
    for axis_at, parts in cuts:
        draws = jax.random.uniform(jax.random.fold_in(jax.random.fold_in(own_key, 6), axis_at), (parts,), jnp.float32, low / len(cuts), largest / len(cuts))
        gain = gain * jnp.repeat(jnp.exp(draws), shape[axis_at] // parts).reshape((-1,) + (1,) * (len(shape) - 1 - axis_at))
    return gain


def centred(own_key, extent, deviation, bound, pieces=(), kind=jnp.bfloat16):
    gain = steps_of(own_key, extent, pieces, -0.22, 0.18) if pieces else 1.0
    entries = jax.random.normal(own_key, extent, jnp.float32) * deviation * gain
    return jnp.minimum(jnp.maximum(entries, -bound), bound).astype(kind)


def setup_inputs(seed: int = 0) -> dict:
    keys = jax.random.split(jax.random.key(seed), 9)
    return {
        "members": centred(keys[0], (P_SIZE, FIELDS, NX, NY), 1.0, 6.0, ((0, 16), (2, 16)), jnp.float32),
        "noise": centred(keys[1], (CYCLES, P_SIZE, FIELDS, NX, NY), 0.3, 4.0, ((1, 16), (3, 16)), jnp.float32),
        "courant": jnp.clip(jax.random.uniform(keys[2], (2, NX, NY), jnp.float32, -0.35, 0.35) * steps_of(keys[2], (2, NX, NY), ((1, 16),), -0.4, 0.0), -0.35, 0.35),
        "diffusion": jnp.clip(0.02 + 0.05 * jax.random.uniform(keys[3], (FIELDS, NX, NY), jnp.float32) ** steps_of(keys[3], (FIELDS, NX, NY), ((1, 16),), -0.2, 0.2), 0.02, 0.07),
        "obs_loc": plant(jax.random.randint(keys[4], (NT, NOBS), 0, ROWS * NY), jax.random.fold_in(keys[4], 1), 0, (ROWS * NY) - 1).astype(jnp.int32),
        "observed": centred(keys[5], (CYCLES, NT, NOBS), 1.0, 6.0, ((1, 16),), jnp.float32),
        "obs_var": jnp.clip(jnp.exp(math.log(1.0) - 2.3025851 * jax.random.uniform(keys[6], (NT, NOBS), jnp.float32) ** steps_of(keys[6], (NT, NOBS), ((0, 16),), -0.2, 0.2)), 0.1, 1.0),
        "ancestors": draw_ancestors(jax.random.fold_in(keys[8], 71), 0),
    }


def advance(fields, courant, diffusion):
    padded = jnp.pad(fields, ((0, 0), (0, 0), (1, 1), (1, 1)))
    northern = padded[:, :, :-2, 1:-1]
    southern = padded[:, :, 2:, 1:-1]
    western = padded[:, :, 1:-1, :-2]
    eastern = padded[:, :, 1:-1, 2:]
    along_x = courant[0]
    along_y = courant[1]
    transport = (jnp.maximum(along_x, 0.0) * (fields - northern) + jnp.minimum(along_x, 0.0) * (southern - fields)
                 + jnp.maximum(along_y, 0.0) * (fields - western) + jnp.minimum(along_y, 0.0) * (eastern - fields))
    laplace_sum = northern + southern + western + eastern - 4.0 * fields
    return fields - transport + diffusion * laplace_sum


def pick_tile(block_tile, lineage):
    return block_tile[lineage]


def reference(members, noise, courant, diffusion, obs_loc, observed, obs_var, ancestors):
    fields = members
    averages = []
    for cycle_index in range(CYCLES):
        fields = fields + noise[cycle_index]
        for step_index in range(STEPS):
            fields = advance(fields, courant, diffusion)
        tile_rows = fields[:, 0].reshape(P_SIZE, NT, ROWS * NY)
        predicted = jnp.take_along_axis(tile_rows, obs_loc[None].astype(jnp.int32), axis=2)
        misfit = observed[cycle_index][None] - predicted
        log_likelihood = -0.5 * jnp.sum(misfit * misfit / obs_var[None], axis=2)
        peak_value = jnp.max(log_likelihood, axis=0)
        shifted = jnp.exp(log_likelihood - peak_value[None])
        weight = shifted / jnp.sum(shifted, axis=0)[None]
        row_weights = jnp.repeat(weight, ROWS, axis=1)
        average = jnp.einsum('pn,pfnm->fnm', row_weights, fields, precision=lax.Precision.HIGHEST)
        averages.append(average)
        blocks = fields.reshape(P_SIZE, FIELDS, NT, ROWS, NY)
        chosen = jax.vmap(pick_tile, in_axes=(2, 0), out_axes=2)(blocks, ancestors[cycle_index])
        fields = chosen.reshape(P_SIZE, FIELDS, NX, NY)
    return fields, jnp.stack(averages)
```

```python
import functools

import jax
import jax.numpy as jnp
from jax import lax
from jax.experimental import pallas as pl
from jax.experimental.pallas import tpu as pltpu
from jax.sharding import PartitionSpec as P

MESH = pl.DeviceIdType.MESH
STEPS = 4
CYCLES = 2
FIELDS = 4
PER = 16
GROUPS = 16
TILES = 16
ROWS = 8
COLS = 384
NOBS = 64
CAP = 2
STAGES = CYCLES * FIELDS


def half_turn(x):
    return pltpu.roll(x, 4, axis=0)


def kernel(members, noise, courant, diffusion, obs_loc, observed, obs_var, ancestors, out, averages, *scratch):
    scratch = list(scratch)
    send = [scratch.pop(0) for _ in range(STAGES)]
    recv = [scratch.pop(0) for _ in range(STAGES)]
    (to_north, to_south, from_north, from_south, state, result, raw, raw_north, raw_south, coef, obs_weight, obs_mean,
     obs_rest, partial, likely, weights, like_send, like_recv, part_send, part_recv, mean_send, mean_recv,
     send_table, recv_table, sem_out, sem_in, sem_halo_out, sem_halo_in, sem_raw_out, sem_raw_in, sem_small_out,
     sem_small_in) = scratch
    me = lax.axis_index("dom")
    tile = lax.axis_index("tile")
    north = lax.rem(tile + TILES - 1, TILES)
    south = lax.rem(tile + 1, TILES)

    def peer(step):
        return lax.rem(me + step, GROUPS)

    barrier = pltpu.get_barrier_semaphore()

    def greet(step, carry):
        pl.semaphore_signal(barrier, inc=1, device_id={"dom": peer(step)}, device_id_type=MESH)
        return carry

    lax.fori_loop(1, GROUPS, greet, 0)
    for neighbour in (north, south):
        pl.semaphore_signal(barrier, inc=1, device_id={"tile": neighbour}, device_id_type=MESH)

    upper = lax.broadcasted_iota(jnp.int32, (ROWS, COLS), 0) < 4
    column = lax.broadcasted_iota(jnp.int32, (ROWS, COLS), 1)
    has_north = jnp.where(tile > 0, 1.0, 0.0).astype(jnp.float32)
    has_south = jnp.where(tile < TILES - 1, 1.0, 0.0).astype(jnp.float32)

    def exchange(source_of, target_of, out_sem, in_sem, prepare=None):
        def one(step, carry):
            other = peer(step)
            if prepare is not None:
                prepare(other)
            pltpu.make_async_remote_copy(
                src_ref=source_of(other), dst_ref=target_of(me), send_sem=out_sem, recv_sem=in_sem,
                device_id={"dom": other}, device_id_type=MESH,
            ).start()
            return carry

        lax.fori_loop(1, GROUPS, one, 0)

    def await_bytes(ref, sem):
        pltpu.make_async_copy(ref, ref, sem).wait()

    def halo_copy(cycle, field, southward):
        src, dst, device = (to_south, from_north, south) if southward else (to_north, from_south, north)
        at = cycle * FIELDS + field
        way = 1 if southward else 0
        return pltpu.make_async_remote_copy(
            src_ref=src.at[at], dst_ref=dst.at[at], send_sem=sem_halo_out.at[at, way],
            recv_sem=sem_halo_in.at[at, way], device_id={"tile": device}, device_id_type=MESH,
        )

    def raw_copy(part, southward):
        rows = pl.ds(0, 3) if part == 0 else pl.ds(3, 3)
        dst, device = (raw_north, south) if southward else (raw_south, north)
        way = 1 if southward else 0
        return pltpu.make_async_remote_copy(
            src_ref=raw.at[rows], dst_ref=dst.at[rows], send_sem=sem_raw_out.at[part, way],
            recv_sem=sem_raw_in.at[part, way], device_id={"tile": device}, device_id_type=MESH,
        )

    def begin(cycle, field):
        at = cycle * FIELDS + field

        def pair(i, carry):
            first, second = 2 * i, 2 * i + 1
            if cycle == 0:
                v0 = members[first, field] + noise[0, first, field]
                v1 = members[second, field] + noise[0, second, field]
            else:
                v0 = recv[field][recv_table[0, first]] + noise[1, first, field]
                v1 = recv[field][recv_table[0, second]] + noise[1, second, field]
            r0, r1 = half_turn(v0), half_turn(v1)
            state[field, first] = r0
            state[field, second] = r1
            to_south[at, i] = jnp.where(upper, r0, v1)
            to_north[at, i] = jnp.where(upper, v0, r1)
            return carry

        lax.fori_loop(0, PER // 2, pair, 0, unroll=2)
        halo_copy(cycle, field, True).start()
        halo_copy(cycle, field, False).start()

    def forecast(cycle, field):
        at = cycle * FIELDS + field
        halo_copy(cycle, field, True).wait_recv()
        halo_copy(cycle, field, False).wait_recv()

        def pair(i, carry):
            top = from_north[at, i] * has_north
            bottom = from_south[at, i] * has_south
            for k, (above, below) in enumerate(((top, half_turn(bottom)), (half_turn(top), bottom))):
                particle = 2 * i + k
                r = state[field, particle]
                x = jnp.concatenate([jnp.where(upper, above, r), jnp.where(upper, r, below)], axis=0)
                for _ in range(STEPS):
                    x = (coef[field, 0] * x
                         + coef[field, 1] * pltpu.roll(x, 1, axis=0)
                         + coef[field, 2] * pltpu.roll(x, 2 * ROWS - 1, axis=0)
                         + coef[field, 3] * pltpu.roll(x, 1, axis=1)
                         + coef[field, 4] * pltpu.roll(x, COLS - 1, axis=1))
                v = half_turn(jnp.where(upper, x[ROWS:], x[:ROWS]))
                result[cycle, field, particle] = v
                if field == 0:
                    miss = v - obs_mean[cycle]
                    cost = obs_weight[...] * miss * miss + obs_rest[cycle]
                    cost = cost[:, :128] + cost[:, 128:256] + cost[:, 256:]
                    partial[pl.ds(particle, 1), :] = jnp.sum(cost, axis=0, keepdims=True)
            return carry

        lax.fori_loop(0, PER // 2, pair, 0)

    def resample(cycle, field):
        stage = cycle * FIELDS + field
        outgoing, incoming = send[stage], recv[stage]

        def fill(other):
            for slot in range(CAP):
                outgoing[CAP * other + slot] = result[cycle, field, send_table[cycle, CAP * other + slot]]

        exchange(lambda other: outgoing.at[pl.ds(CAP * other, CAP)], lambda mine: incoming.at[pl.ds(CAP * mine, CAP)],
                 sem_out.at[stage], sem_in.at[stage], fill)
        for slot in range(CAP):
            incoming[CAP * me + slot] = result[cycle, field, send_table[cycle, CAP * me + slot]]

    def resample_wait(cycle, field):
        stage = cycle * FIELDS + field
        await_bytes(recv[stage].at[pl.ds(0, CAP * (GROUPS - 1))], sem_in.at[stage])

    lane = lax.broadcasted_iota(jnp.int32, (PER, 128), 1)
    line = lax.broadcasted_iota(jnp.int32, (PER, 128), 0)

    def likelihood(cycle):
        total = -0.5 * jnp.sum(partial[...], axis=1, keepdims=True)
        spread = jnp.broadcast_to(total, (PER, 128))
        likely[cycle] = spread
        row = jnp.sum(jnp.where(lane == line, spread, 0.0), axis=0, keepdims=True)
        like_send[cycle] = row
        like_recv[cycle, me] = row
        exchange(lambda other: like_send.at[cycle], lambda mine: like_recv.at[cycle, mine],
                 sem_small_out.at[cycle, 0], sem_small_in.at[cycle, 0])

    def weigh(cycle):
        await_bytes(like_recv.at[cycle, pl.ds(0, GROUPS - 1)], sem_small_in.at[cycle, 0])
        everyone = like_recv[cycle]
        known = lax.broadcasted_iota(jnp.int32, (GROUPS, 1, 128), 2) < PER
        peak = jnp.max(jnp.where(known, everyone, -3.0e38), axis=0)
        peak = jnp.max(peak, axis=1, keepdims=True)
        shifted = jnp.where(known, jnp.exp(jnp.where(known, everyone - peak[None], 0.0)), 0.0)
        total = jnp.sum(jnp.sum(shifted, axis=0), axis=1, keepdims=True)
        weights[...] = jnp.exp(likely[cycle] - peak) / total

    def average(cycle):
        def add(p, sums):
            w = weights[pl.ds(p, 1), :]
            w = jnp.concatenate([w, w, w], axis=1)
            return tuple(s + w * result[cycle, f, p] for f, s in enumerate(sums))

        sums = lax.fori_loop(0, PER, add, tuple(jnp.zeros((ROWS, COLS), jnp.float32) for _ in range(FIELDS)))
        for f in range(FIELDS):
            for k in range(4):
                part_send[cycle, 4 * f + k] = sums[f][2 * k:2 * k + 2]
        part_recv[cycle, me] = part_send[cycle, me]
        exchange(lambda other: part_send.at[cycle, other], lambda mine: part_recv.at[cycle, mine],
                 sem_small_out.at[cycle, 1], sem_small_in.at[cycle, 1])

    def combine(cycle):
        await_bytes(part_recv.at[cycle, pl.ds(0, GROUPS - 1)], sem_small_in.at[cycle, 1])
        total = part_recv[cycle, 0]
        for g in range(1, GROUPS):
            total = total + part_recv[cycle, g]
        mean_send[cycle] = total
        mean_recv[cycle, me] = total
        exchange(lambda other: mean_send.at[cycle], lambda mine: mean_recv.at[cycle, mine],
                 sem_small_out.at[cycle, 2], sem_small_in.at[cycle, 2])

    for m in range(2):
        raw[m] = half_turn(courant[m])
    for f in range(FIELDS):
        raw[2 + f] = half_turn(diffusion[f])

    def coefficients(field):
        def sixteen(m):
            mid = raw[m]
            return jnp.concatenate([jnp.where(upper, raw_north[m], mid), jnp.where(upper, mid, raw_south[m])], axis=0)

        upper2 = jnp.concatenate([jnp.where(upper, has_north, 1.0), jnp.where(upper, 1.0, has_south)], axis=0)
        column2 = jnp.concatenate([column, column], axis=0)
        cx, cy, d = sixteen(0), sixteen(1), sixteen(2 + field)
        coef[field, 0] = upper2 * (1.0 - jnp.abs(cx) - jnp.abs(cy) - 4.0 * d)
        coef[field, 1] = upper2 * (jnp.maximum(cx, 0.0) + d)
        coef[field, 2] = upper2 * (d - jnp.minimum(cx, 0.0))
        coef[field, 3] = jnp.where(column2 > 0, upper2 * (jnp.maximum(cy, 0.0) + d), 0.0)
        coef[field, 4] = jnp.where(column2 < COLS - 1, upper2 * (d - jnp.minimum(cy, 0.0)), 0.0)

    def tables(cycle):
        def one(group, carry):
            slot0, slot1 = jnp.int32(0), jnp.int32(0)
            for j in range(PER):
                old = ancestors[cycle, 0, group * PER + j]
                hit = (old >> 4) == me
                slot1 = jnp.where(hit, slot0, slot1)
                slot0 = jnp.where(hit, old & 15, slot0)
            send_table[cycle, CAP * group] = slot0
            send_table[cycle, CAP * group + 1] = slot1
            return carry

        lax.fori_loop(0, GROUPS, one, 0)
        owners = [ancestors[cycle, 0, me * PER + j] >> 4 for j in range(PER)]
        for j in range(PER):
            later = jnp.int32(0)
            for k in range(j + 1, PER):
                later = jnp.where(owners[k] == owners[j], 1, later)
            recv_table[cycle, j] = CAP * owners[j] + later

    def observations():
        cell = lax.broadcasted_iota(jnp.int32, (ROWS, COLS), 0) * COLS + column
        zero = jnp.zeros((ROWS, COLS), jnp.float32)

        def gather(k, sums):
            here = cell == obs_loc[0, k]
            precision = jnp.where(here, 1.0 / jnp.full((1, COLS), obs_var[0, k], jnp.float32), 0.0)
            return (sums[0] + precision,) + tuple(sums[1 + c] + precision * observed[c, 0, k] for c in range(CYCLES))

        sums = lax.fori_loop(0, NOBS, gather, (zero,) * (1 + CYCLES))
        obs_weight[...] = sums[0]
        seen = sums[0] > 0.0
        means = []
        for c in range(CYCLES):
            means.append(jnp.where(seen, sums[1 + c] / jnp.where(seen, sums[0], 1.0), 0.0))
            obs_mean[c] = means[c]

        def rest(k, sums):
            here = cell == obs_loc[0, k]
            precision = jnp.where(here, 1.0 / jnp.full((1, COLS), obs_var[0, k], jnp.float32), 0.0)
            return tuple(sums[c] + precision * (observed[c, 0, k] - means[c]) * (observed[c, 0, k] - means[c])
                         for c in range(CYCLES))

        sums = lax.fori_loop(0, NOBS, rest, (zero,) * CYCLES)
        for c in range(CYCLES):
            obs_rest[c] = sums[c]

    pl.semaphore_wait(barrier, GROUPS + 1)
    for way in (True, False):
        raw_copy(0, way).start()
    begin(0, 0)
    for way in (True, False):
        raw_copy(1, way).start()
    for f in range(1, FIELDS):
        begin(0, f)
    observations()
    tables(0)
    for f in range(FIELDS):
        if f < 2:
            for way in (True, False):
                raw_copy(f, way).wait_recv()
        coefficients(f)
        forecast(0, f)
        resample(0, f)
        if f == 0:
            likelihood(0)
            tables(1)
    weigh(0)
    average(0)
    for f in range(FIELDS):
        resample_wait(0, f)
        begin(1, f)
        forecast(1, f)
        if f == FIELDS - 1:
            average(1)
        resample(1, f)
        if f == 0:
            likelihood(1)
            combine(0)
        if f == 1:
            weigh(1)
    combine(1)
    for f in range(FIELDS):
        resample_wait(1, f)

        def pick(j, carry, f=f):
            out[j, f] = recv[FIELDS + f][recv_table[1, j]]
            return carry

        lax.fori_loop(0, PER, pick, 0, unroll=4)
    for c in range(CYCLES):
        await_bytes(mean_recv.at[c, pl.ds(0, GROUPS - 1)], sem_small_in.at[c, 2])
        for f in range(FIELDS):
            for k in range(4):
                averages[c, f, 2 * k:2 * k + 2] = mean_recv[c, 4 * f + k]
    for stage in range(STAGES):
        await_bytes(send[stage].at[pl.ds(0, CAP * (GROUPS - 1))], sem_out.at[stage])
        for way in (True, False):
            halo_copy(stage // FIELDS, stage % FIELDS, way).wait_send()
    for part in range(2):
        for way in (True, False):
            raw_copy(part, way).wait_send()
    for c in range(CYCLES):
        await_bytes(like_recv.at[c, pl.ds(0, GROUPS - 1)], sem_small_out.at[c, 0])
        await_bytes(part_recv.at[c, pl.ds(0, GROUPS - 1)], sem_small_out.at[c, 1])
        await_bytes(mean_recv.at[c, pl.ds(0, GROUPS - 1)], sem_small_out.at[c, 2])


def per_device(members, noise, courant, diffusion, obs_loc, observed, obs_var, ancestors):
    f32 = jnp.float32
    vmem = pl.BlockSpec(memory_space=pltpu.VMEM)
    smem = pl.BlockSpec(memory_space=pltpu.SMEM)
    plane = (ROWS, COLS)
    scratch = [pltpu.VMEM((CAP * GROUPS,) + plane, f32) for _ in range(2 * STAGES)]
    scratch += [pltpu.VMEM((STAGES, PER // 2) + plane, f32) for _ in range(4)]
    scratch += [
        pltpu.VMEM((FIELDS, PER) + plane, f32),
        pltpu.VMEM((CYCLES, FIELDS, PER) + plane, f32),
        pltpu.VMEM((2 + FIELDS,) + plane, f32),
        pltpu.VMEM((2 + FIELDS,) + plane, f32),
        pltpu.VMEM((2 + FIELDS,) + plane, f32),
        pltpu.VMEM((FIELDS, 5, 2 * ROWS, COLS), f32),
        pltpu.VMEM(plane, f32),
        pltpu.VMEM((CYCLES,) + plane, f32),
        pltpu.VMEM((CYCLES,) + plane, f32),
        pltpu.VMEM((PER, 128), f32),
        pltpu.VMEM((CYCLES, PER, 128), f32),
        pltpu.VMEM((PER, 128), f32),
        pltpu.VMEM((CYCLES, 1, 128), f32),
        pltpu.VMEM((CYCLES, GROUPS, 1, 128), f32),
        pltpu.VMEM((CYCLES, GROUPS, 2, COLS), f32),
        pltpu.VMEM((CYCLES, GROUPS, 2, COLS), f32),
        pltpu.VMEM((CYCLES, 2, COLS), f32),
        pltpu.VMEM((CYCLES, GROUPS, 2, COLS), f32),
        pltpu.SMEM((CYCLES, CAP * GROUPS), jnp.int32),
        pltpu.SMEM((CYCLES, PER), jnp.int32),
        pltpu.SemaphoreType.DMA((STAGES,)),
        pltpu.SemaphoreType.DMA((STAGES,)),
        pltpu.SemaphoreType.DMA((STAGES, 2)),
        pltpu.SemaphoreType.DMA((STAGES, 2)),
        pltpu.SemaphoreType.DMA((2, 2)),
        pltpu.SemaphoreType.DMA((2, 2)),
        pltpu.SemaphoreType.DMA((CYCLES, 3)),
        pltpu.SemaphoreType.DMA((CYCLES, 3)),
    ]
    return pl.pallas_call(
        kernel,
        out_shape=(
            jax.ShapeDtypeStruct((PER, FIELDS) + plane, f32),
            jax.ShapeDtypeStruct((CYCLES, FIELDS) + plane, f32),
        ),
        in_specs=[vmem] * 4 + [smem] * 4,
        out_specs=(vmem, vmem),
        scratch_shapes=scratch,
        compiler_params=pltpu.CompilerParams(
            collective_id=0, has_side_effects=True, vmem_limit_bytes=48 * 1024 * 1024
        ),
        name="assimilate",
    )(members, noise, courant, diffusion, obs_loc, observed, obs_var, ancestors)


def solution(mesh):
    return jax.shard_map(
        per_device,
        mesh=mesh,
        in_specs=(
            P("dom", None, "tile", None),
            P(None, "dom", None, "tile", None),
            P(None, "tile", None),
            P(None, "tile", None),
            P("tile", None),
            P(None, "tile", None),
            P("tile", None),
            P(None, "tile", None),
        ),
        out_specs=(P("dom", None, "tile", None), P(None, None, "tile", None)),
        check_vma=False,
    )
```

```python
import jax
import jax.numpy as jnp
from jax import lax
from jax.experimental import pallas as pl
from jax.experimental.pallas import tpu as pltpu
from jax.sharding import PartitionSpec as P

MESH = pl.DeviceIdType.MESH
STEPS = 4
CYCLES = 2
FIELDS = 4
PER = 16
GROUPS = 16
ALL = PER * GROUPS
PAIRS = ALL // 2
TILES = 16
ROWS = 8
COLS = 384
LANES = 128
HALF = LANES // 2
NOBS = 64
CHUNKS = 2
PAIR = 2
STRIPS = 8
WIDE = COLS // STRIPS
EDGE = STEPS
SPAN = WIDE + 2 * EDGE
BLOCKS = 4
BLOCK = PAIRS // 2 // BLOCKS


def half_turn(x):
    return pltpu.roll(x, 4, axis=0)


def place(vector, spans, rows=ROWS):
    lane = lax.broadcasted_iota(jnp.int32, (rows, LANES), 1)
    result = None
    for begin, column, length, load, limit in spans:
        low, high = max(begin, vector * LANES), min(begin + length, (vector + 1) * LANES)
        if low >= high:
            continue
        column = column + low - begin
        low, high = low - vector * LANES, high - vector * LANES
        first = max(column, 0) // LANES
        last = min(column + high - low, limit) - 1
        for u in range(first, last // LANES + 1):
            piece = load(u)
            shift = (low - column + LANES * u) % LANES
            if shift:
                piece = pltpu.roll(piece, shift, axis=1)
            start = max(low, low - column + LANES * u)
            result = piece if result is None else jnp.where(lane >= start, piece, result)
    return result


def kernel(members, noise, courant, diffusion, obs_loc, observed, obs_var, ancestors, out, averages,
           members_v, noise_v, courant_v, diffusion_v, obs_loc_s, observed_s, obs_var_s, ancestors_s, out_v,
           noise_send, noise_recv, state_send, state_recv, back_send, back_recv,
           to_north, to_south, from_north, from_south, to_north2, to_south2, from_north2, from_south2,
           state, result, raw, raw_north, raw_south, coef, obs_weight, obs_mean, obs_rest, partial, likely, weights,
           like_send, like_recv, part_send, part_recv, mean_send, mean_recv,
           noise_pairs, twins, state2, lone, coef2, windows, obs2, cost2, like2, weights2, like_send2, like_recv2,
           mean_send2, mean_recv2,
           sem_load, sem_store, sem_out, sem_in, sem_halo_out, sem_halo_in, sem_halo2_out, sem_halo2_in, sem_raw_out,
           sem_raw_in, sem_small_out, sem_small_in):
    me = lax.axis_index("dom")
    tile = lax.axis_index("tile")
    north = lax.rem(tile + TILES - 1, TILES)
    south = lax.rem(tile + 1, TILES)
    strip = lax.rem(me, STRIPS)
    in_pair = lax.div(me, STRIPS)

    def peer(step):
        return lax.rem(me + step, GROUPS)

    barrier = pltpu.get_barrier_semaphore()

    def greet(step, carry):
        pl.semaphore_signal(barrier, inc=1, device_id={"dom": peer(step)}, device_id_type=MESH)
        return carry

    for neighbour in (north, south):
        pl.semaphore_signal(barrier, inc=1, device_id={"tile": neighbour}, device_id_type=MESH)
    lax.fori_loop(1, GROUPS, greet, 0)

    loads = []

    def load(source, target):
        loads.append(pltpu.make_async_copy(source, target, sem_load.at[len(loads)]))
        loads[-1].start()

    for chunk in range(CHUNKS):
        two = pl.ds(PAIR * chunk, PAIR)
        load(members.at[:, two], members_v.at[:, two])
        load(noise.at[0, :, two], noise_v.at[0, :, two])
        load(noise.at[1, :, two], noise_v.at[1, :, two])
    for source, target in ((courant, courant_v), (diffusion, diffusion_v), (obs_loc, obs_loc_s),
                           (observed, observed_s), (obs_var, obs_var_s), (ancestors, ancestors_s)):
        load(source, target)

    upper = lax.broadcasted_iota(jnp.int32, (ROWS, COLS), 0) < 4
    upper1 = lax.broadcasted_iota(jnp.int32, (ROWS, LANES), 0) < 4
    column = lax.broadcasted_iota(jnp.int32, (ROWS, COLS), 1)
    lane8 = lax.broadcasted_iota(jnp.int32, (ROWS, LANES), 1)
    has_north = jnp.where(tile > 0, 1.0, 0.0).astype(jnp.float32)
    has_south = jnp.where(tile < TILES - 1, 1.0, 0.0).astype(jnp.float32)

    def exchange(source_of, target_of, out_sem, in_sem):
        def one(step, carry):
            other = peer(step)
            pltpu.make_async_remote_copy(
                src_ref=source_of(other), dst_ref=target_of(me), send_sem=out_sem, recv_sem=in_sem,
                device_id={"dom": other}, device_id_type=MESH,
            ).start()
            return carry

        lax.fori_loop(1, GROUPS, one, 0)

    def await_bytes(ref, sem):
        pltpu.make_async_copy(ref, ref, sem).wait()

    def others(ref, chunk):
        return ref.at[chunk, pl.ds(0, GROUPS - 1)]

    def tile_copy(source, target, out_sem, in_sem, southward):
        return pltpu.make_async_remote_copy(
            src_ref=source, dst_ref=target, send_sem=out_sem, recv_sem=in_sem,
            device_id={"tile": south if southward else north}, device_id_type=MESH,
        )

    def halo_copy(field, southward):
        source, target = (to_south, from_north) if southward else (to_north, from_south)
        way = 1 if southward else 0
        return tile_copy(source.at[field], target.at[field], sem_halo_out.at[field, way], sem_halo_in.at[field, way],
                         southward)

    def halo_copy2(chunk, block, southward):
        source, target = (to_south2, from_north2) if southward else (to_north2, from_south2)
        way = 1 if southward else 0
        rows = pl.ds(BLOCK * block, BLOCK)
        return tile_copy(source.at[chunk, rows], target.at[chunk, rows], sem_halo2_out.at[chunk, block, way],
                         sem_halo2_in.at[chunk, block, way], southward)

    def raw_copy(part, southward):
        rows = pl.ds(3 * part, 3)
        target = raw_north if southward else raw_south
        way = 1 if southward else 0
        return tile_copy(raw.at[rows], target.at[rows], sem_raw_out.at[part, way], sem_raw_in.at[part, way], southward)

    def begin(field):
        def pair(i, carry):
            first, second = 2 * i, 2 * i + 1
            v0 = members_v[first, field] + noise_v[0, first, field]
            v1 = members_v[second, field] + noise_v[0, second, field]
            r0, r1 = half_turn(v0), half_turn(v1)
            state[field, first] = r0
            state[field, second] = r1
            to_south[field, i] = jnp.where(upper, r0, v1)
            to_north[field, i] = jnp.where(upper, v0, r1)
            return carry

        lax.fori_loop(0, PER // 2, pair, 0, unroll=2)

    def march(x, c):
        width = x.shape[1]
        for _ in range(STEPS):
            x = (c(0) * x + c(1) * pltpu.roll(x, 1, axis=0) + c(2) * pltpu.roll(x, 2 * ROWS - 1, axis=0)
                 + c(3) * pltpu.roll(x, 1, axis=1) + c(4) * pltpu.roll(x, width - 1, axis=1))
        return x

    def forecast(field):
        halo_copy(field, True).wait_recv()
        halo_copy(field, False).wait_recv()

        def pair(i, carry):
            top = from_north[field, i] * has_north
            bottom = from_south[field, i] * has_south
            for k, (above, below) in enumerate(((top, half_turn(bottom)), (half_turn(top), bottom))):
                particle = 2 * i + k
                r = state[field, particle]
                x = jnp.concatenate([jnp.where(upper, above, r), jnp.where(upper, r, below)], axis=0)
                x = march(x, lambda n: coef[field, n])
                v = half_turn(jnp.where(upper, x[ROWS:], x[:ROWS]))
                result[field, particle] = v
                if field == 0:
                    miss = v - obs_mean[0]
                    cost = obs_weight[...] * miss * miss + obs_rest[0]
                    cost = cost[:, :LANES] + cost[:, LANES:2 * LANES] + cost[:, 2 * LANES:]
                    partial[pl.ds(particle, 1), :] = jnp.sum(cost, axis=0, keepdims=True)
            return carry

        lax.fori_loop(0, PER // 2, pair, 0)

    def pack(chunk, get, outgoing, incoming):
        def one(f, carry):
            for g in range(STRIPS):
                def loader(k):
                    return lambda u: get(k, PAIR * chunk + f, pl.ds(LANES * u, LANES))

                spans = [(SPAN * k, WIDE * g - EDGE, SPAN, loader(k), COLS) for k in range(PER)]
                for j in range(PER * SPAN // LANES):
                    outgoing[chunk, STRIPS * f + g, :, LANES * j:LANES * (j + 1)] = place(j, spans)
            return carry

        lax.fori_loop(0, PAIR, one, 0)
        incoming[chunk, me] = outgoing[chunk, me]

    def swap(outgoing, incoming, chunk, which):
        exchange(lambda other: outgoing.at[chunk, other], lambda mine: incoming.at[chunk, mine],
                 sem_out.at[chunk, which], sem_in.at[chunk, which])

    def unpack_noise(chunk):
        await_bytes(others(noise_recv, chunk), sem_in.at[chunk, 0])

        def one(s, carry):
            def load_from(u):
                return noise_recv[chunk, s, :, LANES * u:LANES * (u + 1)]

            for m in range(PER // 2):
                noise_pairs[chunk, PER // 2 * s + m] = place(
                    0, [(HALF * h, SPAN * (2 * m + h), SPAN, load_from, PER * SPAN) for h in range(2)])
            return carry

        lax.fori_loop(0, GROUPS, one, 0)

    def unpack_state(chunk):

        def one(s, carry):
            def load_from(u):
                return state_recv[chunk, s, :, LANES * u:LANES * (u + 1)]

            for k in range(PER):
                twins[chunk, PER * s + k] = place(
                    0, [(HALF * h, SPAN * k, SPAN, load_from, PER * SPAN) for h in range(2)])
            return carry

        lax.fori_loop(0, GROUPS, one, 0)

    def begin2(chunk, block):
        left = lane8 < HALF

        def pair(i, carry):
            v = []
            for k in range(2):
                m = 2 * i + k
                old0, old1 = ancestors_s[0, 0, 2 * m], ancestors_s[0, 0, 2 * m + 1]
                v.append(jnp.where(left, twins[chunk, old0], twins[chunk, old1]) + noise_pairs[chunk, m])
            r0, r1 = half_turn(v[0]), half_turn(v[1])
            state2[chunk, 2 * i] = r0
            state2[chunk, 2 * i + 1] = r1
            to_south2[chunk, i] = jnp.where(upper1, r0, v[1])
            to_north2[chunk, i] = jnp.where(upper1, v[0], r1)
            return carry

        lax.fori_loop(BLOCK * block, BLOCK * (block + 1), pair, 0, unroll=4)
        halo_copy2(chunk, block, True).start()
        halo_copy2(chunk, block, False).start()

    def forecast2(chunk, block):
        halo_copy2(chunk, block, True).wait_recv()
        halo_copy2(chunk, block, False).wait_recv()

        def pair(i, carry):
            top = from_north2[chunk, i] * has_north
            bottom = from_south2[chunk, i] * has_south
            for k, (above, below) in enumerate(((top, half_turn(bottom)), (half_turn(top), bottom))):
                m = 2 * i + k
                r = state2[chunk, m]
                x = jnp.concatenate([jnp.where(upper1, above, r), jnp.where(upper1, r, below)], axis=0)
                x = march(x, lambda n: coef2[chunk, n])
                v = half_turn(jnp.where(upper1, x[ROWS:], x[:ROWS]))
                lone[chunk, 2 * m] = v
                lone[chunk, 2 * m + 1] = pltpu.roll(v, HALF, axis=1)
                if chunk == 0:
                    miss = v - obs2[1]
                    cost = obs2[0] * miss * miss + obs2[2]
                    cost2[pl.ds(m, 1), :] = jnp.sum(cost, axis=0, keepdims=True)
            return carry

        lax.fori_loop(BLOCK * block, BLOCK * (block + 1), pair, 0, unroll=2)

    def pack_back(chunk):
        def one(group, carry):
            def loader(j):
                old = ancestors_s[1, 0, PER * group + j]
                return lambda u: lone[chunk, old]

            spans = [(WIDE * j, EDGE, WIDE, loader(j), LANES) for j in range(PER)]
            for n in range(PER * WIDE // LANES):
                back_send[chunk, group, :, LANES * n:LANES * (n + 1)] = place(n, spans)
            return carry

        lax.fori_loop(0, GROUPS, one, 0)
        back_recv[chunk, me] = back_send[chunk, me]

    def store(chunk):
        two = pl.ds(PAIR * chunk, PAIR)
        return pltpu.make_async_copy(out_v.at[:, two], out.at[:, two], sem_store.at[chunk])

    def finish(chunk):
        await_bytes(others(back_recv, chunk), sem_in.at[chunk, 2])

        def one(f, carry):
            def loader(g):
                return lambda u: back_recv[chunk, STRIPS * f + g, :, LANES * u:LANES * (u + 1)]

            for j in range(PER):
                spans = [(WIDE * g, WIDE * j, WIDE, loader(g), PER * WIDE) for g in range(STRIPS)]
                for u in range(COLS // LANES):
                    out_v[j, PAIR * chunk + f, :, LANES * u:LANES * (u + 1)] = place(u, spans)
            return carry

        lax.fori_loop(0, PAIR, one, 0)
        store(chunk).start()

    lane = lax.broadcasted_iota(jnp.int32, (PER, LANES), 1)
    line = lax.broadcasted_iota(jnp.int32, (PER, LANES), 0)

    def likelihood():
        total = -0.5 * jnp.sum(partial[...], axis=1, keepdims=True)
        spread = jnp.broadcast_to(total, (PER, LANES))
        likely[...] = spread
        row = jnp.sum(jnp.where(lane == line, spread, 0.0), axis=0, keepdims=True)
        like_send[...] = row
        like_recv[me] = row
        exchange(lambda other: like_send, lambda mine: like_recv.at[mine], sem_small_out.at[0], sem_small_in.at[0])

    def weigh():
        await_bytes(like_recv.at[pl.ds(0, GROUPS - 1)], sem_small_in.at[0])
        everyone = like_recv[...]
        known = lax.broadcasted_iota(jnp.int32, (GROUPS, 1, LANES), 2) < PER
        peak = jnp.max(jnp.where(known, everyone, -3.0e38), axis=0)
        peak = jnp.max(peak, axis=1, keepdims=True)
        shifted = jnp.where(known, jnp.exp(jnp.where(known, everyone - peak[None], 0.0)), 0.0)
        total = jnp.sum(jnp.sum(shifted, axis=0), axis=1, keepdims=True)
        weights[...] = jnp.exp(likely[...] - peak) / total

    def average():
        def add(p, sums):
            w = weights[pl.ds(p, 1), :]
            w = jnp.concatenate([w, w, w], axis=1)
            return tuple(s + w * result[f, p] for f, s in enumerate(sums))

        sums = lax.fori_loop(0, PER, add, tuple(jnp.zeros((ROWS, COLS), jnp.float32) for _ in range(FIELDS)))
        for f in range(FIELDS):
            for k in range(4):
                part_send[4 * f + k] = sums[f][2 * k:2 * k + 2]
        part_recv[me] = part_send[me]
        exchange(lambda other: part_send.at[other], lambda mine: part_recv.at[mine], sem_small_out.at[1],
                 sem_small_in.at[1])

    def combine():
        await_bytes(part_recv.at[pl.ds(0, GROUPS - 1)], sem_small_in.at[1])
        total = part_recv[0]
        for g in range(1, GROUPS):
            total = total + part_recv[g]
        mean_send[...] = total
        mean_recv[me] = total
        exchange(lambda other: mean_send, lambda mine: mean_recv.at[mine], sem_small_out.at[2], sem_small_in.at[2])

    place2 = lax.broadcasted_iota(jnp.int32, (PAIRS, LANES), 1)
    line2 = lax.broadcasted_iota(jnp.int32, (PAIRS, LANES), 0)

    def likelihood2():
        cost = cost2[...]
        for h in range(2):
            side = (place2 < HALF) if h == 0 else (place2 >= HALF)
            total = -0.5 * jnp.sum(jnp.where(side, cost, 0.0), axis=1, keepdims=True)
            row = jnp.sum(jnp.where(place2 == line2, total, 0.0), axis=0, keepdims=True)
            like_send2[h:h + 1, :] = row
        like_recv2[me] = like_send2[...]
        exchange(lambda other: like_send2, lambda mine: like_recv2.at[mine], sem_small_out.at[3], sem_small_in.at[3])

    def weigh2():
        await_bytes(like_recv2.at[pl.ds(0, GROUPS - 1)], sem_small_in.at[3])
        total = like_recv2[0]
        for g in range(1, GROUPS):
            total = total + like_recv2[g]
        peak = jnp.max(jnp.max(total, axis=0, keepdims=True), axis=1, keepdims=True)
        shifted = jnp.exp(total - peak)
        weight = shifted / jnp.sum(jnp.sum(shifted, axis=0, keepdims=True), axis=1, keepdims=True)
        sides = [jnp.sum(jnp.where(place2 == line2, weight[h:h + 1], 0.0), axis=1, keepdims=True) for h in range(2)]
        weights2[...] = jnp.where(place2 < HALF, sides[0], sides[1])

    def average2(chunk):
        def add(m, total):
            return total + weights2[pl.ds(m, 1), :] * lone[chunk, 2 * m]

        total = lax.fori_loop(0, PAIRS, add, jnp.zeros((ROWS, LANES), jnp.float32), unroll=8)
        total = total + pltpu.roll(total, HALF, axis=1)
        mean_send2[chunk] = total
        mean_recv2[chunk, me] = total
        exchange(lambda other: mean_send2.at[chunk], lambda mine: mean_recv2.at[chunk, mine],
                 sem_small_out.at[4 + chunk], sem_small_in.at[4 + chunk])

    def write_averages():
        await_bytes(mean_recv.at[pl.ds(0, GROUPS - 1)], sem_small_in.at[2])
        for f in range(FIELDS):
            for k in range(4):
                averages[0, f, 2 * k:2 * k + 2] = mean_recv[4 * f + k]
        for chunk in range(CHUNKS):
            await_bytes(others(mean_recv2, chunk), sem_small_in.at[4 + chunk])
            for f in range(PAIR):
                def loader(g):
                    return lambda u: mean_recv2[chunk, STRIPS * f + g]

                spans = [(WIDE * g, EDGE, WIDE, loader(g), LANES) for g in range(STRIPS)]
                for u in range(COLS // LANES):
                    averages[1, PAIR * chunk + f, :, LANES * u:LANES * (u + 1)] = place(u, spans)

    def edge_coefficients():
        for m in range(2):
            raw[m] = half_turn(courant_v[m])
        for f in range(FIELDS):
            raw[2 + f] = half_turn(diffusion_v[f])

    def coefficients(field):
        def sixteen(m):
            mid = raw[m]
            return jnp.concatenate([jnp.where(upper, raw_north[m], mid), jnp.where(upper, mid, raw_south[m])], axis=0)

        inside = jnp.concatenate([jnp.where(upper, has_north, 1.0), jnp.where(upper, 1.0, has_south)], axis=0)
        column2 = jnp.concatenate([column, column], axis=0)
        cx, cy, d = sixteen(0), sixteen(1), sixteen(2 + field)
        coef[field, 0] = inside * (1.0 - jnp.abs(cx) - jnp.abs(cy) - 4.0 * d)
        coef[field, 1] = inside * (jnp.maximum(cx, 0.0) + d)
        coef[field, 2] = inside * (d - jnp.minimum(cx, 0.0))
        coef[field, 3] = jnp.where(column2 > 0, inside * (jnp.maximum(cy, 0.0) + d), 0.0)
        coef[field, 4] = jnp.where(column2 < COLS - 1, inside * (d - jnp.minimum(cy, 0.0)), 0.0)

    def window(get, rows):
        for g in range(STRIPS):
            spans = [(HALF * h, WIDE * g - EDGE, SPAN, lambda u: get(pl.ds(LANES * u, LANES)), COLS) for h in range(2)]
            windows[g, :rows] = place(0, spans, rows)
        return windows[strip, :rows]

    def coefficients2(chunk):
        lane16 = lax.broadcasted_iota(jnp.int32, (2 * ROWS, LANES), 1)
        used = lax.rem(lane16, HALF) < SPAN
        for n in range(5):
            here = window(lambda cols: coef[PAIR * chunk + in_pair, n, :, cols], 2 * ROWS)
            coef2[chunk, n] = jnp.where(used, here, 0.0)

    def observations():
        cell = lax.broadcasted_iota(jnp.int32, (ROWS, COLS), 0) * COLS + column
        zero = jnp.zeros((ROWS, COLS), jnp.float32)

        def gather(k, sums):
            here = cell == obs_loc_s[0, k]
            precision = jnp.where(here, 1.0 / jnp.full((1, COLS), obs_var_s[0, k], jnp.float32), 0.0)
            return (sums[0] + precision,) + tuple(sums[1 + c] + precision * observed_s[c, 0, k] for c in range(CYCLES))

        sums = lax.fori_loop(0, NOBS, gather, (zero,) * (1 + CYCLES))
        obs_weight[...] = sums[0]
        seen = sums[0] > 0.0
        means = []
        for c in range(CYCLES):
            means.append(jnp.where(seen, sums[1 + c] / jnp.where(seen, sums[0], 1.0), 0.0))
            obs_mean[c] = means[c]

        def rest(k, sums):
            here = cell == obs_loc_s[0, k]
            precision = jnp.where(here, 1.0 / jnp.full((1, COLS), obs_var_s[0, k], jnp.float32), 0.0)
            return tuple(sums[c] + precision * (observed_s[c, 0, k] - means[c]) * (observed_s[c, 0, k] - means[c])
                         for c in range(CYCLES))

        sums = lax.fori_loop(0, NOBS, rest, (zero,) * CYCLES)
        for c in range(CYCLES):
            obs_rest[c] = sums[c]

    def observations2():
        inner = lax.rem(lane8, HALF)
        own = (inner >= EDGE) & (inner < EDGE + WIDE)
        first = jnp.where(in_pair == 0, 1.0, 0.0).astype(jnp.float32)
        obs2[0] = jnp.where(own, window(lambda cols: obs_weight[:, cols], ROWS), 0.0) * first
        obs2[1] = window(lambda cols: obs_mean[1, :, cols], ROWS)
        obs2[2] = jnp.where(own, window(lambda cols: obs_rest[1, :, cols], ROWS), 0.0) * first

    def noise_of(k, field, cols):
        return noise_v[1, k, field, :, cols]

    def state_of(k, field, cols):
        return result[field, k, :, cols]

    for n in (0, 1, 2, 6, 7):
        loads[n].wait()
    edge_coefficients()
    begin(0)
    begin(1)
    pl.semaphore_wait(barrier, GROUPS + 1)
    for way in (True, False):
        raw_copy(0, way).start()
    for f in range(2):
        for way in (True, False):
            halo_copy(f, way).start()
    pack(0, noise_of, noise_send, noise_recv)
    swap(noise_send, noise_recv, 0, 0)
    for n in (3, 4, 5, 8, 9, 10, 11):
        loads[n].wait()
    for f in range(2, FIELDS):
        begin(f)
        for way in (True, False):
            halo_copy(f, way).start()
    for way in (True, False):
        raw_copy(1, way).start()
    observations()
    for way in (True, False):
        raw_copy(0, way).wait_recv()
    coefficients(0)
    forecast(0)
    likelihood()
    for way in (True, False):
        raw_copy(1, way).wait_recv()
    coefficients(1)
    forecast(1)
    pack(0, state_of, state_send, state_recv)
    swap(state_send, state_recv, 0, 1)
    pack(1, noise_of, noise_send, noise_recv)
    swap(noise_send, noise_recv, 1, 0)
    for f in range(2, FIELDS):
        coefficients(f)
        forecast(f)
    pack(1, state_of, state_send, state_recv)
    swap(state_send, state_recv, 1, 1)
    weigh()
    average()
    for chunk in range(CHUNKS):
        coefficients2(chunk)
    observations2()
    unpack_noise(0)
    await_bytes(others(state_recv, 0), sem_in.at[0, 1])
    unpack_state(0)
    for block in range(BLOCKS):
        begin2(0, block)
    for block in range(BLOCKS):
        forecast2(0, block)
    likelihood2()
    pack_back(0)
    combine()
    unpack_noise(1)
    await_bytes(others(state_recv, 1), sem_in.at[1, 1])
    swap(back_send, back_recv, 0, 2)
    unpack_state(1)
    for block in range(BLOCKS):
        begin2(1, block)
    weigh2()
    average2(0)
    for block in range(BLOCKS):
        forecast2(1, block)
    pack_back(1)
    swap(back_send, back_recv, 1, 2)
    average2(1)
    finish(0)
    finish(1)
    write_averages()
    for chunk in range(CHUNKS):
        store(chunk).wait()
        for which, ref in enumerate((noise_recv, state_recv, back_recv)):
            await_bytes(others(ref, chunk), sem_out.at[chunk, which])
        await_bytes(others(mean_recv2, chunk), sem_small_out.at[4 + chunk])
    for way in (True, False):
        for f in range(FIELDS):
            halo_copy(f, way).wait_send()
        for part in range(2):
            raw_copy(part, way).wait_send()
        for chunk in range(CHUNKS):
            for block in range(BLOCKS):
                halo_copy2(chunk, block, way).wait_send()
    for n, ref in enumerate((like_recv, part_recv, mean_recv, like_recv2)):
        await_bytes(ref.at[pl.ds(0, GROUPS - 1)], sem_small_out.at[n])


def per_device(members, noise, courant, diffusion, obs_loc, observed, obs_var, ancestors):
    f32 = jnp.float32
    anywhere = pl.BlockSpec(memory_space=pl.ANY)
    plane = (ROWS, COLS)
    one = (ROWS, LANES)
    operands = (members, noise, courant, diffusion, obs_loc, observed, obs_var, ancestors)

    def vmem(*shape):
        return pltpu.VMEM(shape, f32)

    scratch = [vmem(*a.shape) for a in operands[:4]] + [pltpu.SMEM(a.shape, a.dtype) for a in operands[4:]]
    scratch += [vmem(PER, FIELDS, *plane)]
    scratch += [vmem(CHUNKS, GROUPS, ROWS, PER * SPAN) for _ in range(4)]
    scratch += [vmem(CHUNKS, GROUPS, ROWS, PER * WIDE) for _ in range(2)]
    scratch += [vmem(FIELDS, PER // 2, *plane) for _ in range(4)]
    scratch += [vmem(CHUNKS, PAIRS // 2, *one) for _ in range(4)]
    scratch += [
        vmem(FIELDS, PER, *plane),
        vmem(FIELDS, PER, *plane),
        vmem(2 + FIELDS, *plane),
        vmem(2 + FIELDS, *plane),
        vmem(2 + FIELDS, *plane),
        vmem(FIELDS, 5, 2 * ROWS, COLS),
        vmem(*plane),
        vmem(CYCLES, *plane),
        vmem(CYCLES, *plane),
        vmem(PER, LANES),
        vmem(PER, LANES),
        vmem(PER, LANES),
        vmem(1, LANES),
        vmem(GROUPS, 1, LANES),
        vmem(GROUPS, 2, COLS),
        vmem(GROUPS, 2, COLS),
        vmem(2, COLS),
        vmem(GROUPS, 2, COLS),
        vmem(CHUNKS, PAIRS, *one),
        vmem(CHUNKS, ALL, *one),
        vmem(CHUNKS, PAIRS, *one),
        vmem(CHUNKS, ALL, *one),
        vmem(CHUNKS, 5, 2 * ROWS, LANES),
        vmem(STRIPS, 2 * ROWS, LANES),
        vmem(3, *one),
        vmem(PAIRS, LANES),
        vmem(PAIRS, LANES),
        vmem(PAIRS, LANES),
        vmem(2, LANES),
        vmem(GROUPS, 2, LANES),
        vmem(CHUNKS, *one),
        vmem(CHUNKS, GROUPS, *one),
        pltpu.SemaphoreType.DMA((12,)),
        pltpu.SemaphoreType.DMA((CHUNKS,)),
        pltpu.SemaphoreType.DMA((CHUNKS, 3)),
        pltpu.SemaphoreType.DMA((CHUNKS, 3)),
        pltpu.SemaphoreType.DMA((FIELDS, 2)),
        pltpu.SemaphoreType.DMA((FIELDS, 2)),
        pltpu.SemaphoreType.DMA((CHUNKS, BLOCKS, 2)),
        pltpu.SemaphoreType.DMA((CHUNKS, BLOCKS, 2)),
        pltpu.SemaphoreType.DMA((2, 2)),
        pltpu.SemaphoreType.DMA((2, 2)),
        pltpu.SemaphoreType.DMA((6,)),
        pltpu.SemaphoreType.DMA((6,)),
    ]
    return pl.pallas_call(
        kernel,
        out_shape=(
            jax.ShapeDtypeStruct((PER, FIELDS) + plane, f32),
            jax.ShapeDtypeStruct((CYCLES, FIELDS) + plane, f32),
        ),
        in_specs=[anywhere] * 8,
        out_specs=(anywhere, pl.BlockSpec(memory_space=pltpu.VMEM)),
        scratch_shapes=scratch,
        compiler_params=pltpu.CompilerParams(
            collective_id=0, has_side_effects=True, vmem_limit_bytes=60 * 1024 * 1024
        ),
        name="assimilate",
    )(*operands)


def solution(mesh):
    return jax.shard_map(
        per_device,
        mesh=mesh,
        in_specs=(
            P("dom", None, "tile", None),
            P(None, "dom", None, "tile", None),
            P(None, "tile", None),
            P(None, "tile", None),
            P("tile", None),
            P(None, "tile", None),
            P("tile", None),
            P(None, "tile", None),
        ),
        out_specs=(P("dom", None, "tile", None), P(None, None, "tile", None)),
        check_vma=False,
    )
```

```python
import jax
import jax.numpy as jnp
from jax import lax
from jax.experimental import pallas as pl
from jax.experimental.pallas import tpu as pltpu
from jax.sharding import PartitionSpec as P

MESH = pl.DeviceIdType.MESH
STEPS = 4
CYCLES = 2
FIELDS = 4
PER = 16
GROUPS = 16
ALL = PER * GROUPS
PAIRS = ALL // 2
TILES = 16
ROWS = 8
COLS = 384
LANES = 128
HALF = LANES // 2
NOBS = 64
CHUNKS = 2
PAIR = 2
STRIPS = 8
WIDE = COLS // STRIPS
EDGE = STEPS
SPAN = WIDE + 2 * EDGE
BLOCKS = 4
BLOCK = PAIRS // BLOCKS


def half_turn(x):
    return pltpu.roll(x, 4, axis=0)


def place(vector, spans, rows=ROWS):
    lane = lax.broadcasted_iota(jnp.int32, (rows, LANES), 1)
    result = None
    for begin, column, length, load, limit in spans:
        low, high = max(begin, vector * LANES), min(begin + length, (vector + 1) * LANES)
        if low >= high:
            continue
        column = column + low - begin
        low, high = low - vector * LANES, high - vector * LANES
        first = max(column, 0) // LANES
        last = min(column + high - low, limit) - 1
        for u in range(first, last // LANES + 1):
            piece = load(u)
            shift = (low - column + LANES * u) % LANES
            if shift:
                piece = pltpu.roll(piece, shift, axis=1)
            start = max(low, low - column + LANES * u)
            result = piece if result is None else jnp.where(lane >= start, piece, result)
    return result


def kernel(members, noise, courant, diffusion, obs_loc, observed, obs_var, ancestors, out, averages,
           members_v, noise_v, courant_v, diffusion_v, obs_loc_s, observed_s, obs_var_s, ancestors_s,
           noise_send, noise_recv, state_send, state_recv, back_send, back_recv,
           to_north, to_south, from_north, from_south,
           state, result, raw, raw_north, raw_south, coef, obs_weight, obs_mean, obs_rest, partial, likely, weights,
           like_send, like_recv, part_send, part_recv, mean_send, mean_recv,
           noise_pairs, twins, grid2, lone, coef2, windows, obs2, weights2, like_send2, like_recv2,
           mean_send2, mean_recv2,
           sem_load, sem_out, sem_in, sem_halo_out, sem_halo_in, sem_halo2_out, sem_halo2_in, sem_raw_out,
           sem_raw_in, sem_small_out, sem_small_in):
    me = lax.axis_index("dom")
    tile = lax.axis_index("tile")
    north = lax.rem(tile + TILES - 1, TILES)
    south = lax.rem(tile + 1, TILES)
    strip = lax.rem(me, STRIPS)
    in_pair = lax.div(me, STRIPS)

    def peer(step):
        return lax.rem(me + step, GROUPS)

    barrier = pltpu.get_barrier_semaphore()

    def greet(step, carry):
        pl.semaphore_signal(barrier, inc=1, device_id={"dom": peer(step)}, device_id_type=MESH)
        return carry

    for neighbour in (north, south):
        pl.semaphore_signal(barrier, inc=1, device_id={"tile": neighbour}, device_id_type=MESH)
    lax.fori_loop(1, GROUPS, greet, 0)

    loads = []

    def load(source, target):
        loads.append(pltpu.make_async_copy(source, target, sem_load.at[len(loads)]))
        loads[-1].start()

    for chunk in range(CHUNKS):
        two = pl.ds(PAIR * chunk, PAIR)
        load(members.at[:, two], members_v.at[:, two])
        load(noise.at[0, :, two], noise_v.at[0, :, two])
        load(noise.at[1, :, two], noise_v.at[1, :, two])
    for source, target in ((courant, courant_v), (diffusion, diffusion_v), (obs_loc, obs_loc_s),
                           (observed, observed_s), (obs_var, obs_var_s), (ancestors, ancestors_s)):
        load(source, target)

    upper = lax.broadcasted_iota(jnp.int32, (ROWS, COLS), 0) < 4
    upper1 = lax.broadcasted_iota(jnp.int32, (ROWS, LANES), 0) < 4
    column = lax.broadcasted_iota(jnp.int32, (ROWS, COLS), 1)
    lane8 = lax.broadcasted_iota(jnp.int32, (ROWS, LANES), 1)
    has_north = jnp.where(tile > 0, 1.0, 0.0).astype(jnp.float32)
    has_south = jnp.where(tile < TILES - 1, 1.0, 0.0).astype(jnp.float32)

    def exchange(source_of, target_of, out_sem, in_sem):
        def one(step, carry):
            other = peer(step)
            pltpu.make_async_remote_copy(
                src_ref=source_of(other), dst_ref=target_of(me), send_sem=out_sem, recv_sem=in_sem,
                device_id={"dom": other}, device_id_type=MESH,
            ).start()
            return carry

        lax.fori_loop(1, GROUPS, one, 0)

    def await_bytes(ref, sem):
        pltpu.make_async_copy(ref, ref, sem).wait()

    def others(ref, chunk):
        return ref.at[chunk, pl.ds(0, GROUPS - 1)]

    def tile_copy(source, target, out_sem, in_sem, southward):
        return pltpu.make_async_remote_copy(
            src_ref=source, dst_ref=target, send_sem=out_sem, recv_sem=in_sem,
            device_id={"tile": south if southward else north}, device_id_type=MESH,
        )

    def halo_copy(field, southward):
        source, target = (to_south, from_north) if southward else (to_north, from_south)
        way = 1 if southward else 0
        return tile_copy(source.at[field], target.at[field], sem_halo_out.at[field, way], sem_halo_in.at[field, way],
                         southward)

    def halo_copy2(chunk, block, southward):
        source, target = (ROWS, 0) if southward else (EDGE, ROWS + EDGE)
        way = 1 if southward else 0
        rows = EDGE * BLOCK
        return tile_copy(grid2.at[chunk, block, pl.ds(source * BLOCK, rows)],
                         grid2.at[chunk, block, pl.ds(target * BLOCK, rows)], sem_halo2_out.at[chunk, block, way],
                         sem_halo2_in.at[chunk, block, way], southward)

    def raw_copy(part, southward):
        rows = pl.ds(3 * part, 3)
        target = raw_north if southward else raw_south
        way = 1 if southward else 0
        return tile_copy(raw.at[rows], target.at[rows], sem_raw_out.at[part, way], sem_raw_in.at[part, way], southward)

    def begin(field):
        def pair(i, carry):
            first, second = 2 * i, 2 * i + 1
            v0 = members_v[first, field] + noise_v[0, first, field]
            v1 = members_v[second, field] + noise_v[0, second, field]
            r0, r1 = half_turn(v0), half_turn(v1)
            state[field, first] = r0
            state[field, second] = r1
            to_south[field, i] = jnp.where(upper, r0, v1)
            to_north[field, i] = jnp.where(upper, v0, r1)
            return carry

        lax.fori_loop(0, PER // 2, pair, 0, unroll=2)

    def forecast(field):
        halo_copy(field, True).wait_recv()
        halo_copy(field, False).wait_recv()

        def four(q, carry):
            for i in (2 * q, 2 * q + 1):
                top = from_north[field, i] * has_north
                bottom = from_south[field, i] * has_south
                for k, (above, below) in enumerate(((top, half_turn(bottom)), (half_turn(top), bottom))):
                    particle = 2 * i + k
                    r = state[field, particle]
                    x = jnp.concatenate([jnp.where(upper, above, r), jnp.where(upper, r, below)], axis=0)
                    for _ in range(STEPS):
                        x = (coef[field, 0] * x + coef[field, 1] * pltpu.roll(x, 1, axis=0)
                             + coef[field, 2] * pltpu.roll(x, 2 * ROWS - 1, axis=0)
                             + coef[field, 3] * pltpu.roll(x, 1, axis=1)
                             + coef[field, 4] * pltpu.roll(x, COLS - 1, axis=1))
                    v = half_turn(jnp.where(upper, x[ROWS:], x[:ROWS]))
                    result[field, particle] = v
                    if field == 0:
                        miss = v - obs_mean[0]
                        cost = obs_weight[...] * miss * miss + obs_rest[0]
                        cost = cost[:, :LANES] + cost[:, LANES:2 * LANES] + cost[:, 2 * LANES:]
                        partial[pl.ds(particle, 1), :] = jnp.sum(cost, axis=0, keepdims=True)
            return carry

        lax.fori_loop(0, PER // 4, four, 0)

    def pack(chunk, get, outgoing, incoming):
        def one(f, carry):
            for g in range(STRIPS):
                def loader(k):
                    return lambda u: get(k, PAIR * chunk + f, pl.ds(LANES * u, LANES))

                spans = [(SPAN * k, WIDE * g - EDGE, SPAN, loader(k), COLS) for k in range(PER)]
                for j in range(PER * SPAN // LANES):
                    outgoing[chunk, STRIPS * f + g, :, LANES * j:LANES * (j + 1)] = place(j, spans)
            return carry

        lax.fori_loop(0, PAIR, one, 0)
        incoming[chunk, me] = outgoing[chunk, me]

    def swap(outgoing, incoming, chunk, which):
        exchange(lambda other: outgoing.at[chunk, other], lambda mine: incoming.at[chunk, mine],
                 sem_out.at[chunk, which], sem_in.at[chunk, which])

    def unpack_noise(chunk):
        await_bytes(others(noise_recv, chunk), sem_in.at[chunk, 0])

        def one(s, carry):
            def load_from(u):
                return noise_recv[chunk, s, :, LANES * u:LANES * (u + 1)]

            for m in range(PER // 2):
                noise_pairs[chunk, PER // 2 * s + m] = place(
                    0, [(HALF * h, SPAN * (2 * m + h), SPAN, load_from, PER * SPAN) for h in range(2)])
            return carry

        lax.fori_loop(0, GROUPS, one, 0, unroll=4)

    def unpack_state(chunk):

        def one(s, carry):
            def load_from(u):
                return state_recv[chunk, s, :, LANES * u:LANES * (u + 1)]

            for k in range(PER):
                twins[chunk, PER * s + k] = place(
                    0, [(HALF * h, SPAN * k, SPAN, load_from, PER * SPAN) for h in range(2)])
            return carry

        lax.fori_loop(0, GROUPS, one, 0, unroll=2)

    def begin2(chunk, block):
        left = lane8 < HALF

        def one(i, carry):
            m = BLOCK * block + i
            old0, old1 = ancestors_s[0, 0, 2 * m], ancestors_s[0, 0, 2 * m + 1]
            v = jnp.where(left, twins[chunk, old0], twins[chunk, old1]) + noise_pairs[chunk, m]
            grid2[chunk, block, pl.ds(EDGE * BLOCK + i, ROWS, stride=BLOCK), :] = v
            return carry

        lax.fori_loop(0, BLOCK, one, 0, unroll=8)
        halo_copy2(chunk, block, True).start()
        halo_copy2(chunk, block, False).start()

    def forecast2(chunk, block):
        halo_copy2(chunk, block, True).wait_recv()
        halo_copy2(chunk, block, False).wait_recv()
        high = ROWS + 2 * EDGE

        def tall(n, r):
            return jnp.concatenate([coef2[chunk, n, r]] * (BLOCK // ROWS), axis=0)

        x = [grid2[chunk, block, BLOCK * r:BLOCK * (r + 1), :] for r in range(high)]
        x = [v * has_north if r < EDGE else v * has_south if r >= EDGE + ROWS else v for r, v in enumerate(x)]
        for s in range(1, STEPS + 1):
            new = list(x)
            for r in range(s, high - s):
                new[r] = (tall(0, r) * x[r] + tall(1, r) * x[r - 1] + tall(2, r) * x[r + 1]
                          + tall(3, r) * pltpu.roll(x[r], 1, axis=1) + tall(4, r) * pltpu.roll(x[r], LANES - 1, axis=1))
            x = new
        for r in range(ROWS):
            lone[chunk, ALL * r + BLOCK * block:ALL * r + BLOCK * (block + 1), :] = x[EDGE + r]
            low = ALL * r + PAIRS + BLOCK * block
            lone[chunk, low:low + BLOCK, :] = pltpu.roll(x[EDGE + r], HALF, axis=1)

    def pack_back(chunk):
        def one(group, carry):
            def loader(j):
                old = ancestors_s[1, 0, PER * group + j]
                tall = lone[chunk, pl.ds((old & 1) * PAIRS + (old >> 1), ROWS, stride=ALL), :]
                return lambda u: tall

            spans = [(WIDE * j, EDGE, WIDE, loader(j), LANES) for j in range(PER)]
            for n in range(PER * WIDE // LANES):
                back_send[chunk, group, :, LANES * n:LANES * (n + 1)] = place(n, spans)
            return carry

        lax.fori_loop(0, GROUPS, one, 0, unroll=4)
        back_recv[chunk, me] = back_send[chunk, me]

    def finish(chunk):
        await_bytes(others(back_recv, chunk), sem_in.at[chunk, 2])

        def one(f, carry):
            def loader(g):
                return lambda u: back_recv[chunk, STRIPS * f + g, :, LANES * u:LANES * (u + 1)]

            for j in range(PER):
                spans = [(WIDE * g, WIDE * j, WIDE, loader(g), PER * WIDE) for g in range(STRIPS)]
                for u in range(COLS // LANES):
                    out[j, PAIR * chunk + f, :, LANES * u:LANES * (u + 1)] = place(u, spans)
            return carry

        lax.fori_loop(0, PAIR, one, 0)

    lane = lax.broadcasted_iota(jnp.int32, (PER, LANES), 1)
    line = lax.broadcasted_iota(jnp.int32, (PER, LANES), 0)

    def likelihood():
        total = -0.5 * jnp.sum(partial[...], axis=1, keepdims=True)
        spread = jnp.broadcast_to(total, (PER, LANES))
        likely[...] = spread
        row = jnp.sum(jnp.where(lane == line, spread, 0.0), axis=0, keepdims=True)
        like_send[...] = row
        like_recv[me] = row
        exchange(lambda other: like_send, lambda mine: like_recv.at[mine], sem_small_out.at[0], sem_small_in.at[0])

    def weigh():
        await_bytes(like_recv.at[pl.ds(0, GROUPS - 1)], sem_small_in.at[0])
        everyone = like_recv[...]
        known = lax.broadcasted_iota(jnp.int32, (GROUPS, 1, LANES), 2) < PER
        peak = jnp.max(jnp.where(known, everyone, -3.0e38), axis=0)
        peak = jnp.max(peak, axis=1, keepdims=True)
        shifted = jnp.where(known, jnp.exp(jnp.where(known, everyone - peak[None], 0.0)), 0.0)
        total = jnp.sum(jnp.sum(shifted, axis=0), axis=1, keepdims=True)
        weights[...] = jnp.exp(likely[...] - peak) / total

    def average():
        def add(p, sums):
            w = weights[pl.ds(p, 1), :]
            w = jnp.concatenate([w, w, w], axis=1)
            return tuple(s + w * result[f, p] for f, s in enumerate(sums))

        sums = lax.fori_loop(0, PER, add, tuple(jnp.zeros((ROWS, COLS), jnp.float32) for _ in range(FIELDS)))
        for f in range(FIELDS):
            for k in range(4):
                part_send[4 * f + k] = sums[f][2 * k:2 * k + 2]
        part_recv[me] = part_send[me]
        exchange(lambda other: part_send.at[other], lambda mine: part_recv.at[mine], sem_small_out.at[1],
                 sem_small_in.at[1])

    def combine():
        await_bytes(part_recv.at[pl.ds(0, GROUPS - 1)], sem_small_in.at[1])
        total = part_recv[0]
        for g in range(1, GROUPS):
            total = total + part_recv[g]
        mean_send[...] = total
        mean_recv[me] = total
        exchange(lambda other: mean_send, lambda mine: mean_recv.at[mine], sem_small_out.at[2], sem_small_in.at[2])

    place2 = lax.broadcasted_iota(jnp.int32, (PAIRS, LANES), 1)
    line2 = lax.broadcasted_iota(jnp.int32, (PAIRS, LANES), 0)

    def likelihood2():
        cost = jnp.zeros((PAIRS, LANES), jnp.float32)
        for r in range(ROWS):
            miss = lone[0, ALL * r:ALL * r + PAIRS, :] - obs2[1, r:r + 1]
            cost = cost + obs2[0, r:r + 1] * miss * miss + obs2[2, r:r + 1]
        for h in range(2):
            side = (place2 < HALF) if h == 0 else (place2 >= HALF)
            total = -0.5 * jnp.sum(jnp.where(side, cost, 0.0), axis=1, keepdims=True)
            row = jnp.sum(jnp.where(place2 == line2, total, 0.0), axis=0, keepdims=True)
            like_send2[h:h + 1, :] = row
        like_recv2[me] = like_send2[...]
        exchange(lambda other: like_send2, lambda mine: like_recv2.at[mine], sem_small_out.at[3], sem_small_in.at[3])

    def weigh2():
        await_bytes(like_recv2.at[pl.ds(0, GROUPS - 1)], sem_small_in.at[3])
        total = like_recv2[0]
        for g in range(1, GROUPS):
            total = total + like_recv2[g]
        peak = jnp.max(jnp.max(total, axis=0, keepdims=True), axis=1, keepdims=True)
        shifted = jnp.exp(total - peak)
        weight = shifted / jnp.sum(jnp.sum(shifted, axis=0, keepdims=True), axis=1, keepdims=True)
        sides = [jnp.sum(jnp.where(place2 == line2, weight[h:h + 1], 0.0), axis=1, keepdims=True) for h in range(2)]
        weights2[...] = jnp.where(place2 < HALF, sides[0], sides[1])

    def average2(chunk):
        for r in range(ROWS):
            part = weights2[...] * lone[chunk, ALL * r:ALL * r + PAIRS, :]
            mean_send2[chunk, r:r + 1, :] = jnp.sum(part, axis=0, keepdims=True)
        total = mean_send2[chunk]
        total = total + pltpu.roll(total, HALF, axis=1)
        mean_send2[chunk] = total
        mean_recv2[chunk, me] = total
        exchange(lambda other: mean_send2.at[chunk], lambda mine: mean_recv2.at[chunk, mine],
                 sem_small_out.at[4 + chunk], sem_small_in.at[4 + chunk])

    def write_averages():
        await_bytes(mean_recv.at[pl.ds(0, GROUPS - 1)], sem_small_in.at[2])
        for f in range(FIELDS):
            for k in range(4):
                averages[0, f, 2 * k:2 * k + 2] = mean_recv[4 * f + k]
        for chunk in range(CHUNKS):
            await_bytes(others(mean_recv2, chunk), sem_small_in.at[4 + chunk])
            for f in range(PAIR):
                def loader(g):
                    return lambda u: mean_recv2[chunk, STRIPS * f + g]

                spans = [(WIDE * g, EDGE, WIDE, loader(g), LANES) for g in range(STRIPS)]
                for u in range(COLS // LANES):
                    averages[1, PAIR * chunk + f, :, LANES * u:LANES * (u + 1)] = place(u, spans)

    def edge_coefficients():
        for m in range(2):
            raw[m] = half_turn(courant_v[m])
        for f in range(FIELDS):
            raw[2 + f] = half_turn(diffusion_v[f])

    def coefficients(field):
        def sixteen(m):
            mid = raw[m]
            return jnp.concatenate([jnp.where(upper, raw_north[m], mid), jnp.where(upper, mid, raw_south[m])], axis=0)

        inside = jnp.concatenate([jnp.where(upper, has_north, 1.0), jnp.where(upper, 1.0, has_south)], axis=0)
        column2 = jnp.concatenate([column, column], axis=0)
        cx, cy, d = sixteen(0), sixteen(1), sixteen(2 + field)
        coef[field, 0] = inside * (1.0 - jnp.abs(cx) - jnp.abs(cy) - 4.0 * d)
        coef[field, 1] = inside * (jnp.maximum(cx, 0.0) + d)
        coef[field, 2] = inside * (d - jnp.minimum(cx, 0.0))
        coef[field, 3] = jnp.where(column2 > 0, inside * (jnp.maximum(cy, 0.0) + d), 0.0)
        coef[field, 4] = jnp.where(column2 < COLS - 1, inside * (d - jnp.minimum(cy, 0.0)), 0.0)

    def window(get, rows):
        for g in range(STRIPS):
            spans = [(HALF * h, WIDE * g - EDGE, SPAN, lambda u: get(pl.ds(LANES * u, LANES)), COLS) for h in range(2)]
            windows[g, :rows] = place(0, spans, rows)
        return windows[strip, :rows]

    def coefficients2(chunk):
        lane16 = lax.broadcasted_iota(jnp.int32, (2 * ROWS, LANES), 1)
        used = lax.rem(lane16, HALF) < SPAN
        for n in range(5):
            here = window(lambda cols: coef[PAIR * chunk + in_pair, n, :, cols], 2 * ROWS)
            here = jnp.where(used, here, 0.0)
            for r in range(2 * ROWS):
                coef2[chunk, n, r] = jnp.broadcast_to(here[r:r + 1], (ROWS, LANES))

    def observations():
        cell = lax.broadcasted_iota(jnp.int32, (ROWS, COLS), 0) * COLS + column
        zero = jnp.zeros((ROWS, COLS), jnp.float32)

        def gather(k, sums):
            here = cell == obs_loc_s[0, k]
            precision = jnp.where(here, 1.0 / jnp.full((1, COLS), obs_var_s[0, k], jnp.float32), 0.0)
            return (sums[0] + precision,) + tuple(sums[1 + c] + precision * observed_s[c, 0, k] for c in range(CYCLES))

        sums = lax.fori_loop(0, NOBS, gather, (zero,) * (1 + CYCLES), unroll=8)
        obs_weight[...] = sums[0]
        seen = sums[0] > 0.0
        means = []
        for c in range(CYCLES):
            means.append(jnp.where(seen, sums[1 + c] / jnp.where(seen, sums[0], 1.0), 0.0))
            obs_mean[c] = means[c]

        def rest(k, sums):
            here = cell == obs_loc_s[0, k]
            precision = jnp.where(here, 1.0 / jnp.full((1, COLS), obs_var_s[0, k], jnp.float32), 0.0)
            return tuple(sums[c] + precision * (observed_s[c, 0, k] - means[c]) * (observed_s[c, 0, k] - means[c])
                         for c in range(CYCLES))

        sums = lax.fori_loop(0, NOBS, rest, (zero,) * CYCLES, unroll=8)
        for c in range(CYCLES):
            obs_rest[c] = sums[c]

    def observations2():
        inner = lax.rem(lane8, HALF)
        own = (inner >= EDGE) & (inner < EDGE + WIDE)
        first = jnp.where(in_pair == 0, 1.0, 0.0).astype(jnp.float32)
        obs2[0] = jnp.where(own, window(lambda cols: obs_weight[:, cols], ROWS), 0.0) * first
        obs2[1] = window(lambda cols: obs_mean[1, :, cols], ROWS)
        obs2[2] = jnp.where(own, window(lambda cols: obs_rest[1, :, cols], ROWS), 0.0) * first

    def noise_of(k, field, cols):
        return noise_v[1, k, field, :, cols]

    def state_of(k, field, cols):
        return result[field, k, :, cols]

    for n in (0, 1, 2, 6, 7):
        loads[n].wait()
    edge_coefficients()
    begin(0)
    begin(1)
    pl.semaphore_wait(barrier, GROUPS + 1)
    for way in (True, False):
        raw_copy(0, way).start()
    for f in range(2):
        for way in (True, False):
            halo_copy(f, way).start()
    pack(0, noise_of, noise_send, noise_recv)
    swap(noise_send, noise_recv, 0, 0)
    for n in (3, 4, 5, 8, 9, 10, 11):
        loads[n].wait()
    for f in range(2, FIELDS):
        begin(f)
        for way in (True, False):
            halo_copy(f, way).start()
    for way in (True, False):
        raw_copy(1, way).start()
    observations()
    for way in (True, False):
        raw_copy(0, way).wait_recv()
    coefficients(0)
    forecast(0)
    likelihood()
    for way in (True, False):
        raw_copy(1, way).wait_recv()
    coefficients(1)
    forecast(1)
    pack(0, state_of, state_send, state_recv)
    swap(state_send, state_recv, 0, 1)
    pack(1, noise_of, noise_send, noise_recv)
    swap(noise_send, noise_recv, 1, 0)
    for f in range(2, FIELDS):
        coefficients(f)
        forecast(f)
    pack(1, state_of, state_send, state_recv)
    swap(state_send, state_recv, 1, 1)
    weigh()
    average()
    for chunk in range(CHUNKS):
        coefficients2(chunk)
    observations2()
    unpack_noise(0)
    await_bytes(others(state_recv, 0), sem_in.at[0, 1])
    unpack_state(0)
    for block in range(BLOCKS):
        begin2(0, block)
    for block in range(BLOCKS):
        forecast2(0, block)
    likelihood2()
    pack_back(0)
    combine()
    unpack_noise(1)
    await_bytes(others(state_recv, 1), sem_in.at[1, 1])
    swap(back_send, back_recv, 0, 2)
    unpack_state(1)
    for block in range(BLOCKS):
        begin2(1, block)
    weigh2()
    average2(0)
    for block in range(BLOCKS):
        forecast2(1, block)
    pack_back(1)
    swap(back_send, back_recv, 1, 2)
    average2(1)
    finish(0)
    finish(1)
    write_averages()
    for chunk in range(CHUNKS):
        for which, ref in enumerate((noise_recv, state_recv, back_recv)):
            await_bytes(others(ref, chunk), sem_out.at[chunk, which])
        await_bytes(others(mean_recv2, chunk), sem_small_out.at[4 + chunk])
    for way in (True, False):
        for f in range(FIELDS):
            halo_copy(f, way).wait_send()
        for part in range(2):
            raw_copy(part, way).wait_send()
        for chunk in range(CHUNKS):
            for block in range(BLOCKS):
                halo_copy2(chunk, block, way).wait_send()
    for n, ref in enumerate((like_recv, part_recv, mean_recv, like_recv2)):
        await_bytes(ref.at[pl.ds(0, GROUPS - 1)], sem_small_out.at[n])


def per_device(members, noise, courant, diffusion, obs_loc, observed, obs_var, ancestors):
    f32 = jnp.float32
    anywhere = pl.BlockSpec(memory_space=pl.ANY)
    plane = (ROWS, COLS)
    one = (ROWS, LANES)
    operands = (members, noise, courant, diffusion, obs_loc, observed, obs_var, ancestors)

    def vmem(*shape):
        return pltpu.VMEM(shape, f32)

    scratch = [vmem(*a.shape) for a in operands[:4]] + [pltpu.SMEM(a.shape, a.dtype) for a in operands[4:]]
    scratch += [vmem(CHUNKS, GROUPS, ROWS, PER * SPAN) for _ in range(4)]
    scratch += [vmem(CHUNKS, GROUPS, ROWS, PER * WIDE) for _ in range(2)]
    scratch += [vmem(FIELDS, PER // 2, *plane) for _ in range(4)]
    scratch += [
        vmem(FIELDS, PER, *plane),
        vmem(FIELDS, PER, *plane),
        vmem(2 + FIELDS, *plane),
        vmem(2 + FIELDS, *plane),
        vmem(2 + FIELDS, *plane),
        vmem(FIELDS, 5, 2 * ROWS, COLS),
        vmem(*plane),
        vmem(CYCLES, *plane),
        vmem(CYCLES, *plane),
        vmem(PER, LANES),
        vmem(PER, LANES),
        vmem(PER, LANES),
        vmem(1, LANES),
        vmem(GROUPS, 1, LANES),
        vmem(GROUPS, 2, COLS),
        vmem(GROUPS, 2, COLS),
        vmem(2, COLS),
        vmem(GROUPS, 2, COLS),
        vmem(CHUNKS, PAIRS, *one),
        vmem(CHUNKS, ALL, *one),
        vmem(CHUNKS, BLOCKS, (ROWS + 2 * EDGE) * BLOCK, LANES),
        vmem(CHUNKS, ROWS * ALL, LANES),
        vmem(CHUNKS, 5, 2 * ROWS, *one),
        vmem(STRIPS, 2 * ROWS, LANES),
        vmem(3, *one),
        vmem(PAIRS, LANES),
        vmem(2, LANES),
        vmem(GROUPS, 2, LANES),
        vmem(CHUNKS, *one),
        vmem(CHUNKS, GROUPS, *one),
        pltpu.SemaphoreType.DMA((12,)),
        pltpu.SemaphoreType.DMA((CHUNKS, 3)),
        pltpu.SemaphoreType.DMA((CHUNKS, 3)),
        pltpu.SemaphoreType.DMA((FIELDS, 2)),
        pltpu.SemaphoreType.DMA((FIELDS, 2)),
        pltpu.SemaphoreType.DMA((CHUNKS, BLOCKS, 2)),
        pltpu.SemaphoreType.DMA((CHUNKS, BLOCKS, 2)),
        pltpu.SemaphoreType.DMA((2, 2)),
        pltpu.SemaphoreType.DMA((2, 2)),
        pltpu.SemaphoreType.DMA((6,)),
        pltpu.SemaphoreType.DMA((6,)),
    ]
    return pl.pallas_call(
        kernel,
        out_shape=(
            jax.ShapeDtypeStruct((PER, FIELDS) + plane, f32),
            jax.ShapeDtypeStruct((CYCLES, FIELDS) + plane, f32),
        ),
        in_specs=[anywhere] * 8,
        out_specs=(pl.BlockSpec(memory_space=pltpu.VMEM), pl.BlockSpec(memory_space=pltpu.VMEM)),
        scratch_shapes=scratch,
        compiler_params=pltpu.CompilerParams(
            collective_id=0, has_side_effects=True, vmem_limit_bytes=60 * 1024 * 1024
        ),
        name="assimilate",
    )(*operands)


def solution(mesh):
    return jax.shard_map(
        per_device,
        mesh=mesh,
        in_specs=(
            P("dom", None, "tile", None),
            P(None, "dom", None, "tile", None),
            P(None, "tile", None),
            P(None, "tile", None),
            P("tile", None),
            P(None, "tile", None),
            P("tile", None),
            P(None, "tile", None),
        ),
        out_specs=(P("dom", None, "tile", None), P(None, None, "tile", None)),
        check_vma=False,
    )
```

```python
import jax
import jax.numpy as jnp
from jax import lax
from jax.experimental import pallas as pl
from jax.experimental.pallas import tpu as pltpu
from jax.sharding import PartitionSpec as P

MESH = pl.DeviceIdType.MESH
STEPS = 4
CYCLES = 2
FIELDS = 4
PER = 16
GROUPS = 16
ALL = PER * GROUPS
PAIRS = ALL // 2
TILES = 16
ROWS = 8
COLS = 384
LANES = 128
HALF = LANES // 2
NOBS = 64
CHUNKS = 2
PAIR = 2
STRIPS = 8
WIDE = COLS // STRIPS
EDGE = STEPS
SPAN = WIDE + 2 * EDGE
BLOCKS = 4
BLOCK = PAIRS // BLOCKS


def half_turn(x):
    return pltpu.roll(x, 4, axis=0)


def place(vector, spans, rows=ROWS):
    lane = lax.broadcasted_iota(jnp.int32, (rows, LANES), 1)
    result = None
    for begin, column, length, load, limit in spans:
        low, high = max(begin, vector * LANES), min(begin + length, (vector + 1) * LANES)
        if low >= high:
            continue
        column = column + low - begin
        low, high = low - vector * LANES, high - vector * LANES
        first = max(column, 0) // LANES
        last = min(column + high - low, limit) - 1
        for u in range(first, last // LANES + 1):
            piece = load(u)
            shift = (low - column + LANES * u) % LANES
            if shift:
                piece = pltpu.roll(piece, shift, axis=1)
            start = max(low, low - column + LANES * u)
            result = piece if result is None else jnp.where(lane >= start, piece, result)
    return result


def kernel(members, noise, courant, diffusion, obs_loc, observed, obs_var, ancestors, out, averages,
           members_v, noise_v, courant_v, diffusion_v, obs_loc_s, observed_s, obs_var_s, ancestors_s,
           noise_send, noise_recv, state_send, state_recv, back_send, back_recv,
           to_north, to_south, from_north, from_south,
           state, result, raw, raw_north, raw_south, coef, obs_weight, obs_mean, obs_rest, partial, weights,
           like_send, like_recv, mean_own,
           noise_pairs, twins, grid2, lone, coef2, windows, obs2, weights2, like_send2, like_recv2,
           mean_send2, mean_recv2,
           sem_load, sem_out, sem_in, sem_halo_out, sem_halo_in, sem_halo2_out, sem_halo2_in, sem_raw_out,
           sem_raw_in, sem_small_out, sem_small_in):
    me = lax.axis_index("dom")
    tile = lax.axis_index("tile")
    north = lax.rem(tile + TILES - 1, TILES)
    south = lax.rem(tile + 1, TILES)
    strip = lax.rem(me, STRIPS)
    in_pair = lax.div(me, STRIPS)

    def peer(step):
        return lax.rem(me + step, GROUPS)

    barrier = pltpu.get_barrier_semaphore()

    def greet(step, carry):
        pl.semaphore_signal(barrier, inc=1, device_id={"dom": peer(step)}, device_id_type=MESH)
        return carry

    for neighbour in (north, south):
        pl.semaphore_signal(barrier, inc=1, device_id={"tile": neighbour}, device_id_type=MESH)
    lax.fori_loop(1, GROUPS, greet, 0)

    loads = []

    def load(source, target):
        loads.append(pltpu.make_async_copy(source, target, sem_load.at[len(loads)]))
        loads[-1].start()

    for chunk in range(CHUNKS):
        two = pl.ds(PAIR * chunk, PAIR)
        load(members.at[:, two], members_v.at[:, two])
        load(noise.at[0, :, two], noise_v.at[0, :, two])
        load(noise.at[1, :, two], noise_v.at[1, :, two])
    for source, target in ((courant, courant_v), (diffusion, diffusion_v), (obs_loc, obs_loc_s),
                           (observed, observed_s), (obs_var, obs_var_s), (ancestors, ancestors_s)):
        load(source, target)

    upper = lax.broadcasted_iota(jnp.int32, (ROWS, COLS), 0) < 4
    upper1 = lax.broadcasted_iota(jnp.int32, (ROWS, LANES), 0) < 4
    column = lax.broadcasted_iota(jnp.int32, (ROWS, COLS), 1)
    lane8 = lax.broadcasted_iota(jnp.int32, (ROWS, LANES), 1)
    has_north = jnp.where(tile > 0, 1.0, 0.0).astype(jnp.float32)
    has_south = jnp.where(tile < TILES - 1, 1.0, 0.0).astype(jnp.float32)

    def exchange(source_of, target_of, out_sem, in_sem):
        def one(step, carry):
            other = peer(step)
            pltpu.make_async_remote_copy(
                src_ref=source_of(other), dst_ref=target_of(me), send_sem=out_sem, recv_sem=in_sem,
                device_id={"dom": other}, device_id_type=MESH,
            ).start()
            return carry

        lax.fori_loop(1, GROUPS, one, 0)

    def await_bytes(ref, sem):
        pltpu.make_async_copy(ref, ref, sem).wait()

    def others(ref, chunk):
        return ref.at[chunk, pl.ds(0, GROUPS - 1)]

    def tile_copy(source, target, out_sem, in_sem, southward):
        return pltpu.make_async_remote_copy(
            src_ref=source, dst_ref=target, send_sem=out_sem, recv_sem=in_sem,
            device_id={"tile": south if southward else north}, device_id_type=MESH,
        )

    def halo_copy(field, southward):
        source, target = (to_south, from_north) if southward else (to_north, from_south)
        way = 1 if southward else 0
        return tile_copy(source.at[field], target.at[field], sem_halo_out.at[field, way], sem_halo_in.at[field, way],
                         southward)

    def halo_copy2(chunk, block, southward):
        source, target = (ROWS, 0) if southward else (EDGE, ROWS + EDGE)
        way = 1 if southward else 0
        rows = EDGE * BLOCK
        return tile_copy(grid2.at[chunk, block, pl.ds(source * BLOCK, rows)],
                         grid2.at[chunk, block, pl.ds(target * BLOCK, rows)], sem_halo2_out.at[chunk, block, way],
                         sem_halo2_in.at[chunk, block, way], southward)

    def raw_copy(part, southward):
        rows = pl.ds(3 * part, 3)
        target = raw_north if southward else raw_south
        way = 1 if southward else 0
        return tile_copy(raw.at[rows], target.at[rows], sem_raw_out.at[part, way], sem_raw_in.at[part, way], southward)

    def begin(field):
        def pair(i, carry):
            first, second = 2 * i, 2 * i + 1
            v0 = members_v[first, field] + noise_v[0, first, field]
            v1 = members_v[second, field] + noise_v[0, second, field]
            r0, r1 = half_turn(v0), half_turn(v1)
            state[field, first] = r0
            state[field, second] = r1
            to_south[field, i] = jnp.where(upper, r0, v1)
            to_north[field, i] = jnp.where(upper, v0, r1)
            return carry

        lax.fori_loop(0, PER // 2, pair, 0, unroll=2)

    def forecast(field):
        def four(q, carry):
            for i in (2 * q, 2 * q + 1):
                top = from_north[field, i] * has_north
                bottom = from_south[field, i] * has_south
                for k, (above, below) in enumerate(((top, half_turn(bottom)), (half_turn(top), bottom))):
                    particle = 2 * i + k
                    r = state[field, particle]
                    x = jnp.concatenate([jnp.where(upper, above, r), jnp.where(upper, r, below)], axis=0)
                    for _ in range(STEPS):
                        x = (coef[field, 0] * x + coef[field, 1] * pltpu.roll(x, 1, axis=0)
                             + coef[field, 2] * pltpu.roll(x, 2 * ROWS - 1, axis=0)
                             + coef[field, 3] * pltpu.roll(x, 1, axis=1)
                             + coef[field, 4] * pltpu.roll(x, COLS - 1, axis=1))
                    v = half_turn(jnp.where(upper, x[ROWS:], x[:ROWS]))
                    result[field, particle] = v
                    if field == 0:
                        miss = v - obs_mean[0]
                        cost = obs_weight[...] * miss * miss + obs_rest[0]
                        cost = cost[:, :LANES] + cost[:, LANES:2 * LANES] + cost[:, 2 * LANES:]
                        partial[pl.ds(particle, 1), :] = jnp.sum(cost, axis=0, keepdims=True)
            return carry

        lax.fori_loop(0, PER // 4, four, 0)

    def pack(chunk, get, outgoing, incoming):
        def one(f, carry):
            for g in range(STRIPS):
                def loader(k):
                    return lambda u: get(k, PAIR * chunk + f, pl.ds(LANES * u, LANES))

                spans = [(SPAN * k, WIDE * g - EDGE, SPAN, loader(k), COLS) for k in range(PER)]
                for j in range(PER * SPAN // LANES):
                    outgoing[chunk, STRIPS * f + g, :, LANES * j:LANES * (j + 1)] = place(j, spans)
            return carry

        lax.fori_loop(0, PAIR, one, 0)
        incoming[chunk, me] = outgoing[chunk, me]

    def swap(outgoing, incoming, chunk, which):
        exchange(lambda other: outgoing.at[chunk, other], lambda mine: incoming.at[chunk, mine],
                 sem_out.at[chunk, which], sem_in.at[chunk, which])

    def unpack_noise(chunk):
        await_bytes(others(noise_recv, chunk), sem_in.at[chunk, 0])

        def one(s, carry):
            def load_from(u):
                return noise_recv[chunk, s, :, LANES * u:LANES * (u + 1)]

            for m in range(PER // 2):
                noise_pairs[chunk, PER // 2 * s + m] = place(
                    0, [(HALF * h, SPAN * (2 * m + h), SPAN, load_from, PER * SPAN) for h in range(2)])
            return carry

        lax.fori_loop(0, GROUPS, one, 0, unroll=4)

    def unpack_state(chunk):

        def one(s, carry):
            def load_from(u):
                return state_recv[chunk, s, :, LANES * u:LANES * (u + 1)]

            for k in range(PER):
                twins[chunk, PER * s + k] = place(
                    0, [(HALF * h, SPAN * k, SPAN, load_from, PER * SPAN) for h in range(2)])
            return carry

        lax.fori_loop(0, GROUPS, one, 0, unroll=2)

    def begin2(chunk, block):
        left = lane8 < HALF

        def one(i, carry):
            m = BLOCK * block + i
            old0, old1 = ancestors_s[0, 0, 2 * m], ancestors_s[0, 0, 2 * m + 1]
            v = jnp.where(left, twins[chunk, old0], twins[chunk, old1]) + noise_pairs[chunk, m]
            grid2[chunk, block, pl.ds(EDGE * BLOCK + i, ROWS, stride=BLOCK), :] = v
            return carry

        lax.fori_loop(0, BLOCK, one, 0, unroll=8)
        halo_copy2(chunk, block, True).start()
        halo_copy2(chunk, block, False).start()

    def forecast2(chunk, block):
        halo_copy2(chunk, block, True).wait_recv()
        halo_copy2(chunk, block, False).wait_recv()
        high = ROWS + 2 * EDGE

        def tall(n, r):
            return jnp.concatenate([coef2[chunk, n, r]] * (BLOCK // ROWS), axis=0)

        x = [grid2[chunk, block, BLOCK * r:BLOCK * (r + 1), :] for r in range(high)]
        x = [v * has_north if r < EDGE else v * has_south if r >= EDGE + ROWS else v for r, v in enumerate(x)]
        for s in range(1, STEPS + 1):
            new = list(x)
            for r in range(s, high - s):
                new[r] = (tall(0, r) * x[r] + tall(1, r) * x[r - 1] + tall(2, r) * x[r + 1]
                          + tall(3, r) * pltpu.roll(x[r], 1, axis=1) + tall(4, r) * pltpu.roll(x[r], LANES - 1, axis=1))
            x = new
        for r in range(ROWS):
            lone[chunk, ALL * r + BLOCK * block:ALL * r + BLOCK * (block + 1), :] = x[EDGE + r]
            low = ALL * r + PAIRS + BLOCK * block
            lone[chunk, low:low + BLOCK, :] = pltpu.roll(x[EDGE + r], HALF, axis=1)

    def pack_back(chunk):
        def one(group, carry):
            def loader(j):
                old = ancestors_s[1, 0, PER * group + j]
                tall = lone[chunk, pl.ds((old & 1) * PAIRS + (old >> 1), ROWS, stride=ALL), :]
                return lambda u: tall

            spans = [(WIDE * j, EDGE, WIDE, loader(j), LANES) for j in range(PER)]
            for n in range(PER * WIDE // LANES):
                back_send[chunk, group, :, LANES * n:LANES * (n + 1)] = place(n, spans)
            return carry

        lax.fori_loop(0, GROUPS, one, 0, unroll=4)
        back_recv[chunk, me] = back_send[chunk, me]

    def finish(chunk):
        await_bytes(others(back_recv, chunk), sem_in.at[chunk, 2])

        def one(f, carry):
            def loader(g):
                return lambda u: back_recv[chunk, STRIPS * f + g, :, LANES * u:LANES * (u + 1)]

            for j in range(PER):
                spans = [(WIDE * g, WIDE * j, WIDE, loader(g), PER * WIDE) for g in range(STRIPS)]
                for u in range(COLS // LANES):
                    out[j, PAIR * chunk + f, :, LANES * u:LANES * (u + 1)] = place(u, spans)
            return carry

        lax.fori_loop(0, PAIR, one, 0)

    lane = lax.broadcasted_iota(jnp.int32, (PER, LANES), 1)
    line = lax.broadcasted_iota(jnp.int32, (PER, LANES), 0)

    def likelihood():
        total = -0.5 * jnp.sum(partial[...], axis=1, keepdims=True)
        row = jnp.sum(jnp.where(lane == line, total, 0.0), axis=0, keepdims=True)
        like_send[...] = row
        like_recv[me] = row
        exchange(lambda other: like_send, lambda mine: like_recv.at[mine], sem_small_out.at[0], sem_small_in.at[0])

    def weigh():
        await_bytes(like_recv.at[pl.ds(0, GROUPS - 1)], sem_small_in.at[0])
        everyone = like_recv[...]
        known = lax.broadcasted_iota(jnp.int32, (GROUPS, 1, LANES), 2) < PER
        peak = jnp.max(jnp.where(known, everyone, -3.0e38), axis=0)
        peak = jnp.max(peak, axis=1, keepdims=True)
        shifted = jnp.where(known, jnp.exp(jnp.where(known, everyone - peak[None], 0.0)), 0.0)
        total = jnp.sum(jnp.sum(shifted, axis=0), axis=1, keepdims=True)
        weight = shifted / total[None]
        for g in range(GROUPS):
            own = jnp.sum(jnp.where(lane == line, weight[g], 0.0), axis=1, keepdims=True)
            weights[PER * g:PER * (g + 1), :] = jnp.broadcast_to(own, (PER, LANES))

    def average(chunk):
        def add(q, sums):
            return tuple(s + weights[pl.ds(4 * q + k, 1), :] * twins[chunk, 4 * q + k] for k, s in enumerate(sums))

        sums = lax.fori_loop(0, ALL // 4, add, (jnp.zeros((ROWS, LANES), jnp.float32),) * 4, unroll=4)
        mean_own[chunk] = (sums[0] + sums[1]) + (sums[2] + sums[3])

    place2 = lax.broadcasted_iota(jnp.int32, (PAIRS, LANES), 1)
    line2 = lax.broadcasted_iota(jnp.int32, (PAIRS, LANES), 0)

    def likelihood2():
        cost = jnp.zeros((PAIRS, LANES), jnp.float32)
        for r in range(ROWS):
            miss = lone[0, ALL * r:ALL * r + PAIRS, :] - obs2[1, r:r + 1]
            cost = cost + obs2[0, r:r + 1] * miss * miss + obs2[2, r:r + 1]
        for h in range(2):
            side = (place2 < HALF) if h == 0 else (place2 >= HALF)
            total = -0.5 * jnp.sum(jnp.where(side, cost, 0.0), axis=1, keepdims=True)
            row = jnp.sum(jnp.where(place2 == line2, total, 0.0), axis=0, keepdims=True)
            like_send2[h:h + 1, :] = row
        like_recv2[me] = like_send2[...]
        exchange(lambda other: like_send2, lambda mine: like_recv2.at[mine], sem_small_out.at[1], sem_small_in.at[1])

    def weigh2():
        await_bytes(like_recv2.at[pl.ds(0, GROUPS - 1)], sem_small_in.at[1])
        total = like_recv2[0]
        for g in range(1, GROUPS):
            total = total + like_recv2[g]
        peak = jnp.max(jnp.max(total, axis=0, keepdims=True), axis=1, keepdims=True)
        shifted = jnp.exp(total - peak)
        weight = shifted / jnp.sum(jnp.sum(shifted, axis=0, keepdims=True), axis=1, keepdims=True)
        sides = [jnp.sum(jnp.where(place2 == line2, weight[h:h + 1], 0.0), axis=1, keepdims=True) for h in range(2)]
        weights2[...] = jnp.where(place2 < HALF, sides[0], sides[1])

    def average2(chunk):
        for r in range(ROWS):
            part = weights2[...] * lone[chunk, ALL * r:ALL * r + PAIRS, :]
            mean_send2[chunk, r:r + 1, :] = jnp.sum(part, axis=0, keepdims=True)
        total = mean_send2[chunk]
        total = total + pltpu.roll(total, HALF, axis=1)
        total = jnp.where(lane8 < HALF, mean_own[chunk], total)
        mean_send2[chunk] = total
        mean_recv2[chunk, me] = total
        exchange(lambda other: mean_send2.at[chunk], lambda mine: mean_recv2.at[chunk, mine],
                 sem_small_out.at[2 + chunk], sem_small_in.at[2 + chunk])

    def write_means(chunk):
        await_bytes(others(mean_recv2, chunk), sem_small_in.at[2 + chunk])
        for c in range(CYCLES):
            for f in range(PAIR):
                def loader(g):
                    return lambda u: mean_recv2[chunk, STRIPS * f + g]

                spans = [(WIDE * g, HALF * c + EDGE, WIDE, loader(g), LANES) for g in range(STRIPS)]
                for u in range(COLS // LANES):
                    averages[c, PAIR * chunk + f, :, LANES * u:LANES * (u + 1)] = place(u, spans)

    def edge_coefficients():
        for m in range(2):
            raw[m] = half_turn(courant_v[m])
        for f in range(FIELDS):
            raw[2 + f] = half_turn(diffusion_v[f])

    def coefficients(field):
        def sixteen(m):
            mid = raw[m]
            return jnp.concatenate([jnp.where(upper, raw_north[m], mid), jnp.where(upper, mid, raw_south[m])], axis=0)

        inside = jnp.concatenate([jnp.where(upper, has_north, 1.0), jnp.where(upper, 1.0, has_south)], axis=0)
        column2 = jnp.concatenate([column, column], axis=0)
        cx, cy, d = sixteen(0), sixteen(1), sixteen(2 + field)
        coef[field, 0] = inside * (1.0 - jnp.abs(cx) - jnp.abs(cy) - 4.0 * d)
        coef[field, 1] = inside * (jnp.maximum(cx, 0.0) + d)
        coef[field, 2] = inside * (d - jnp.minimum(cx, 0.0))
        coef[field, 3] = jnp.where(column2 > 0, inside * (jnp.maximum(cy, 0.0) + d), 0.0)
        coef[field, 4] = jnp.where(column2 < COLS - 1, inside * (d - jnp.minimum(cy, 0.0)), 0.0)

    def window(get, rows):
        for g in range(STRIPS):
            spans = [(HALF * h, WIDE * g - EDGE, SPAN, lambda u: get(pl.ds(LANES * u, LANES)), COLS) for h in range(2)]
            windows[g, :rows] = place(0, spans, rows)
        return windows[strip, :rows]

    def coefficients2(chunk):
        lane16 = lax.broadcasted_iota(jnp.int32, (2 * ROWS, LANES), 1)
        used = lax.rem(lane16, HALF) < SPAN
        for n in range(5):
            here = window(lambda cols: coef[PAIR * chunk + in_pair, n, :, cols], 2 * ROWS)
            here = jnp.where(used, here, 0.0)
            for r in range(2 * ROWS):
                coef2[chunk, n, r] = jnp.broadcast_to(here[r:r + 1], (ROWS, LANES))

    def observations():
        cell = lax.broadcasted_iota(jnp.int32, (ROWS, COLS), 0) * COLS + column
        zero = jnp.zeros((ROWS, COLS), jnp.float32)

        def gather(k, sums):
            here = cell == obs_loc_s[0, k]
            precision = jnp.where(here, 1.0 / jnp.full((1, COLS), obs_var_s[0, k], jnp.float32), 0.0)
            return (sums[0] + precision,) + tuple(sums[1 + c] + precision * observed_s[c, 0, k] for c in range(CYCLES))

        sums = lax.fori_loop(0, NOBS, gather, (zero,) * (1 + CYCLES), unroll=8)
        obs_weight[...] = sums[0]
        seen = sums[0] > 0.0
        means = []
        for c in range(CYCLES):
            means.append(jnp.where(seen, sums[1 + c] / jnp.where(seen, sums[0], 1.0), 0.0))
            obs_mean[c] = means[c]

        def rest(k, sums):
            here = cell == obs_loc_s[0, k]
            precision = jnp.where(here, 1.0 / jnp.full((1, COLS), obs_var_s[0, k], jnp.float32), 0.0)
            return tuple(sums[c] + precision * (observed_s[c, 0, k] - means[c]) * (observed_s[c, 0, k] - means[c])
                         for c in range(CYCLES))

        sums = lax.fori_loop(0, NOBS, rest, (zero,) * CYCLES, unroll=8)
        for c in range(CYCLES):
            obs_rest[c] = sums[c]

    def observations2():
        inner = lax.rem(lane8, HALF)
        own = (inner >= EDGE) & (inner < EDGE + WIDE)
        first = jnp.where(in_pair == 0, 1.0, 0.0).astype(jnp.float32)
        obs2[0] = jnp.where(own, window(lambda cols: obs_weight[:, cols], ROWS), 0.0) * first
        obs2[1] = window(lambda cols: obs_mean[1, :, cols], ROWS)
        obs2[2] = jnp.where(own, window(lambda cols: obs_rest[1, :, cols], ROWS), 0.0) * first

    def noise_of(k, field, cols):
        return noise_v[1, k, field, :, cols]

    def state_of(k, field, cols):
        return result[field, k, :, cols]

    for n in (0, 1, 2, 6, 7):
        loads[n].wait()
    edge_coefficients()
    begin(0)
    begin(1)
    pl.semaphore_wait(barrier, GROUPS + 1)

    def edges(ready):
        for way in (True, False):
            halo_copy(ready, way).wait_recv()

    def send_edges(field):
        for way in (True, False):
            halo_copy(field, way).start()

    for way in (True, False):
        raw_copy(0, way).start()
    send_edges(0)
    pack(0, noise_of, noise_send, noise_recv)
    swap(noise_send, noise_recv, 0, 0)
    send_edges(1)
    for way in (True, False):
        raw_copy(1, way).start()
    for n in (3, 4, 5, 8, 9, 10, 11):
        loads[n].wait()
    for f in range(2, FIELDS):
        begin(f)
    observations()
    for way in (True, False):
        raw_copy(0, way).wait_recv()
    coefficients(0)
    edges(0)
    send_edges(2)
    forecast(0)
    likelihood()
    for way in (True, False):
        raw_copy(1, way).wait_recv()
    coefficients(1)
    edges(1)
    send_edges(3)
    forecast(1)
    pack(0, state_of, state_send, state_recv)
    swap(state_send, state_recv, 0, 1)
    pack(1, noise_of, noise_send, noise_recv)

    for f in range(2, FIELDS):
        coefficients(f)
        edges(f)
        forecast(f)
    pack(1, state_of, state_send, state_recv)
    for chunk in range(CHUNKS):
        coefficients2(chunk)
    observations2()
    unpack_noise(0)
    await_bytes(others(state_recv, 0), sem_out.at[0, 1])
    swap(noise_send, noise_recv, 1, 0)
    swap(state_send, state_recv, 1, 1)
    weigh()
    await_bytes(others(state_recv, 0), sem_in.at[0, 1])
    unpack_state(0)
    for block in range(BLOCKS):
        begin2(0, block)
    average(0)
    for block in range(BLOCKS):
        forecast2(0, block)
    likelihood2()
    pack_back(0)
    unpack_noise(1)
    await_bytes(others(state_recv, 1), sem_in.at[1, 1])
    swap(back_send, back_recv, 0, 2)
    unpack_state(1)
    for block in range(BLOCKS):
        begin2(1, block)

    weigh2()
    average2(0)
    average(1)
    for block in range(BLOCKS):
        forecast2(1, block)
    pack_back(1)
    swap(back_send, back_recv, 1, 2)
    average2(1)
    write_means(0)
    finish(0)
    finish(1)
    write_means(1)
    for chunk in range(CHUNKS):
        for which, ref in enumerate((noise_recv, state_recv, back_recv)):
            if (chunk, which) != (0, 1):
                await_bytes(others(ref, chunk), sem_out.at[chunk, which])
        await_bytes(others(mean_recv2, chunk), sem_small_out.at[2 + chunk])
    for way in (True, False):
        for f in range(FIELDS):
            halo_copy(f, way).wait_send()
        for part in range(2):
            raw_copy(part, way).wait_send()
        for chunk in range(CHUNKS):
            for block in range(BLOCKS):
                halo_copy2(chunk, block, way).wait_send()
    for n, ref in enumerate((like_recv, like_recv2)):
        await_bytes(ref.at[pl.ds(0, GROUPS - 1)], sem_small_out.at[n])


def per_device(members, noise, courant, diffusion, obs_loc, observed, obs_var, ancestors):
    f32 = jnp.float32
    anywhere = pl.BlockSpec(memory_space=pl.ANY)
    plane = (ROWS, COLS)
    one = (ROWS, LANES)
    operands = (members, noise, courant, diffusion, obs_loc, observed, obs_var, ancestors)

    def vmem(*shape):
        return pltpu.VMEM(shape, f32)

    scratch = [vmem(*a.shape) for a in operands[:4]] + [pltpu.SMEM(a.shape, a.dtype) for a in operands[4:]]
    scratch += [vmem(CHUNKS, GROUPS, ROWS, PER * SPAN) for _ in range(4)]
    scratch += [vmem(CHUNKS, GROUPS, ROWS, PER * WIDE) for _ in range(2)]
    scratch += [vmem(FIELDS, PER // 2, *plane) for _ in range(4)]
    scratch += [
        vmem(FIELDS, PER, *plane),
        vmem(FIELDS, PER, *plane),
        vmem(2 + FIELDS, *plane),
        vmem(2 + FIELDS, *plane),
        vmem(2 + FIELDS, *plane),
        vmem(FIELDS, 5, 2 * ROWS, COLS),
        vmem(*plane),
        vmem(CYCLES, *plane),
        vmem(CYCLES, *plane),
        vmem(PER, LANES),
        vmem(ALL, LANES),
        vmem(1, LANES),
        vmem(GROUPS, 1, LANES),
        vmem(CHUNKS, *one),
        vmem(CHUNKS, PAIRS, *one),
        vmem(CHUNKS, ALL, *one),
        vmem(CHUNKS, BLOCKS, (ROWS + 2 * EDGE) * BLOCK, LANES),
        vmem(CHUNKS, ROWS * ALL, LANES),
        vmem(CHUNKS, 5, 2 * ROWS, *one),
        vmem(STRIPS, 2 * ROWS, LANES),
        vmem(3, *one),
        vmem(PAIRS, LANES),
        vmem(2, LANES),
        vmem(GROUPS, 2, LANES),
        vmem(CHUNKS, *one),
        vmem(CHUNKS, GROUPS, *one),
        pltpu.SemaphoreType.DMA((12,)),
        pltpu.SemaphoreType.DMA((CHUNKS, 3)),
        pltpu.SemaphoreType.DMA((CHUNKS, 3)),
        pltpu.SemaphoreType.DMA((FIELDS, 2)),
        pltpu.SemaphoreType.DMA((FIELDS, 2)),
        pltpu.SemaphoreType.DMA((CHUNKS, BLOCKS, 2)),
        pltpu.SemaphoreType.DMA((CHUNKS, BLOCKS, 2)),
        pltpu.SemaphoreType.DMA((2, 2)),
        pltpu.SemaphoreType.DMA((2, 2)),
        pltpu.SemaphoreType.DMA((4,)),
        pltpu.SemaphoreType.DMA((4,)),
    ]
    return pl.pallas_call(
        kernel,
        out_shape=(
            jax.ShapeDtypeStruct((PER, FIELDS) + plane, f32),
            jax.ShapeDtypeStruct((CYCLES, FIELDS) + plane, f32),
        ),
        in_specs=[anywhere] * 8,
        out_specs=(pl.BlockSpec(memory_space=pltpu.VMEM), pl.BlockSpec(memory_space=pltpu.VMEM)),
        scratch_shapes=scratch,
        compiler_params=pltpu.CompilerParams(
            collective_id=0, has_side_effects=True, vmem_limit_bytes=60 * 1024 * 1024
        ),
        name="assimilate",
    )(*operands)


def solution(mesh):
    return jax.shard_map(
        per_device,
        mesh=mesh,
        in_specs=(
            P("dom", None, "tile", None),
            P(None, "dom", None, "tile", None),
            P(None, "tile", None),
            P(None, "tile", None),
            P("tile", None),
            P(None, "tile", None),
            P("tile", None),
            P(None, "tile", None),
        ),
        out_specs=(P("dom", None, "tile", None), P(None, None, "tile", None)),
        check_vma=False,
    )
```

```python
import jax
import jax.numpy as jnp
from jax import lax
from jax.experimental import pallas as pl
from jax.experimental.pallas import tpu as pltpu
from jax.sharding import PartitionSpec as P

MESH = pl.DeviceIdType.MESH
STEPS = 4
CYCLES = 2
FIELDS = 4
PER = 16
GROUPS = 16
CHIPS = 8
ALL = PER * GROUPS
PAIRS = ALL // 2
TILES = 16
ROWS = 8
COLS = 384
LANES = 128
HALF = LANES // 2
NOBS = 64
CHUNKS = 2
PAIR = 2
PARTS = 4
SLOTS = FIELDS + PAIR
STRIPS = 8
WIDE = COLS // STRIPS
EDGE = STEPS
SPAN = WIDE + 2 * EDGE
BLOCKS = 4
BLOCK = PAIRS // BLOCKS


def half_turn(x):
    return pltpu.roll(x, 4, axis=0)


def place(vector, spans, rows=ROWS):
    lane = lax.broadcasted_iota(jnp.int32, (rows, LANES), 1)
    result = None
    for begin, column, length, load, limit in spans:
        low, high = max(begin, vector * LANES), min(begin + length, (vector + 1) * LANES)
        if low >= high:
            continue
        column = column + low - begin
        low, high = low - vector * LANES, high - vector * LANES
        first = max(column, 0) // LANES
        last = min(column + high - low, limit) - 1
        for u in range(first, last // LANES + 1):
            piece = load(u)
            shift = (low - column + LANES * u) % LANES
            if shift:
                piece = pltpu.roll(piece, shift, axis=1)
            start = max(low, low - column + LANES * u)
            result = piece if result is None else jnp.where(lane >= start, piece, result)
    return result


def kernel(members, noise, courant, diffusion, obs_loc, observed, obs_var, ancestors, out, averages,
           out_v, averages_v,
           members_v, noise_v, courant_v, diffusion_v, obs_loc_s, observed_s, obs_var_s, ancestors_s,
           noise_send, noise_recv, late_send, late_recv, late_rows, state_send, state_recv, back_send, back_recv,
           to_north, to_south, from_north, from_south,
           state, result, raw, raw_north, raw_south, coef, obs_weight, obs_mean, obs_rest, partial, weights,
           like_send, like_recv, mean_own,
           noise_pairs, twins, grid2, lone, coef2, windows, obs2, weights2, like_send2, like_recv2,
           mean_send2, mean_recv2,
           sem_load, sem_store, sem_out, sem_in, sem_halo_out, sem_halo_in, sem_halo2_out, sem_halo2_in, sem_raw_out,
           sem_raw_in, sem_small_out, sem_small_in):
    me = lax.axis_index("dom")
    tile = lax.axis_index("tile")
    north = lax.rem(tile + TILES - 1, TILES)
    south = lax.rem(tile + 1, TILES)
    strip = lax.rem(me, STRIPS)
    in_pair = lax.div(me, STRIPS)
    chip = lax.div(me, 2)
    core = lax.rem(me, 2)

    def peer(step):
        return lax.rem(me + step, GROUPS)

    barrier = pltpu.get_barrier_semaphore()

    def greet(step, carry):
        pl.semaphore_signal(barrier, inc=1, device_id={"dom": peer(step)}, device_id_type=MESH)
        return carry

    for neighbour in (north, south):
        pl.semaphore_signal(barrier, inc=1, device_id={"tile": neighbour}, device_id_type=MESH)
    lax.fori_loop(1, GROUPS, greet, 0)

    loads = []

    def load(source, target):
        loads.append(pltpu.make_async_copy(source, target, sem_load.at[len(loads)]))
        loads[-1].start()

    for chunk in range(CHUNKS):
        two = pl.ds(PAIR * chunk, PAIR)
        load(members.at[:, two], members_v.at[:, two])
        load(noise.at[0, :, two], noise_v.at[0, :, two])
        load(noise.at[1, :, two], noise_v.at[1, :, two])
    for source, target in ((courant, courant_v), (diffusion, diffusion_v), (obs_loc, obs_loc_s),
                           (observed, observed_s), (obs_var, obs_var_s), (ancestors, ancestors_s)):
        load(source, target)

    upper = lax.broadcasted_iota(jnp.int32, (ROWS, COLS), 0) < 4
    upper1 = lax.broadcasted_iota(jnp.int32, (ROWS, LANES), 0) < 4
    column = lax.broadcasted_iota(jnp.int32, (ROWS, COLS), 1)
    lane8 = lax.broadcasted_iota(jnp.int32, (ROWS, LANES), 1)
    has_north = jnp.where(tile > 0, 1.0, 0.0).astype(jnp.float32)
    has_south = jnp.where(tile < TILES - 1, 1.0, 0.0).astype(jnp.float32)

    def exchange(source_of, target_of, out_sem, in_sem):
        def one(step, carry):
            other = peer(step)
            pltpu.make_async_remote_copy(
                src_ref=source_of(other), dst_ref=target_of(me), send_sem=out_sem, recv_sem=in_sem,
                device_id={"dom": other}, device_id_type=MESH,
            ).start()
            return carry

        lax.fori_loop(1, GROUPS, one, 0)

    def await_bytes(ref, sem):
        pltpu.make_async_copy(ref, ref, sem).wait()

    def others(ref, chunk):
        return ref.at[chunk, pl.ds(0, GROUPS - 1)]

    def tile_copy(source, target, out_sem, in_sem, southward):
        return pltpu.make_async_remote_copy(
            src_ref=source, dst_ref=target, send_sem=out_sem, recv_sem=in_sem,
            device_id={"tile": south if southward else north}, device_id_type=MESH,
        )

    def halo_copy(field, southward):
        source, target = (to_south, from_north) if southward else (to_north, from_south)
        way = 1 if southward else 0
        return tile_copy(source.at[field], target.at[field], sem_halo_out.at[field, way], sem_halo_in.at[field, way],
                         southward)

    def halo_copy2(chunk, block, southward):
        source, target = (ROWS, 0) if southward else (EDGE, ROWS + EDGE)
        way = 1 if southward else 0
        rows = EDGE * BLOCK
        return tile_copy(grid2.at[chunk, block, pl.ds(source * BLOCK, rows)],
                         grid2.at[chunk, block, pl.ds(target * BLOCK, rows)], sem_halo2_out.at[chunk, block, way],
                         sem_halo2_in.at[chunk, block, way], southward)

    def raw_copy(part, southward):
        rows = pl.ds(3 * part, 3)
        target = raw_north if southward else raw_south
        way = 1 if southward else 0
        return tile_copy(raw.at[rows], target.at[rows], sem_raw_out.at[part, way], sem_raw_in.at[part, way], southward)

    def begin(field):
        def start_of(particle):
            if field < FIELDS:
                return members_v[particle, field] + noise_v[0, particle, field]
            return noise_v[1, particle, field - PAIR]

        def pair(i, carry):
            first, second = 2 * i, 2 * i + 1
            v0, v1 = start_of(first), start_of(second)
            r0, r1 = half_turn(v0), half_turn(v1)
            state[field, first] = r0
            state[field, second] = r1
            to_south[field, i] = jnp.where(upper, r0, v1)
            to_north[field, i] = jnp.where(upper, v0, r1)
            return carry

        lax.fori_loop(0, PER // 2, pair, 0, unroll=2)

    def forecast(field):
        by = field if field < FIELDS else field - PAIR

        def four(q, carry):
            for i in (2 * q, 2 * q + 1):
                top = from_north[field, i] * has_north
                bottom = from_south[field, i] * has_south
                for k, (above, below) in enumerate(((top, half_turn(bottom)), (half_turn(top), bottom))):
                    particle = 2 * i + k
                    r = state[field, particle]
                    x = jnp.concatenate([jnp.where(upper, above, r), jnp.where(upper, r, below)], axis=0)
                    for _ in range(STEPS):
                        x = (coef[by, 0] * x + coef[by, 1] * pltpu.roll(x, 1, axis=0)
                             + coef[by, 2] * pltpu.roll(x, 2 * ROWS - 1, axis=0)
                             + coef[by, 3] * pltpu.roll(x, 1, axis=1)
                             + coef[by, 4] * pltpu.roll(x, COLS - 1, axis=1))
                    v = half_turn(jnp.where(upper, x[ROWS:], x[:ROWS]))
                    result[field, particle] = v
                    if field == 0:
                        miss = v - obs_mean[0]
                        cost = obs_weight[...] * miss * miss + obs_rest[0]
                        cost = cost[:, :LANES] + cost[:, LANES:2 * LANES] + cost[:, 2 * LANES:]
                        partial[pl.ds(particle, 1), :] = jnp.sum(cost, axis=0, keepdims=True)
            return carry

        lax.fori_loop(0, PER // 4, four, 0)

    def pack(chunk, get, outgoing, incoming):
        def one(f, carry):
            for g in range(STRIPS):
                def loader(k):
                    return lambda u: get(k, PAIR * chunk + f, pl.ds(LANES * u, LANES))

                spans = [(SPAN * k, WIDE * g - EDGE, SPAN, loader(k), COLS) for k in range(PER)]
                for j in range(PER * SPAN // LANES):
                    outgoing[chunk, STRIPS * f + g, :, LANES * j:LANES * (j + 1)] = place(j, spans)
            return carry

        lax.fori_loop(0, PAIR, one, 0)
        incoming[chunk, me] = outgoing[chunk, me]

    def swap(outgoing, incoming, chunk, which):
        exchange(lambda other: outgoing.at[chunk, other], lambda mine: incoming.at[chunk, mine],
                 sem_out.at[chunk, which], sem_in.at[chunk, which])

    def pack_late():
        def one(f, carry):
            for g in range(STRIPS):
                def loader(k):
                    return lambda u: result[FIELDS + f, k, :, pl.ds(LANES * u, LANES)]

                spans = [(WIDE * k, WIDE * g, WIDE, loader(k), COLS) for k in range(PER)]
                for j in range(PER * WIDE // LANES):
                    late_send[STRIPS * f + g, :, LANES * j:LANES * (j + 1)] = place(j, spans)
            return carry

        lax.fori_loop(0, PAIR, one, 0)
        late_recv[me] = late_send[me]

    def swap_late():
        exchange(lambda other: late_send.at[other], lambda mine: late_recv.at[mine], sem_out.at[1, 0], sem_in.at[1, 0])

    def add_late():
        await_bytes(late_recv.at[pl.ds(0, GROUPS - 1)], sem_in.at[1, 0])

        def one(s, carry):
            def load_from(u):
                return late_recv[s, :, LANES * u:LANES * (u + 1)]

            for m in range(PER // 2):
                late_rows[pl.ds(PER // 2 * s + m, ROWS, stride=PAIRS), :] = place(
                    0, [(HALF * h + EDGE, WIDE * (2 * m + h), WIDE, load_from, PER * WIDE) for h in range(2)])
            return carry

        lax.fori_loop(0, GROUPS, one, 0, unroll=4)

    def sum_late():
        for r in range(ROWS):
            x = lone[1, ALL * r:ALL * r + PAIRS, :] + late_rows[PAIRS * r:PAIRS * (r + 1), :]
            lone[1, ALL * r:ALL * r + PAIRS, :] = x
            lone[1, ALL * r + PAIRS:ALL * (r + 1), :] = pltpu.roll(x, HALF, axis=1)

    def unpack_noise(chunk):
        await_bytes(others(noise_recv, chunk), sem_in.at[chunk, 0])

        def one(s, carry):
            def load_from(u):
                return noise_recv[chunk, s, :, LANES * u:LANES * (u + 1)]

            for m in range(PER // 2):
                noise_pairs[chunk, PER // 2 * s + m] = place(
                    0, [(HALF * h, SPAN * (2 * m + h), SPAN, load_from, PER * SPAN) for h in range(2)])
            return carry

        lax.fori_loop(0, GROUPS, one, 0, unroll=4)

    def unpack_state(chunk):

        def one(s, carry):
            def load_from(u):
                return state_recv[chunk, s, :, LANES * u:LANES * (u + 1)]

            for k in range(PER):
                twins[chunk, PER * s + k] = place(
                    0, [(HALF * h, SPAN * k, SPAN, load_from, PER * SPAN) for h in range(2)])
            return carry

        lax.fori_loop(0, GROUPS, one, 0, unroll=2)

    def begin2(chunk, block):
        left = lane8 < HALF

        def one(i, carry):
            m = BLOCK * block + i
            old0, old1 = ancestors_s[0, 0, 2 * m], ancestors_s[0, 0, 2 * m + 1]
            v = jnp.where(left, twins[chunk, old0], twins[chunk, old1])
            if chunk == 0:
                v = v + noise_pairs[chunk, m]
            grid2[chunk, block, pl.ds(EDGE * BLOCK + i, ROWS, stride=BLOCK), :] = v
            return carry

        lax.fori_loop(0, BLOCK, one, 0, unroll=8)
        halo_copy2(chunk, block, True).start()
        halo_copy2(chunk, block, False).start()

    def forecast2(chunk, block):
        halo_copy2(chunk, block, True).wait_recv()
        halo_copy2(chunk, block, False).wait_recv()
        high = ROWS + 2 * EDGE

        def tall(n, r):
            return jnp.concatenate([coef2[chunk, n, r]] * (BLOCK // ROWS), axis=0)

        x = [grid2[chunk, block, BLOCK * r:BLOCK * (r + 1), :] for r in range(high)]
        x = [v * has_north if r < EDGE else v * has_south if r >= EDGE + ROWS else v for r, v in enumerate(x)]
        for s in range(1, STEPS + 1):
            new = list(x)
            for r in range(s, high - s):
                new[r] = (tall(0, r) * x[r] + tall(1, r) * x[r - 1] + tall(2, r) * x[r + 1]
                          + tall(3, r) * pltpu.roll(x[r], 1, axis=1) + tall(4, r) * pltpu.roll(x[r], LANES - 1, axis=1))
            x = new
        for r in range(ROWS):
            lone[chunk, ALL * r + BLOCK * block:ALL * r + BLOCK * (block + 1), :] = x[EDGE + r]
            if chunk == 0:
                low = ALL * r + PAIRS + BLOCK * block
                lone[chunk, low:low + BLOCK, :] = pltpu.roll(x[EDGE + r], HALF, axis=1)

    def pack_back(chunk):
        def one(group, carry):
            def loader(j):
                old = ancestors_s[1, 0, PER * group + j]
                tall = lone[chunk, pl.ds((old & 1) * PAIRS + (old >> 1), ROWS, stride=ALL), :]
                return lambda u: tall

            spans = [(WIDE * j, EDGE, WIDE, loader(j), LANES) for j in range(PER)]
            for n in range(PER * WIDE // LANES):
                back_send[chunk, group, :, LANES * n:LANES * (n + 1)] = place(n, spans)
            return carry

        lax.fori_loop(0, GROUPS, one, 0, unroll=4)
        back_recv[chunk, me] = back_send[chunk, me]

    def stores(chunk):
        two = pl.ds(PAIR * chunk, PAIR)
        return (pltpu.make_async_copy(out_v.at[:, two], out.at[:, two], sem_store.at[chunk, 0]),
                pltpu.make_async_copy(averages_v.at[:, two], averages.at[:, two], sem_store.at[chunk, 1]))

    def finish(chunk):
        await_bytes(others(back_recv, chunk), sem_in.at[chunk, 2])

        def one(f, carry):
            def loader(g):
                return lambda u: back_recv[chunk, STRIPS * f + g, :, LANES * u:LANES * (u + 1)]

            for j in range(PER):
                spans = [(WIDE * g, WIDE * j, WIDE, loader(g), PER * WIDE) for g in range(STRIPS)]
                for u in range(COLS // LANES):
                    out_v[j, PAIR * chunk + f, :, LANES * u:LANES * (u + 1)] = place(u, spans)
            return carry

        lax.fori_loop(0, PAIR, one, 0)

    lane = lax.broadcasted_iota(jnp.int32, (PER, LANES), 1)
    line = lax.broadcasted_iota(jnp.int32, (PER, LANES), 0)

    def likelihood():
        total = -0.5 * jnp.sum(partial[...], axis=1, keepdims=True)
        row = jnp.sum(jnp.where(lane == line, total, 0.0), axis=0, keepdims=True)
        like_send[...] = row
        like_recv[me] = row
        exchange(lambda other: like_send, lambda mine: like_recv.at[mine], sem_small_out.at[0], sem_small_in.at[0])

    def weigh():
        await_bytes(like_recv.at[pl.ds(0, GROUPS - 1)], sem_small_in.at[0])
        everyone = like_recv[...]
        known = lax.broadcasted_iota(jnp.int32, (GROUPS, 1, LANES), 2) < PER
        peak = jnp.max(jnp.where(known, everyone, -3.0e38), axis=0)
        peak = jnp.max(peak, axis=1, keepdims=True)
        shifted = jnp.where(known, jnp.exp(jnp.where(known, everyone - peak[None], 0.0)), 0.0)
        total = jnp.sum(jnp.sum(shifted, axis=0), axis=1, keepdims=True)
        weight = shifted / total[None]
        for g in range(GROUPS):
            own = jnp.sum(jnp.where(lane == line, weight[g], 0.0), axis=1, keepdims=True)
            weights[PER * g:PER * (g + 1), :] = jnp.broadcast_to(own, (PER, LANES))

    def average(chunk):
        def add(q, sums):
            return tuple(s + weights[pl.ds(4 * q + k, 1), :] * twins[chunk, 4 * q + k] for k, s in enumerate(sums))

        sums = lax.fori_loop(0, ALL // 4, add, (jnp.zeros((ROWS, LANES), jnp.float32),) * 4, unroll=4)
        mean_own[chunk] = (sums[0] + sums[1]) + (sums[2] + sums[3])

    place2 = lax.broadcasted_iota(jnp.int32, (PAIRS, LANES), 1)
    line2 = lax.broadcasted_iota(jnp.int32, (PAIRS, LANES), 0)

    def likelihood2():
        cost = jnp.zeros((PAIRS, LANES), jnp.float32)
        for r in range(ROWS):
            miss = lone[0, ALL * r:ALL * r + PAIRS, :] - obs2[1, r:r + 1]
            cost = cost + obs2[0, r:r + 1] * miss * miss + obs2[2, r:r + 1]
        for h in range(2):
            side = (place2 < HALF) if h == 0 else (place2 >= HALF)
            total = -0.5 * jnp.sum(jnp.where(side, cost, 0.0), axis=1, keepdims=True)
            row = jnp.sum(jnp.where(place2 == line2, total, 0.0), axis=0, keepdims=True)
            like_send2[h:h + 1, :] = row
        like_recv2[me] = like_send2[...]
        exchange(lambda other: like_send2, lambda mine: like_recv2.at[mine], sem_small_out.at[1], sem_small_in.at[1])

    def weigh2():
        await_bytes(like_recv2.at[pl.ds(0, GROUPS - 1)], sem_small_in.at[1])
        total = like_recv2[0]
        for g in range(1, GROUPS):
            total = total + like_recv2[g]
        peak = jnp.max(jnp.max(total, axis=0, keepdims=True), axis=1, keepdims=True)
        shifted = jnp.exp(total - peak)
        weight = shifted / jnp.sum(jnp.sum(shifted, axis=0, keepdims=True), axis=1, keepdims=True)
        sides = [jnp.sum(jnp.where(place2 == line2, weight[h:h + 1], 0.0), axis=1, keepdims=True) for h in range(2)]
        weights2[...] = jnp.where(place2 < HALF, sides[0], sides[1])

    def average2(chunk):
        for r in range(ROWS):
            part = weights2[...] * lone[chunk, ALL * r:ALL * r + PAIRS, :]
            mean_send2[chunk, r:r + 1, :] = jnp.sum(part, axis=0, keepdims=True)
        total = mean_send2[chunk]
        total = total + pltpu.roll(total, HALF, axis=1)
        total = jnp.where(lane8 < HALF, mean_own[chunk], total)
        mean_send2[chunk] = total
        mean_recv2[chunk, core, chip] = total

        def one(step, carry):
            pltpu.make_async_remote_copy(
                src_ref=mean_send2.at[chunk], dst_ref=mean_recv2.at[chunk, core, chip],
                send_sem=sem_small_out.at[2 + chunk], recv_sem=sem_small_in.at[2 + chunk],
                device_id={"dom": 2 * lax.rem(chip + step, CHIPS) + core}, device_id_type=MESH,
            ).start()
            return carry

        lax.fori_loop(1, CHIPS, one, 0)

    def means_across(chunk):
        return pltpu.make_async_remote_copy(
            src_ref=mean_recv2.at[chunk, core], dst_ref=mean_recv2.at[chunk, core],
            send_sem=sem_small_out.at[4 + chunk], recv_sem=sem_small_in.at[4 + chunk],
            device_id={"dom": 2 * chip + 1 - core}, device_id_type=MESH,
        )

    def pass_means(chunk):
        await_bytes(mean_recv2.at[chunk, 0, pl.ds(0, CHIPS - 1)], sem_small_in.at[2 + chunk])
        means_across(chunk).start()

    def write_means(chunk):
        means_across(chunk).wait_recv()
        for c in range(CYCLES):
            for f in range(PAIR):
                def loader(g):
                    return lambda u: mean_recv2[chunk, g % 2, (STRIPS * f + g) // 2]

                spans = [(WIDE * g, HALF * c + EDGE, WIDE, loader(g), LANES) for g in range(STRIPS)]
                for u in range(COLS // LANES):
                    averages_v[c, PAIR * chunk + f, :, LANES * u:LANES * (u + 1)] = place(u, spans)

    def edge_coefficients():
        for m in range(2):
            raw[m] = half_turn(courant_v[m])
        for f in range(FIELDS):
            raw[2 + f] = half_turn(diffusion_v[f])

    def coefficients(field):
        def sixteen(m):
            mid = raw[m]
            return jnp.concatenate([jnp.where(upper, raw_north[m], mid), jnp.where(upper, mid, raw_south[m])], axis=0)

        inside = jnp.concatenate([jnp.where(upper, has_north, 1.0), jnp.where(upper, 1.0, has_south)], axis=0)
        column2 = jnp.concatenate([column, column], axis=0)
        cx, cy, d = sixteen(0), sixteen(1), sixteen(2 + field)
        coef[field, 0] = inside * (1.0 - jnp.abs(cx) - jnp.abs(cy) - 4.0 * d)
        coef[field, 1] = inside * (jnp.maximum(cx, 0.0) + d)
        coef[field, 2] = inside * (d - jnp.minimum(cx, 0.0))
        coef[field, 3] = jnp.where(column2 > 0, inside * (jnp.maximum(cy, 0.0) + d), 0.0)
        coef[field, 4] = jnp.where(column2 < COLS - 1, inside * (d - jnp.minimum(cy, 0.0)), 0.0)

    def window(get, rows):
        for g in range(STRIPS):
            spans = [(HALF * h, WIDE * g - EDGE, SPAN, lambda u: get(pl.ds(LANES * u, LANES)), COLS) for h in range(2)]
            windows[g, :rows] = place(0, spans, rows)
        return windows[strip, :rows]

    def coefficients2(chunk):
        lane16 = lax.broadcasted_iota(jnp.int32, (2 * ROWS, LANES), 1)
        used = lax.rem(lane16, HALF) < SPAN
        for n in range(5):
            here = window(lambda cols: coef[PAIR * chunk + in_pair, n, :, cols], 2 * ROWS)
            here = jnp.where(used, here, 0.0)
            for r in range(2 * ROWS):
                coef2[chunk, n, r] = jnp.broadcast_to(here[r:r + 1], (ROWS, LANES))

    def observations():
        cell = lax.broadcasted_iota(jnp.int32, (ROWS, COLS), 0) * COLS + column
        zero = jnp.zeros((ROWS, COLS), jnp.float32)

        def gather(k, sums):
            here = cell == obs_loc_s[0, k]
            precision = jnp.where(here, 1.0 / jnp.full((1, COLS), obs_var_s[0, k], jnp.float32), 0.0)
            return (sums[0] + precision,) + tuple(sums[1 + c] + precision * observed_s[c, 0, k] for c in range(CYCLES))

        sums = lax.fori_loop(0, NOBS, gather, (zero,) * (1 + CYCLES), unroll=8)
        obs_weight[...] = sums[0]
        seen = sums[0] > 0.0
        means = []
        for c in range(CYCLES):
            means.append(jnp.where(seen, sums[1 + c] / jnp.where(seen, sums[0], 1.0), 0.0))
            obs_mean[c] = means[c]

        def rest(k, sums):
            here = cell == obs_loc_s[0, k]
            precision = jnp.where(here, 1.0 / jnp.full((1, COLS), obs_var_s[0, k], jnp.float32), 0.0)
            return tuple(sums[c] + precision * (observed_s[c, 0, k] - means[c]) * (observed_s[c, 0, k] - means[c])
                         for c in range(CYCLES))

        sums = lax.fori_loop(0, NOBS, rest, (zero,) * CYCLES, unroll=8)
        for c in range(CYCLES):
            obs_rest[c] = sums[c]

    def observations2():
        inner = lax.rem(lane8, HALF)
        own = (inner >= EDGE) & (inner < EDGE + WIDE)
        first = jnp.where(in_pair == 0, 1.0, 0.0).astype(jnp.float32)
        obs2[0] = jnp.where(own, window(lambda cols: obs_weight[:, cols], ROWS), 0.0) * first
        obs2[1] = window(lambda cols: obs_mean[1, :, cols], ROWS)
        obs2[2] = jnp.where(own, window(lambda cols: obs_rest[1, :, cols], ROWS), 0.0) * first

    def noise_of(k, field, cols):
        return noise_v[1, k, field, :, cols]

    def state_of(k, field, cols):
        return result[field, k, :, cols]

    for n in (0, 1, 2, 6, 7):
        loads[n].wait()
    edge_coefficients()
    begin(0)
    begin(1)
    pl.semaphore_wait(barrier, GROUPS + 1)

    def edges(ready):
        for way in (True, False):
            halo_copy(ready, way).wait_recv()

    def send_edges(field):
        for way in (True, False):
            halo_copy(field, way).start()

    for way in (True, False):
        raw_copy(0, way).start()
    send_edges(0)
    pack(0, noise_of, noise_send, noise_recv)
    swap(noise_send, noise_recv, 0, 0)
    send_edges(1)
    for way in (True, False):
        raw_copy(1, way).start()
    for n in (3, 4, 5, 8, 9, 10, 11):
        loads[n].wait()
    for f in range(2, FIELDS):
        begin(f)
    observations()
    for way in (True, False):
        raw_copy(0, way).wait_recv()
    coefficients(0)
    edges(0)
    send_edges(2)
    forecast(0)
    likelihood()
    for way in (True, False):
        raw_copy(1, way).wait_recv()
    coefficients(1)
    edges(1)
    send_edges(3)
    forecast(1)
    pack(0, state_of, state_send, state_recv)
    swap(state_send, state_recv, 0, 1)
    for f in range(2, FIELDS):
        coefficients(f)
        edges(f)
        begin(f + PAIR)
        send_edges(f + PAIR)
        forecast(f)
    pack(1, state_of, state_send, state_recv)
    swap(state_send, state_recv, 1, 1)
    for chunk in range(CHUNKS):
        coefficients2(chunk)
    observations2()
    unpack_noise(0)
    for f in range(FIELDS, SLOTS):
        edges(f)
        forecast(f)
    pack_late()
    swap_late()
    weigh()
    await_bytes(others(state_recv, 0), sem_in.at[0, 1])
    unpack_state(0)
    for block in range(BLOCKS):
        begin2(0, block)
    average(0)
    for block in range(BLOCKS):
        forecast2(0, block)
    likelihood2()
    pack_back(0)
    swap(back_send, back_recv, 0, 2)
    await_bytes(others(state_recv, 1), sem_in.at[1, 1])
    unpack_state(1)
    for block in range(BLOCKS):
        begin2(1, block)
    weigh2()
    average2(0)
    average(1)
    for block in range(BLOCKS):
        forecast2(1, block)
    add_late()
    sum_late()
    average2(1)
    pack_back(1)
    swap(back_send, back_recv, 1, 2)
    pass_means(0)
    finish(0)
    write_means(0)
    for copy in stores(0):
        copy.start()
    pass_means(1)
    finish(1)
    stores(1)[0].start()
    write_means(1)
    stores(1)[1].start()
    await_bytes(others(noise_recv, 0), sem_out.at[0, 0])
    await_bytes(late_recv.at[pl.ds(0, GROUPS - 1)], sem_out.at[1, 0])
    for chunk in range(CHUNKS):
        await_bytes(others(state_recv, chunk), sem_out.at[chunk, 1])
    for chunk in range(CHUNKS):
        await_bytes(others(back_recv, chunk), sem_out.at[chunk, 2])
        await_bytes(mean_recv2.at[chunk, 0, pl.ds(0, CHIPS - 1)], sem_small_out.at[2 + chunk])
        means_across(chunk).wait_send()
        for copy in stores(chunk):
            copy.wait()
    for way in (True, False):
        for f in range(SLOTS):
            halo_copy(f, way).wait_send()
        for part in range(2):
            raw_copy(part, way).wait_send()
        for chunk in range(CHUNKS):
            for block in range(BLOCKS):
                halo_copy2(chunk, block, way).wait_send()
    for n, ref in enumerate((like_recv, like_recv2)):
        await_bytes(ref.at[pl.ds(0, GROUPS - 1)], sem_small_out.at[n])


def hand_over(ensemble, averages, ensemble_out, averages_out, sem):
    size = PER // PARTS
    copies = [pltpu.make_async_copy(ensemble.at[pl.ds(size * n, size)], ensemble_out.at[pl.ds(size * n, size)], sem.at[n])
              for n in range(PARTS)]
    copies.append(pltpu.make_async_copy(averages, averages_out, sem.at[PARTS]))
    for copy in copies:
        copy.start()
    for copy in copies:
        copy.wait()


def per_device(members, noise, courant, diffusion, obs_loc, observed, obs_var, ancestors):
    f32 = jnp.float32
    anywhere = pl.BlockSpec(memory_space=pl.ANY)
    plane = (ROWS, COLS)
    one = (ROWS, LANES)
    operands = (members, noise, courant, diffusion, obs_loc, observed, obs_var, ancestors)

    def vmem(*shape):
        return pltpu.VMEM(shape, f32)

    scratch = [vmem(PER, FIELDS, *plane), vmem(CYCLES, FIELDS, *plane)]
    scratch += [vmem(*a.shape) for a in operands[:4]] + [pltpu.SMEM(a.shape, a.dtype) for a in operands[4:]]
    scratch += [vmem(1, GROUPS, ROWS, PER * SPAN) for _ in range(2)]
    scratch += [vmem(GROUPS, ROWS, PER * WIDE) for _ in range(2)] + [vmem(ROWS * PAIRS, LANES)]
    scratch += [vmem(CHUNKS, GROUPS, ROWS, PER * SPAN) for _ in range(2)]
    scratch += [vmem(CHUNKS, GROUPS, ROWS, PER * WIDE) for _ in range(2)]
    scratch += [vmem(SLOTS, PER // 2, *plane) for _ in range(4)]
    scratch += [
        vmem(SLOTS, PER, *plane),
        vmem(SLOTS, PER, *plane),
        vmem(2 + FIELDS, *plane),
        vmem(2 + FIELDS, *plane),
        vmem(2 + FIELDS, *plane),
        vmem(FIELDS, 5, 2 * ROWS, COLS),
        vmem(*plane),
        vmem(CYCLES, *plane),
        vmem(CYCLES, *plane),
        vmem(PER, LANES),
        vmem(ALL, LANES),
        vmem(1, LANES),
        vmem(GROUPS, 1, LANES),
        vmem(CHUNKS, *one),
        vmem(1, PAIRS, *one),
        vmem(CHUNKS, ALL, *one),
        vmem(CHUNKS, BLOCKS, (ROWS + 2 * EDGE) * BLOCK, LANES),
        vmem(CHUNKS, ROWS * ALL, LANES),
        vmem(CHUNKS, 5, 2 * ROWS, *one),
        vmem(STRIPS, 2 * ROWS, LANES),
        vmem(3, *one),
        vmem(PAIRS, LANES),
        vmem(2, LANES),
        vmem(GROUPS, 2, LANES),
        vmem(CHUNKS, *one),
        vmem(CHUNKS, 2, CHIPS, *one),
        pltpu.SemaphoreType.DMA((12,)),
        pltpu.SemaphoreType.DMA((CHUNKS, 2)),
        pltpu.SemaphoreType.DMA((CHUNKS, 3)),
        pltpu.SemaphoreType.DMA((CHUNKS, 3)),
        pltpu.SemaphoreType.DMA((SLOTS, 2)),
        pltpu.SemaphoreType.DMA((SLOTS, 2)),
        pltpu.SemaphoreType.DMA((CHUNKS, BLOCKS, 2)),
        pltpu.SemaphoreType.DMA((CHUNKS, BLOCKS, 2)),
        pltpu.SemaphoreType.DMA((2, 2)),
        pltpu.SemaphoreType.DMA((2, 2)),
        pltpu.SemaphoreType.DMA((6,)),
        pltpu.SemaphoreType.DMA((6,)),
    ]
    results = pl.pallas_call(
        kernel,
        out_shape=(
            jax.ShapeDtypeStruct((PER, FIELDS) + plane, f32),
            jax.ShapeDtypeStruct((CYCLES, FIELDS) + plane, f32),
        ),
        in_specs=[anywhere] * 8,
        out_specs=(anywhere, anywhere),
        scratch_shapes=scratch,
        compiler_params=pltpu.CompilerParams(
            collective_id=0, has_side_effects=True, vmem_limit_bytes=60 * 1024 * 1024
        ),
        name="assimilate",
    )(*operands)
    return pl.pallas_call(
        hand_over,
        out_shape=tuple(jax.ShapeDtypeStruct(r.shape, f32) for r in results),
        in_specs=[anywhere] * 2,
        out_specs=(anywhere, anywhere),
        scratch_shapes=[pltpu.SemaphoreType.DMA((PARTS + 1,))],
        compiler_params=pltpu.CompilerParams(vmem_limit_bytes=60 * 1024 * 1024),
        name="hand_over",
    )(*results)


def solution(mesh):
    return jax.shard_map(
        per_device,
        mesh=mesh,
        in_specs=(
            P("dom", None, "tile", None),
            P(None, "dom", None, "tile", None),
            P(None, "tile", None),
            P(None, "tile", None),
            P("tile", None),
            P(None, "tile", None),
            P("tile", None),
            P(None, "tile", None),
        ),
        out_specs=(P("dom", None, "tile", None), P(None, None, "tile", None)),
        check_vma=False,
    )
```

```python
import jax
import jax.numpy as jnp
from jax import lax
from jax.experimental import pallas as pl
from jax.experimental.pallas import tpu as pltpu
from jax.sharding import PartitionSpec as P

MESH = pl.DeviceIdType.MESH
STEPS = 4
CYCLES = 2
FIELDS = 4
PER = 16
GROUPS = 16
CHIPS = 8
ALL = PER * GROUPS
PAIRS = ALL // 2
TILES = 16
ROWS = 8
COLS = 384
LANES = 128
HALF = LANES // 2
NOBS = 64
CHUNKS = 2
PAIR = 2
PARTS = 4
SLOTS = FIELDS + PAIR
STRIPS = 8
WIDE = COLS // STRIPS
EDGE = STEPS
SPAN = WIDE + 2 * EDGE
BLOCKS = 4
BLOCK = PAIRS // BLOCKS


def half_turn(x):
    return pltpu.roll(x, 4, axis=0)


def place(vector, spans, rows=ROWS):
    lane = lax.broadcasted_iota(jnp.int32, (rows, LANES), 1)
    result = None
    for begin, column, length, load, limit in spans:
        low, high = max(begin, vector * LANES), min(begin + length, (vector + 1) * LANES)
        if low >= high:
            continue
        column = column + low - begin
        low, high = low - vector * LANES, high - vector * LANES
        first = max(column, 0) // LANES
        last = min(column + high - low, limit) - 1
        for u in range(first, last // LANES + 1):
            piece = load(u)
            shift = (low - column + LANES * u) % LANES
            if shift:
                piece = pltpu.roll(piece, shift, axis=1)
            start = max(low, low - column + LANES * u)
            result = piece if result is None else jnp.where(lane >= start, piece, result)
    return result


def kernel(members, noise, courant, diffusion, obs_loc, observed, obs_var, ancestors, out, averages,
           out_v, averages_v,
           members_v, noise_v, courant_v, diffusion_v, obs_loc_s, observed_s, obs_var_s, ancestors_s,
           noise_send, noise_recv, late_send, late_recv, late_rows, state_send, state_recv, back_send, back_recv,
           to_north, to_south, from_north, from_south,
           state, result, raw, raw_north, raw_south, coef, obs_weight, obs_mean, obs_rest, partial, weights,
           like_send, like_recv, mean_own,
           noise_pairs, twins, grid2, lone, coef2, windows, obs2, weights2, like_send2, like_recv2,
           mean_send2, mean_recv2,
           sem_load, sem_store, sem_out, sem_in, sem_halo_out, sem_halo_in, sem_halo2_out, sem_halo2_in, sem_raw_out,
           sem_raw_in, sem_small_out, sem_small_in):
    me = lax.axis_index("dom")
    tile = lax.axis_index("tile")
    north = lax.rem(tile + TILES - 1, TILES)
    south = lax.rem(tile + 1, TILES)
    strip = lax.rem(me, STRIPS)
    in_pair = lax.div(me, STRIPS)
    chip = lax.div(me, 2)
    core = lax.rem(me, 2)

    def peer(step):
        return lax.rem(me + step, GROUPS)

    barrier = pltpu.get_barrier_semaphore()

    def greet(step, carry):
        pl.semaphore_signal(barrier, inc=1, device_id={"dom": peer(step)}, device_id_type=MESH)
        return carry

    for neighbour in (north, south):
        pl.semaphore_signal(barrier, inc=1, device_id={"tile": neighbour}, device_id_type=MESH)
    lax.fori_loop(1, GROUPS, greet, 0)

    loads = []

    def load(source, target):
        loads.append(pltpu.make_async_copy(source, target, sem_load.at[len(loads)]))
        loads[-1].start()

    for chunk in range(CHUNKS):
        two = pl.ds(PAIR * chunk, PAIR)
        load(noise.at[1, :, two], noise_v.at[1, :, two])
        load(members.at[:, two], members_v.at[:, two])
        load(noise.at[0, :, two], noise_v.at[0, :, two])
    for source, target in ((courant, courant_v), (diffusion, diffusion_v), (obs_loc, obs_loc_s),
                           (observed, observed_s), (obs_var, obs_var_s), (ancestors, ancestors_s)):
        load(source, target)

    upper = lax.broadcasted_iota(jnp.int32, (ROWS, COLS), 0) < 4
    upper1 = lax.broadcasted_iota(jnp.int32, (ROWS, LANES), 0) < 4
    column = lax.broadcasted_iota(jnp.int32, (ROWS, COLS), 1)
    lane8 = lax.broadcasted_iota(jnp.int32, (ROWS, LANES), 1)
    has_north = jnp.where(tile > 0, 1.0, 0.0).astype(jnp.float32)
    has_south = jnp.where(tile < TILES - 1, 1.0, 0.0).astype(jnp.float32)

    def exchange(source_of, target_of, out_sem, in_sem):
        def one(step, carry):
            near = lax.div(step + 1, 2)
            other = peer(jnp.where(lax.rem(step, 2) == 1, near, GROUPS - near))
            pltpu.make_async_remote_copy(
                src_ref=source_of(other), dst_ref=target_of(me), send_sem=out_sem, recv_sem=in_sem,
                device_id={"dom": other}, device_id_type=MESH,
            ).start()
            return carry

        lax.fori_loop(1, GROUPS, one, 0)

    def await_bytes(ref, sem):
        pltpu.make_async_copy(ref, ref, sem).wait()

    def others(ref, chunk):
        return ref.at[chunk, pl.ds(0, GROUPS - 1)]

    def tile_copy(source, target, out_sem, in_sem, southward):
        return pltpu.make_async_remote_copy(
            src_ref=source, dst_ref=target, send_sem=out_sem, recv_sem=in_sem,
            device_id={"tile": south if southward else north}, device_id_type=MESH,
        )

    def halo_copy(field, southward):
        source, target = (to_south, from_north) if southward else (to_north, from_south)
        way = 1 if southward else 0
        return tile_copy(source.at[field], target.at[field], sem_halo_out.at[field, way], sem_halo_in.at[field, way],
                         southward)

    def halo_copy2(chunk, block, southward):
        source, target = (ROWS, 0) if southward else (EDGE, ROWS + EDGE)
        way = 1 if southward else 0
        rows = EDGE * BLOCK
        return tile_copy(grid2.at[chunk, block, pl.ds(source * BLOCK, rows)],
                         grid2.at[chunk, block, pl.ds(target * BLOCK, rows)], sem_halo2_out.at[chunk, block, way],
                         sem_halo2_in.at[chunk, block, way], southward)

    def raw_copy(part, southward):
        rows = pl.ds(3 * part, 3)
        target = raw_north if southward else raw_south
        way = 1 if southward else 0
        return tile_copy(raw.at[rows], target.at[rows], sem_raw_out.at[part, way], sem_raw_in.at[part, way], southward)

    def begin(field):
        def start_of(particle):
            if field < FIELDS:
                return members_v[particle, field] + noise_v[0, particle, field]
            return noise_v[1, particle, field - PAIR]

        def pair(i, carry):
            first, second = 2 * i, 2 * i + 1
            v0, v1 = start_of(first), start_of(second)
            r0, r1 = half_turn(v0), half_turn(v1)
            state[field, first] = r0
            state[field, second] = r1
            to_south[field, i] = jnp.where(upper, r0, v1)
            to_north[field, i] = jnp.where(upper, v0, r1)
            return carry

        lax.fori_loop(0, PER // 2, pair, 0, unroll=2)

    def forecast(field):
        by = field if field < FIELDS else field - PAIR

        def four(q, carry):
            for i in (2 * q, 2 * q + 1):
                top = from_north[field, i] * has_north
                bottom = from_south[field, i] * has_south
                for k, (above, below) in enumerate(((top, half_turn(bottom)), (half_turn(top), bottom))):
                    particle = 2 * i + k
                    r = state[field, particle]
                    x = jnp.concatenate([jnp.where(upper, above, r), jnp.where(upper, r, below)], axis=0)
                    for _ in range(STEPS):
                        x = (coef[by, 0] * x + coef[by, 1] * pltpu.roll(x, 1, axis=0)
                             + coef[by, 2] * pltpu.roll(x, 2 * ROWS - 1, axis=0)
                             + coef[by, 3] * pltpu.roll(x, 1, axis=1)
                             + coef[by, 4] * pltpu.roll(x, COLS - 1, axis=1))
                    v = half_turn(jnp.where(upper, x[ROWS:], x[:ROWS]))
                    result[field, particle] = v
                    if field == 0:
                        miss = v - obs_mean[0]
                        cost = obs_weight[...] * miss * miss + obs_rest[0]
                        cost = cost[:, :LANES] + cost[:, LANES:2 * LANES] + cost[:, 2 * LANES:]
                        partial[pl.ds(particle, 1), :] = jnp.sum(cost, axis=0, keepdims=True)
            return carry

        lax.fori_loop(0, PER // 4, four, 0)

    def pack(chunk, get, outgoing, incoming):
        def one(f, carry):
            for g in range(STRIPS):
                def loader(k):
                    return lambda u: get(k, PAIR * chunk + f, pl.ds(LANES * u, LANES))

                spans = [(SPAN * k, WIDE * g - EDGE, SPAN, loader(k), COLS) for k in range(PER)]
                for j in range(PER * SPAN // LANES):
                    outgoing[chunk, STRIPS * f + g, :, LANES * j:LANES * (j + 1)] = place(j, spans)
            return carry

        lax.fori_loop(0, PAIR, one, 0)
        incoming[chunk, me] = outgoing[chunk, me]

    def swap(outgoing, incoming, chunk, which):
        exchange(lambda other: outgoing.at[chunk, other], lambda mine: incoming.at[chunk, mine],
                 sem_out.at[chunk, which], sem_in.at[chunk, which])

    def pack_late():
        def one(f, carry):
            for g in range(STRIPS):
                def loader(k):
                    return lambda u: result[FIELDS + f, k, :, pl.ds(LANES * u, LANES)]

                spans = [(WIDE * k, WIDE * g, WIDE, loader(k), COLS) for k in range(PER)]
                for j in range(PER * WIDE // LANES):
                    late_send[STRIPS * f + g, :, LANES * j:LANES * (j + 1)] = place(j, spans)
            return carry

        lax.fori_loop(0, PAIR, one, 0)
        late_recv[me] = late_send[me]

    def swap_late():
        exchange(lambda other: late_send.at[other], lambda mine: late_recv.at[mine], sem_out.at[1, 0], sem_in.at[1, 0])

    def add_late():
        await_bytes(late_recv.at[pl.ds(0, GROUPS - 1)], sem_in.at[1, 0])

        def one(s, carry):
            def load_from(u):
                return late_recv[s, :, LANES * u:LANES * (u + 1)]

            for m in range(PER // 2):
                late_rows[pl.ds(PER // 2 * s + m, ROWS, stride=PAIRS), :] = place(
                    0, [(HALF * h + EDGE, WIDE * (2 * m + h), WIDE, load_from, PER * WIDE) for h in range(2)])
            return carry

        lax.fori_loop(0, GROUPS, one, 0, unroll=4)

    def sum_late():
        for r in range(ROWS):
            x = lone[1, ALL * r:ALL * r + PAIRS, :] + late_rows[PAIRS * r:PAIRS * (r + 1), :]
            lone[1, ALL * r:ALL * r + PAIRS, :] = x
            lone[1, ALL * r + PAIRS:ALL * (r + 1), :] = pltpu.roll(x, HALF, axis=1)

    def unpack_noise(chunk):
        await_bytes(others(noise_recv, chunk), sem_in.at[chunk, 0])

        def one(s, carry):
            def load_from(u):
                return noise_recv[chunk, s, :, LANES * u:LANES * (u + 1)]

            for m in range(PER // 2):
                noise_pairs[chunk, PER // 2 * s + m] = place(
                    0, [(HALF * h, SPAN * (2 * m + h), SPAN, load_from, PER * SPAN) for h in range(2)])
            return carry

        lax.fori_loop(0, GROUPS, one, 0, unroll=4)

    def unpack_state(chunk):

        def one(s, carry):
            def load_from(u):
                return state_recv[chunk, s, :, LANES * u:LANES * (u + 1)]

            for k in range(PER):
                twins[chunk, PER * s + k] = place(
                    0, [(HALF * h, SPAN * k, SPAN, load_from, PER * SPAN) for h in range(2)])
            return carry

        lax.fori_loop(0, GROUPS, one, 0, unroll=2)

    def begin2(chunk, block):
        left = lane8 < HALF

        def one(i, carry):
            m = BLOCK * block + i
            old0, old1 = ancestors_s[0, 0, 2 * m], ancestors_s[0, 0, 2 * m + 1]
            v = jnp.where(left, twins[chunk, old0], twins[chunk, old1])
            if chunk == 0:
                v = v + noise_pairs[chunk, m]
            grid2[chunk, block, pl.ds(EDGE * BLOCK + i, ROWS, stride=BLOCK), :] = v
            return carry

        lax.fori_loop(0, BLOCK, one, 0, unroll=8)
        halo_copy2(chunk, block, True).start()
        halo_copy2(chunk, block, False).start()

    def forecast2(chunk, block):
        halo_copy2(chunk, block, True).wait_recv()
        halo_copy2(chunk, block, False).wait_recv()
        high = ROWS + 2 * EDGE

        def tall(n, r):
            return jnp.concatenate([coef2[chunk, n, r]] * (BLOCK // ROWS), axis=0)

        x = [grid2[chunk, block, BLOCK * r:BLOCK * (r + 1), :] for r in range(high)]
        x = [v * has_north if r < EDGE else v * has_south if r >= EDGE + ROWS else v for r, v in enumerate(x)]
        for s in range(1, STEPS + 1):
            new = list(x)
            for r in range(s, high - s):
                new[r] = (tall(0, r) * x[r] + tall(1, r) * x[r - 1] + tall(2, r) * x[r + 1]
                          + tall(3, r) * pltpu.roll(x[r], 1, axis=1) + tall(4, r) * pltpu.roll(x[r], LANES - 1, axis=1))
            x = new
        for r in range(ROWS):
            lone[chunk, ALL * r + BLOCK * block:ALL * r + BLOCK * (block + 1), :] = x[EDGE + r]
            if chunk == 0:
                low = ALL * r + PAIRS + BLOCK * block
                lone[chunk, low:low + BLOCK, :] = pltpu.roll(x[EDGE + r], HALF, axis=1)

    def pack_back(chunk):
        def one(group, carry):
            def loader(j):
                old = ancestors_s[1, 0, PER * group + j]
                tall = lone[chunk, pl.ds((old & 1) * PAIRS + (old >> 1), ROWS, stride=ALL), :]
                return lambda u: tall

            spans = [(WIDE * j, EDGE, WIDE, loader(j), LANES) for j in range(PER)]
            for n in range(PER * WIDE // LANES):
                back_send[chunk, group, :, LANES * n:LANES * (n + 1)] = place(n, spans)
            return carry

        lax.fori_loop(0, GROUPS, one, 0, unroll=4)
        back_recv[chunk, me] = back_send[chunk, me]

    def stores(chunk):
        two = pl.ds(PAIR * chunk, PAIR)
        return (pltpu.make_async_copy(out_v.at[:, two], out.at[:, two], sem_store.at[chunk, 0]),
                pltpu.make_async_copy(averages_v.at[:, two], averages.at[:, two], sem_store.at[chunk, 1]))

    def finish(chunk):
        await_bytes(others(back_recv, chunk), sem_in.at[chunk, 2])

        def one(f, carry):
            def loader(g):
                return lambda u: back_recv[chunk, STRIPS * f + g, :, LANES * u:LANES * (u + 1)]

            for j in range(PER):
                spans = [(WIDE * g, WIDE * j, WIDE, loader(g), PER * WIDE) for g in range(STRIPS)]
                for u in range(COLS // LANES):
                    out_v[j, PAIR * chunk + f, :, LANES * u:LANES * (u + 1)] = place(u, spans)
            return carry

        lax.fori_loop(0, PAIR, one, 0)

    lane = lax.broadcasted_iota(jnp.int32, (PER, LANES), 1)
    line = lax.broadcasted_iota(jnp.int32, (PER, LANES), 0)

    def likelihood():
        total = -0.5 * jnp.sum(partial[...], axis=1, keepdims=True)
        row = jnp.sum(jnp.where(lane == line, total, 0.0), axis=0, keepdims=True)
        like_send[...] = row
        like_recv[me] = row
        exchange(lambda other: like_send, lambda mine: like_recv.at[mine], sem_small_out.at[0], sem_small_in.at[0])

    def weigh():
        await_bytes(like_recv.at[pl.ds(0, GROUPS - 1)], sem_small_in.at[0])
        everyone = like_recv[...]
        known = lax.broadcasted_iota(jnp.int32, (GROUPS, 1, LANES), 2) < PER
        peak = jnp.max(jnp.where(known, everyone, -3.0e38), axis=0)
        peak = jnp.max(peak, axis=1, keepdims=True)
        shifted = jnp.where(known, jnp.exp(jnp.where(known, everyone - peak[None], 0.0)), 0.0)
        total = jnp.sum(jnp.sum(shifted, axis=0), axis=1, keepdims=True)
        weight = shifted / total[None]
        for g in range(GROUPS):
            own = jnp.sum(jnp.where(lane == line, weight[g], 0.0), axis=1, keepdims=True)
            weights[PER * g:PER * (g + 1), :] = jnp.broadcast_to(own, (PER, LANES))

    def average(chunk):
        def add(q, sums):
            return tuple(s + weights[pl.ds(4 * q + k, 1), :] * twins[chunk, 4 * q + k] for k, s in enumerate(sums))

        sums = lax.fori_loop(0, ALL // 4, add, (jnp.zeros((ROWS, LANES), jnp.float32),) * 4, unroll=4)
        mean_own[chunk] = (sums[0] + sums[1]) + (sums[2] + sums[3])

    place2 = lax.broadcasted_iota(jnp.int32, (PAIRS, LANES), 1)
    line2 = lax.broadcasted_iota(jnp.int32, (PAIRS, LANES), 0)

    def likelihood2():
        cost = jnp.zeros((PAIRS, LANES), jnp.float32)
        for r in range(ROWS):
            miss = lone[0, ALL * r:ALL * r + PAIRS, :] - obs2[1, r:r + 1]
            cost = cost + obs2[0, r:r + 1] * miss * miss + obs2[2, r:r + 1]
        for h in range(2):
            side = (place2 < HALF) if h == 0 else (place2 >= HALF)
            total = -0.5 * jnp.sum(jnp.where(side, cost, 0.0), axis=1, keepdims=True)
            row = jnp.sum(jnp.where(place2 == line2, total, 0.0), axis=0, keepdims=True)
            like_send2[h:h + 1, :] = row
        like_recv2[me] = like_send2[...]
        exchange(lambda other: like_send2, lambda mine: like_recv2.at[mine], sem_small_out.at[1], sem_small_in.at[1])

    def weigh2():
        await_bytes(like_recv2.at[pl.ds(0, GROUPS - 1)], sem_small_in.at[1])
        total = like_recv2[0]
        for g in range(1, GROUPS):
            total = total + like_recv2[g]
        peak = jnp.max(jnp.max(total, axis=0, keepdims=True), axis=1, keepdims=True)
        shifted = jnp.exp(total - peak)
        weight = shifted / jnp.sum(jnp.sum(shifted, axis=0, keepdims=True), axis=1, keepdims=True)
        sides = [jnp.sum(jnp.where(place2 == line2, weight[h:h + 1], 0.0), axis=1, keepdims=True) for h in range(2)]
        weights2[...] = jnp.where(place2 < HALF, sides[0], sides[1])

    def average2(chunk):
        for r in range(ROWS):
            part = weights2[...] * lone[chunk, ALL * r:ALL * r + PAIRS, :]
            mean_send2[chunk, r:r + 1, :] = jnp.sum(part, axis=0, keepdims=True)
        total = mean_send2[chunk]
        total = total + pltpu.roll(total, HALF, axis=1)
        total = jnp.where(lane8 < HALF, mean_own[chunk], total)
        mean_send2[chunk] = total
        mean_recv2[chunk, core, chip] = total

        def one(step, carry):
            pltpu.make_async_remote_copy(
                src_ref=mean_send2.at[chunk], dst_ref=mean_recv2.at[chunk, core, chip],
                send_sem=sem_small_out.at[2 + chunk], recv_sem=sem_small_in.at[2 + chunk],
                device_id={"dom": 2 * lax.rem(chip + step, CHIPS) + core}, device_id_type=MESH,
            ).start()
            return carry

        lax.fori_loop(1, CHIPS, one, 0)

    def means_across(chunk):
        return pltpu.make_async_remote_copy(
            src_ref=mean_recv2.at[chunk, core], dst_ref=mean_recv2.at[chunk, core],
            send_sem=sem_small_out.at[4 + chunk], recv_sem=sem_small_in.at[4 + chunk],
            device_id={"dom": 2 * chip + 1 - core}, device_id_type=MESH,
        )

    def pass_means(chunk):
        await_bytes(mean_recv2.at[chunk, 0, pl.ds(0, CHIPS - 1)], sem_small_in.at[2 + chunk])
        means_across(chunk).start()

    def write_means(chunk):
        means_across(chunk).wait_recv()
        for c in range(CYCLES):
            for f in range(PAIR):
                def loader(g):
                    return lambda u: mean_recv2[chunk, g % 2, (STRIPS * f + g) // 2]

                spans = [(WIDE * g, HALF * c + EDGE, WIDE, loader(g), LANES) for g in range(STRIPS)]
                for u in range(COLS // LANES):
                    averages_v[c, PAIR * chunk + f, :, LANES * u:LANES * (u + 1)] = place(u, spans)

    def edge_coefficients():
        for m in range(2):
            raw[m] = half_turn(courant_v[m])
        for f in range(FIELDS):
            raw[2 + f] = half_turn(diffusion_v[f])

    def coefficients(field):
        def sixteen(m):
            mid = raw[m]
            return jnp.concatenate([jnp.where(upper, raw_north[m], mid), jnp.where(upper, mid, raw_south[m])], axis=0)

        inside = jnp.concatenate([jnp.where(upper, has_north, 1.0), jnp.where(upper, 1.0, has_south)], axis=0)
        column2 = jnp.concatenate([column, column], axis=0)
        cx, cy, d = sixteen(0), sixteen(1), sixteen(2 + field)
        coef[field, 0] = inside * (1.0 - jnp.abs(cx) - jnp.abs(cy) - 4.0 * d)
        coef[field, 1] = inside * (jnp.maximum(cx, 0.0) + d)
        coef[field, 2] = inside * (d - jnp.minimum(cx, 0.0))
        coef[field, 3] = jnp.where(column2 > 0, inside * (jnp.maximum(cy, 0.0) + d), 0.0)
        coef[field, 4] = jnp.where(column2 < COLS - 1, inside * (d - jnp.minimum(cy, 0.0)), 0.0)

    def window(get, rows):
        for g in range(STRIPS):
            spans = [(HALF * h, WIDE * g - EDGE, SPAN, lambda u: get(pl.ds(LANES * u, LANES)), COLS) for h in range(2)]
            windows[g, :rows] = place(0, spans, rows)
        return windows[strip, :rows]

    def coefficients2(chunk):
        lane16 = lax.broadcasted_iota(jnp.int32, (2 * ROWS, LANES), 1)
        used = lax.rem(lane16, HALF) < SPAN
        for n in range(5):
            here = window(lambda cols: coef[PAIR * chunk + in_pair, n, :, cols], 2 * ROWS)
            here = jnp.where(used, here, 0.0)
            for r in range(2 * ROWS):
                coef2[chunk, n, r] = jnp.broadcast_to(here[r:r + 1], (ROWS, LANES))

    def observations():
        cell = lax.broadcasted_iota(jnp.int32, (ROWS, COLS), 0) * COLS + column
        zero = jnp.zeros((ROWS, COLS), jnp.float32)

        def gather(k, sums):
            here = cell == obs_loc_s[0, k]
            precision = jnp.where(here, 1.0 / jnp.full((1, COLS), obs_var_s[0, k], jnp.float32), 0.0)
            return (sums[0] + precision,) + tuple(sums[1 + c] + precision * observed_s[c, 0, k] for c in range(CYCLES))

        sums = lax.fori_loop(0, NOBS, gather, (zero,) * (1 + CYCLES), unroll=8)
        obs_weight[...] = sums[0]
        seen = sums[0] > 0.0
        means = []
        for c in range(CYCLES):
            means.append(jnp.where(seen, sums[1 + c] / jnp.where(seen, sums[0], 1.0), 0.0))
            obs_mean[c] = means[c]

        def rest(k, sums):
            here = cell == obs_loc_s[0, k]
            precision = jnp.where(here, 1.0 / jnp.full((1, COLS), obs_var_s[0, k], jnp.float32), 0.0)
            return tuple(sums[c] + precision * (observed_s[c, 0, k] - means[c]) * (observed_s[c, 0, k] - means[c])
                         for c in range(CYCLES))

        sums = lax.fori_loop(0, NOBS, rest, (zero,) * CYCLES, unroll=8)
        for c in range(CYCLES):
            obs_rest[c] = sums[c]

    def observations2():
        inner = lax.rem(lane8, HALF)
        own = (inner >= EDGE) & (inner < EDGE + WIDE)
        first = jnp.where(in_pair == 0, 1.0, 0.0).astype(jnp.float32)
        obs2[0] = jnp.where(own, window(lambda cols: obs_weight[:, cols], ROWS), 0.0) * first
        obs2[1] = window(lambda cols: obs_mean[1, :, cols], ROWS)
        obs2[2] = jnp.where(own, window(lambda cols: obs_rest[1, :, cols], ROWS), 0.0) * first

    def noise_of(k, field, cols):
        return noise_v[1, k, field, :, cols]

    def state_of(k, field, cols):
        return result[field, k, :, cols]

    loads[0].wait()
    pack(0, noise_of, noise_send, noise_recv)
    for n in (1, 2, 6, 7):
        loads[n].wait()
    edge_coefficients()
    begin(0)
    pl.semaphore_wait(barrier, GROUPS + 1)

    def edges(ready):
        for way in (True, False):
            halo_copy(ready, way).wait_recv()

    def send_edges(field):
        for way in (True, False):
            halo_copy(field, way).start()

    for way in (True, False):
        raw_copy(0, way).start()
    send_edges(0)
    swap(noise_send, noise_recv, 0, 0)
    begin(1)
    send_edges(1)
    for way in (True, False):
        raw_copy(1, way).start()
    for n in (3, 4, 5, 8, 9, 10, 11):
        loads[n].wait()
    for f in range(2, FIELDS):
        begin(f)
    observations()
    for way in (True, False):
        raw_copy(0, way).wait_recv()
    coefficients(0)
    edges(0)
    send_edges(2)
    forecast(0)
    likelihood()
    for way in (True, False):
        raw_copy(1, way).wait_recv()
    coefficients(1)
    edges(1)
    send_edges(3)
    forecast(1)
    pack(0, state_of, state_send, state_recv)
    swap(state_send, state_recv, 0, 1)
    for f in range(2, FIELDS):
        coefficients(f)
        edges(f)
        begin(f + PAIR)
        send_edges(f + PAIR)
        forecast(f)
    pack(1, state_of, state_send, state_recv)
    swap(state_send, state_recv, 1, 1)
    for chunk in range(CHUNKS):
        coefficients2(chunk)
    observations2()
    unpack_noise(0)
    for f in range(FIELDS, SLOTS):
        edges(f)
        forecast(f)
    pack_late()
    swap_late()
    weigh()
    await_bytes(others(state_recv, 0), sem_in.at[0, 1])
    unpack_state(0)
    for block in range(BLOCKS):
        begin2(0, block)
    average(0)
    for block in range(BLOCKS):
        forecast2(0, block)
    likelihood2()
    pack_back(0)
    swap(back_send, back_recv, 0, 2)
    await_bytes(others(state_recv, 1), sem_in.at[1, 1])
    unpack_state(1)
    for block in range(BLOCKS):
        begin2(1, block)
    weigh2()
    average2(0)
    average(1)
    for block in range(BLOCKS):
        forecast2(1, block)
    add_late()
    sum_late()
    average2(1)
    pack_back(1)
    swap(back_send, back_recv, 1, 2)
    pass_means(0)
    finish(0)
    write_means(0)
    for copy in stores(0):
        copy.start()
    pass_means(1)
    finish(1)
    stores(1)[0].start()
    write_means(1)
    stores(1)[1].start()
    await_bytes(others(noise_recv, 0), sem_out.at[0, 0])
    await_bytes(late_recv.at[pl.ds(0, GROUPS - 1)], sem_out.at[1, 0])
    for chunk in range(CHUNKS):
        await_bytes(others(state_recv, chunk), sem_out.at[chunk, 1])
    for chunk in range(CHUNKS):
        await_bytes(others(back_recv, chunk), sem_out.at[chunk, 2])
        await_bytes(mean_recv2.at[chunk, 0, pl.ds(0, CHIPS - 1)], sem_small_out.at[2 + chunk])
        means_across(chunk).wait_send()
        for copy in stores(chunk):
            copy.wait()
    for way in (True, False):
        for f in range(SLOTS):
            halo_copy(f, way).wait_send()
        for part in range(2):
            raw_copy(part, way).wait_send()
        for chunk in range(CHUNKS):
            for block in range(BLOCKS):
                halo_copy2(chunk, block, way).wait_send()
    for n, ref in enumerate((like_recv, like_recv2)):
        await_bytes(ref.at[pl.ds(0, GROUPS - 1)], sem_small_out.at[n])


def hand_over(ensemble, averages, ensemble_out, averages_out, ensemble_v, averages_v, sem_in, sem_out):
    size = PER // PARTS
    ways = [(ensemble.at[pl.ds(size * n, size)], ensemble_v.at[pl.ds(size * n, size)],
             ensemble_out.at[pl.ds(size * n, size)]) for n in range(PARTS)]
    ways.append((averages, averages_v, averages_out))
    into = [pltpu.make_async_copy(source, middle, sem_in.at[n]) for n, (source, middle, _) in enumerate(ways)]
    away = [pltpu.make_async_copy(middle, target, sem_out.at[n]) for n, (_, middle, target) in enumerate(ways)]
    for copy in into:
        copy.start()
    for first, second in zip(into, away):
        first.wait()
        second.start()
    for copy in away:
        copy.wait()


def per_device(members, noise, courant, diffusion, obs_loc, observed, obs_var, ancestors):
    f32 = jnp.float32
    anywhere = pl.BlockSpec(memory_space=pl.ANY)
    plane = (ROWS, COLS)
    one = (ROWS, LANES)
    operands = (members, noise, courant, diffusion, obs_loc, observed, obs_var, ancestors)

    def vmem(*shape):
        return pltpu.VMEM(shape, f32)

    scratch = [vmem(PER, FIELDS, *plane), vmem(CYCLES, FIELDS, *plane)]
    scratch += [vmem(*a.shape) for a in operands[:4]] + [pltpu.SMEM(a.shape, a.dtype) for a in operands[4:]]
    scratch += [vmem(1, GROUPS, ROWS, PER * SPAN) for _ in range(2)]
    scratch += [vmem(GROUPS, ROWS, PER * WIDE) for _ in range(2)] + [vmem(ROWS * PAIRS, LANES)]
    scratch += [vmem(CHUNKS, GROUPS, ROWS, PER * SPAN) for _ in range(2)]
    scratch += [vmem(CHUNKS, GROUPS, ROWS, PER * WIDE) for _ in range(2)]
    scratch += [vmem(SLOTS, PER // 2, *plane) for _ in range(4)]
    scratch += [
        vmem(SLOTS, PER, *plane),
        vmem(SLOTS, PER, *plane),
        vmem(2 + FIELDS, *plane),
        vmem(2 + FIELDS, *plane),
        vmem(2 + FIELDS, *plane),
        vmem(FIELDS, 5, 2 * ROWS, COLS),
        vmem(*plane),
        vmem(CYCLES, *plane),
        vmem(CYCLES, *plane),
        vmem(PER, LANES),
        vmem(ALL, LANES),
        vmem(1, LANES),
        vmem(GROUPS, 1, LANES),
        vmem(CHUNKS, *one),
        vmem(1, PAIRS, *one),
        vmem(CHUNKS, ALL, *one),
        vmem(CHUNKS, BLOCKS, (ROWS + 2 * EDGE) * BLOCK, LANES),
        vmem(CHUNKS, ROWS * ALL, LANES),
        vmem(CHUNKS, 5, 2 * ROWS, *one),
        vmem(STRIPS, 2 * ROWS, LANES),
        vmem(3, *one),
        vmem(PAIRS, LANES),
        vmem(2, LANES),
        vmem(GROUPS, 2, LANES),
        vmem(CHUNKS, *one),
        vmem(CHUNKS, 2, CHIPS, *one),
        pltpu.SemaphoreType.DMA((12,)),
        pltpu.SemaphoreType.DMA((CHUNKS, 2)),
        pltpu.SemaphoreType.DMA((CHUNKS, 3)),
        pltpu.SemaphoreType.DMA((CHUNKS, 3)),
        pltpu.SemaphoreType.DMA((SLOTS, 2)),
        pltpu.SemaphoreType.DMA((SLOTS, 2)),
        pltpu.SemaphoreType.DMA((CHUNKS, BLOCKS, 2)),
        pltpu.SemaphoreType.DMA((CHUNKS, BLOCKS, 2)),
        pltpu.SemaphoreType.DMA((2, 2)),
        pltpu.SemaphoreType.DMA((2, 2)),
        pltpu.SemaphoreType.DMA((6,)),
        pltpu.SemaphoreType.DMA((6,)),
    ]
    results = pl.pallas_call(
        kernel,
        out_shape=(
            jax.ShapeDtypeStruct((PER, FIELDS) + plane, f32),
            jax.ShapeDtypeStruct((CYCLES, FIELDS) + plane, f32),
        ),
        in_specs=[anywhere] * 8,
        out_specs=(anywhere, anywhere),
        scratch_shapes=scratch,
        compiler_params=pltpu.CompilerParams(
            collective_id=0, has_side_effects=True, vmem_limit_bytes=60 * 1024 * 1024
        ),
        name="assimilate",
    )(*operands)
    return pl.pallas_call(
        hand_over,
        out_shape=tuple(jax.ShapeDtypeStruct(r.shape, f32) for r in results),
        in_specs=[anywhere] * 2,
        out_specs=(anywhere, anywhere),
        scratch_shapes=[vmem(*r.shape) for r in results] + [pltpu.SemaphoreType.DMA((PARTS + 1,))] * 2,
        compiler_params=pltpu.CompilerParams(vmem_limit_bytes=60 * 1024 * 1024),
        name="hand_over",
    )(*results)


def solution(mesh):
    return jax.shard_map(
        per_device,
        mesh=mesh,
        in_specs=(
            P("dom", None, "tile", None),
            P(None, "dom", None, "tile", None),
            P(None, "tile", None),
            P(None, "tile", None),
            P("tile", None),
            P(None, "tile", None),
            P("tile", None),
            P(None, "tile", None),
        ),
        out_specs=(P("dom", None, "tile", None), P(None, None, "tile", None)),
        check_vma=False,
    )
```

```python
import jax
import jax.numpy as jnp
from jax import lax
from jax.experimental import pallas as pl
from jax.experimental.pallas import tpu as pltpu
from jax.sharding import PartitionSpec as P

MESH = pl.DeviceIdType.MESH
STEPS = 4
CYCLES = 2
FIELDS = 4
PER = 16
GROUPS = 16
CHIPS = 8
ALL = PER * GROUPS
PAIRS = ALL // 2
TILES = 16
ROWS = 8
COLS = 384
LANES = 128
HALF = LANES // 2
NOBS = 64
CHUNKS = 2
PAIR = 2
PARTS = 4
SLOTS = FIELDS + PAIR
STRIPS = 8
WIDE = COLS // STRIPS
EDGE = STEPS
SPAN = WIDE + 2 * EDGE
BLOCKS = 4
BLOCK = PAIRS // BLOCKS


def half_turn(x):
    return pltpu.roll(x, 4, axis=0)


def place(vector, spans, rows=ROWS):
    lane = lax.broadcasted_iota(jnp.int32, (rows, LANES), 1)
    result = None
    for begin, column, length, load, limit in spans:
        low, high = max(begin, vector * LANES), min(begin + length, (vector + 1) * LANES)
        if low >= high:
            continue
        column = column + low - begin
        low, high = low - vector * LANES, high - vector * LANES
        first = max(column, 0) // LANES
        last = min(column + high - low, limit) - 1
        for u in range(first, last // LANES + 1):
            piece = load(u)
            shift = (low - column + LANES * u) % LANES
            if shift:
                piece = pltpu.roll(piece, shift, axis=1)
            start = max(low, low - column + LANES * u)
            result = piece if result is None else jnp.where(lane >= start, piece, result)
    return result


def kernel(members, noise, courant, diffusion, obs_loc, observed, obs_var, ancestors, out, averages,
           out_v, averages_v,
           members_v, noise_v, courant_v, diffusion_v, obs_loc_s, observed_s, obs_var_s, ancestors_s,
           noise_send, noise_recv, late_send, late_recv, late_rows, state_send, state_recv, back_send, back_recv,
           to_north, to_south, from_north, from_south,
           state, result, raw, raw_north, raw_south, coef, obs_weight, obs_mean, obs_rest, partial, weights,
           like_send, like_recv, mean_own,
           noise_pairs, twins, grid2, lone, coef2, windows, obs2, weights2, like_send2, like_recv2,
           mean_send2, mean_recv2,
           sem_load, sem_store, sem_out, sem_in, sem_halo_out, sem_halo_in, sem_halo2_out, sem_halo2_in, sem_raw_out,
           sem_raw_in, sem_small_out, sem_small_in):
    me = lax.axis_index("dom")
    tile = lax.axis_index("tile")
    north = lax.rem(tile + TILES - 1, TILES)
    south = lax.rem(tile + 1, TILES)
    strip = lax.rem(me, STRIPS)
    in_pair = lax.div(me, STRIPS)
    chip = lax.div(me, 2)
    core = lax.rem(me, 2)

    def peer(step):
        return lax.rem(me + step, GROUPS)

    barrier = pltpu.get_barrier_semaphore()

    def greet(step, carry):
        pl.semaphore_signal(barrier, inc=1, device_id={"dom": peer(step)}, device_id_type=MESH)
        return carry

    for neighbour in (north, south):
        pl.semaphore_signal(barrier, inc=1, device_id={"tile": neighbour}, device_id_type=MESH)
    lax.fori_loop(1, GROUPS, greet, 0)

    loads = []

    def load(source, target):
        loads.append(pltpu.make_async_copy(source, target, sem_load.at[len(loads)]))
        loads[-1].start()

    for chunk in range(CHUNKS):
        two = pl.ds(PAIR * chunk, PAIR)
        load(noise.at[1, :, two], noise_v.at[1, :, two])
        load(members.at[:, two], members_v.at[:, two])
        load(noise.at[0, :, two], noise_v.at[0, :, two])
    for source, target in ((courant, courant_v), (diffusion, diffusion_v), (obs_loc, obs_loc_s),
                           (observed, observed_s), (obs_var, obs_var_s), (ancestors, ancestors_s)):
        load(source, target)

    upper = lax.broadcasted_iota(jnp.int32, (ROWS, COLS), 0) < 4
    upper1 = lax.broadcasted_iota(jnp.int32, (ROWS, LANES), 0) < 4
    column = lax.broadcasted_iota(jnp.int32, (ROWS, COLS), 1)
    lane8 = lax.broadcasted_iota(jnp.int32, (ROWS, LANES), 1)
    has_north = jnp.where(tile > 0, 1.0, 0.0).astype(jnp.float32)
    has_south = jnp.where(tile < TILES - 1, 1.0, 0.0).astype(jnp.float32)

    def exchange(source_of, target_of, out_sem, in_sem):
        def one(step, carry):
            near = lax.div(step + 1, 2)
            other = peer(jnp.where(lax.rem(step, 2) == 1, near, GROUPS - near))
            pltpu.make_async_remote_copy(
                src_ref=source_of(other), dst_ref=target_of(me), send_sem=out_sem, recv_sem=in_sem,
                device_id={"dom": other}, device_id_type=MESH,
            ).start()
            return carry

        lax.fori_loop(1, GROUPS, one, 0)

    def await_bytes(ref, sem):
        pltpu.make_async_copy(ref, ref, sem).wait()

    def others(ref, chunk):
        return ref.at[chunk, pl.ds(0, GROUPS - 1)]

    def tile_copy(source, target, out_sem, in_sem, southward):
        return pltpu.make_async_remote_copy(
            src_ref=source, dst_ref=target, send_sem=out_sem, recv_sem=in_sem,
            device_id={"tile": south if southward else north}, device_id_type=MESH,
        )

    def halo_copy(field, southward):
        source, target = (to_south, from_north) if southward else (to_north, from_south)
        way = 1 if southward else 0
        return tile_copy(source.at[field], target.at[field], sem_halo_out.at[field, way], sem_halo_in.at[field, way],
                         southward)

    def halo_copy2(chunk, block, southward):
        source, target = (ROWS, 0) if southward else (EDGE, ROWS + EDGE)
        way = 1 if southward else 0
        rows = EDGE * BLOCK
        return tile_copy(grid2.at[chunk, block, pl.ds(source * BLOCK, rows)],
                         grid2.at[chunk, block, pl.ds(target * BLOCK, rows)], sem_halo2_out.at[chunk, block, way],
                         sem_halo2_in.at[chunk, block, way], southward)

    def raw_copy(part, southward):
        rows = pl.ds(3 * part, 3)
        target = raw_north if southward else raw_south
        way = 1 if southward else 0
        return tile_copy(raw.at[rows], target.at[rows], sem_raw_out.at[part, way], sem_raw_in.at[part, way], southward)

    def begin(field):
        def start_of(particle):
            if field < FIELDS:
                return members_v[particle, field] + noise_v[0, particle, field]
            return noise_v[1, particle, field - PAIR]

        def pair(i, carry):
            first, second = 2 * i, 2 * i + 1
            v0, v1 = start_of(first), start_of(second)
            r0, r1 = half_turn(v0), half_turn(v1)
            state[field, first] = r0
            state[field, second] = r1
            to_south[field, i] = jnp.where(upper, r0, v1)
            to_north[field, i] = jnp.where(upper, v0, r1)
            return carry

        lax.fori_loop(0, PER // 2, pair, 0, unroll=2)

    def forecast(field):
        by = field if field < FIELDS else field - PAIR

        def four(q, carry):
            for i in (2 * q, 2 * q + 1):
                top = from_north[field, i] * has_north
                bottom = from_south[field, i] * has_south
                for k, (above, below) in enumerate(((top, half_turn(bottom)), (half_turn(top), bottom))):
                    particle = 2 * i + k
                    r = state[field, particle]
                    x = jnp.concatenate([jnp.where(upper, above, r), jnp.where(upper, r, below)], axis=0)
                    for _ in range(STEPS):
                        x = (coef[by, 0] * x + coef[by, 1] * pltpu.roll(x, 1, axis=0)
                             + coef[by, 2] * pltpu.roll(x, 2 * ROWS - 1, axis=0)
                             + coef[by, 3] * pltpu.roll(x, 1, axis=1)
                             + coef[by, 4] * pltpu.roll(x, COLS - 1, axis=1))
                    v = half_turn(jnp.where(upper, x[ROWS:], x[:ROWS]))
                    result[field, particle] = v
                    if field == 0:
                        miss = v - obs_mean[0]
                        cost = obs_weight[...] * miss * miss + obs_rest[0]
                        cost = cost[:, :LANES] + cost[:, LANES:2 * LANES] + cost[:, 2 * LANES:]
                        partial[pl.ds(particle, 1), :] = jnp.sum(cost, axis=0, keepdims=True)
            return carry

        lax.fori_loop(0, PER // 4, four, 0)

    def pack(chunk, get, outgoing, incoming):
        def one(f, carry):
            for g in range(STRIPS):
                def loader(k):
                    return lambda u: get(k, PAIR * chunk + f, pl.ds(LANES * u, LANES))

                spans = [(SPAN * k, WIDE * g - EDGE, SPAN, loader(k), COLS) for k in range(PER)]
                for j in range(PER * SPAN // LANES):
                    outgoing[chunk, STRIPS * f + g, :, LANES * j:LANES * (j + 1)] = place(j, spans)
            return carry

        lax.fori_loop(0, PAIR, one, 0)
        incoming[chunk, me] = outgoing[chunk, me]

    def swap(outgoing, incoming, chunk, which):
        exchange(lambda other: outgoing.at[chunk, other], lambda mine: incoming.at[chunk, mine],
                 sem_out.at[chunk, which], sem_in.at[chunk, which])

    def pack_late():
        def one(f, carry):
            for g in range(STRIPS):
                def loader(k):
                    return lambda u: result[FIELDS + f, k, :, pl.ds(LANES * u, LANES)]

                spans = [(WIDE * k, WIDE * g, WIDE, loader(k), COLS) for k in range(PER)]
                for j in range(PER * WIDE // LANES):
                    late_send[STRIPS * f + g, :, LANES * j:LANES * (j + 1)] = place(j, spans)
            return carry

        lax.fori_loop(0, PAIR, one, 0)
        late_recv[me] = late_send[me]

    def swap_late():
        exchange(lambda other: late_send.at[other], lambda mine: late_recv.at[mine], sem_out.at[1, 0], sem_in.at[1, 0])

    def add_late():
        await_bytes(late_recv.at[pl.ds(0, GROUPS - 1)], sem_in.at[1, 0])

        def one(s, carry):
            def load_from(u):
                return late_recv[s, :, LANES * u:LANES * (u + 1)]

            for m in range(PER // 2):
                late_rows[pl.ds(PER // 2 * s + m, ROWS, stride=PAIRS), :] = place(
                    0, [(HALF * h + EDGE, WIDE * (2 * m + h), WIDE, load_from, PER * WIDE) for h in range(2)])
            return carry

        lax.fori_loop(0, GROUPS, one, 0, unroll=4)

    def sum_late():
        for r in range(ROWS):
            x = lone[1, ALL * r:ALL * r + PAIRS, :] + late_rows[PAIRS * r:PAIRS * (r + 1), :]
            lone[1, ALL * r:ALL * r + PAIRS, :] = x
            lone[1, ALL * r + PAIRS:ALL * (r + 1), :] = pltpu.roll(x, HALF, axis=1)

    def unpack_noise(chunk):
        await_bytes(others(noise_recv, chunk), sem_in.at[chunk, 0])

        def one(s, carry):
            def load_from(u):
                return noise_recv[chunk, s, :, LANES * u:LANES * (u + 1)]

            for m in range(PER // 2):
                noise_pairs[chunk, PER // 2 * s + m] = place(
                    0, [(HALF * h, SPAN * (2 * m + h), SPAN, load_from, PER * SPAN) for h in range(2)])
            return carry

        lax.fori_loop(0, GROUPS, one, 0, unroll=4)

    def unpack_state(chunk):

        def one(s, carry):
            def load_from(u):
                return state_recv[chunk, s, :, LANES * u:LANES * (u + 1)]

            for k in range(PER):
                twins[chunk, PER * s + k] = place(
                    0, [(HALF * h, SPAN * k, SPAN, load_from, PER * SPAN) for h in range(2)])
            return carry

        lax.fori_loop(0, GROUPS, one, 0, unroll=2)

    def begin2(chunk, block):
        left = lane8 < HALF

        def one(i, carry):
            m = BLOCK * block + i
            old0, old1 = ancestors_s[0, 0, 2 * m], ancestors_s[0, 0, 2 * m + 1]
            v = jnp.where(left, twins[chunk, old0], twins[chunk, old1])
            if chunk == 0:
                v = v + noise_pairs[chunk, m]
            grid2[chunk, block, pl.ds(EDGE * BLOCK + i, ROWS, stride=BLOCK), :] = v
            return carry

        lax.fori_loop(0, BLOCK, one, 0, unroll=8)
        halo_copy2(chunk, block, True).start()
        halo_copy2(chunk, block, False).start()

    def forecast2(chunk, block):
        halo_copy2(chunk, block, True).wait_recv()
        halo_copy2(chunk, block, False).wait_recv()
        high = ROWS + 2 * EDGE

        def tall(n, r):
            return jnp.concatenate([coef2[chunk, n, r]] * (BLOCK // ROWS), axis=0)

        x = [grid2[chunk, block, BLOCK * r:BLOCK * (r + 1), :] for r in range(high)]
        x = [v * has_north if r < EDGE else v * has_south if r >= EDGE + ROWS else v for r, v in enumerate(x)]
        for s in range(1, STEPS + 1):
            new = list(x)
            for r in range(s, high - s):
                new[r] = (tall(0, r) * x[r] + tall(1, r) * x[r - 1] + tall(2, r) * x[r + 1]
                          + tall(3, r) * pltpu.roll(x[r], 1, axis=1) + tall(4, r) * pltpu.roll(x[r], LANES - 1, axis=1))
            x = new
        for r in range(ROWS):
            lone[chunk, ALL * r + BLOCK * block:ALL * r + BLOCK * (block + 1), :] = x[EDGE + r]
            if chunk == 0:
                low = ALL * r + PAIRS + BLOCK * block
                lone[chunk, low:low + BLOCK, :] = pltpu.roll(x[EDGE + r], HALF, axis=1)

    def pack_back(chunk):
        def one(group, carry):
            def loader(j):
                old = ancestors_s[1, 0, PER * group + j]
                tall = lone[chunk, pl.ds((old & 1) * PAIRS + (old >> 1), ROWS, stride=ALL), :]
                return lambda u: tall

            spans = [(WIDE * j, EDGE, WIDE, loader(j), LANES) for j in range(PER)]
            for n in range(PER * WIDE // LANES):
                back_send[chunk, group, :, LANES * n:LANES * (n + 1)] = place(n, spans)
            return carry

        lax.fori_loop(0, GROUPS, one, 0, unroll=4)
        back_recv[chunk, me] = back_send[chunk, me]

    def stores(chunk):
        two = pl.ds(PAIR * chunk, PAIR)
        return (pltpu.make_async_copy(out_v.at[:, two], out.at[:, two], sem_store.at[chunk, 0]),
                pltpu.make_async_copy(averages_v.at[:, two], averages.at[:, two], sem_store.at[chunk, 1]))

    def finish(chunk):
        await_bytes(others(back_recv, chunk), sem_in.at[chunk, 2])

        def one(f, carry):
            def loader(g):
                return lambda u: back_recv[chunk, STRIPS * f + g, :, LANES * u:LANES * (u + 1)]

            for j in range(PER):
                spans = [(WIDE * g, WIDE * j, WIDE, loader(g), PER * WIDE) for g in range(STRIPS)]
                for u in range(COLS // LANES):
                    out_v[j, PAIR * chunk + f, :, LANES * u:LANES * (u + 1)] = place(u, spans)
            return carry

        lax.fori_loop(0, PAIR, one, 0)

    lane = lax.broadcasted_iota(jnp.int32, (PER, LANES), 1)
    line = lax.broadcasted_iota(jnp.int32, (PER, LANES), 0)

    def likelihood():
        total = -0.5 * jnp.sum(partial[...], axis=1, keepdims=True)
        row = jnp.sum(jnp.where(lane == line, total, 0.0), axis=0, keepdims=True)
        like_send[...] = row
        like_recv[me] = row
        exchange(lambda other: like_send, lambda mine: like_recv.at[mine], sem_small_out.at[0], sem_small_in.at[0])

    def weigh():
        await_bytes(like_recv.at[pl.ds(0, GROUPS - 1)], sem_small_in.at[0])
        everyone = like_recv[...]
        known = lax.broadcasted_iota(jnp.int32, (GROUPS, 1, LANES), 2) < PER
        peak = jnp.max(jnp.where(known, everyone, -3.0e38), axis=0)
        peak = jnp.max(peak, axis=1, keepdims=True)
        shifted = jnp.where(known, jnp.exp(jnp.where(known, everyone - peak[None], 0.0)), 0.0)
        total = jnp.sum(jnp.sum(shifted, axis=0), axis=1, keepdims=True)
        weight = shifted / total[None]
        for g in range(GROUPS):
            own = jnp.sum(jnp.where(lane == line, weight[g], 0.0), axis=1, keepdims=True)
            weights[PER * g:PER * (g + 1), :] = jnp.broadcast_to(own, (PER, LANES))

    def average(chunk):
        def add(q, sums):
            return tuple(s + weights[pl.ds(4 * q + k, 1), :] * twins[chunk, 4 * q + k] for k, s in enumerate(sums))

        sums = lax.fori_loop(0, ALL // 4, add, (jnp.zeros((ROWS, LANES), jnp.float32),) * 4, unroll=4)
        mean_own[chunk] = (sums[0] + sums[1]) + (sums[2] + sums[3])

    place2 = lax.broadcasted_iota(jnp.int32, (PAIRS, LANES), 1)
    line2 = lax.broadcasted_iota(jnp.int32, (PAIRS, LANES), 0)

    def likelihood2():
        cost = jnp.zeros((PAIRS, LANES), jnp.float32)
        for r in range(ROWS):
            miss = lone[0, ALL * r:ALL * r + PAIRS, :] - obs2[1, r:r + 1]
            cost = cost + obs2[0, r:r + 1] * miss * miss + obs2[2, r:r + 1]
        for h in range(2):
            side = (place2 < HALF) if h == 0 else (place2 >= HALF)
            total = -0.5 * jnp.sum(jnp.where(side, cost, 0.0), axis=1, keepdims=True)
            row = jnp.sum(jnp.where(place2 == line2, total, 0.0), axis=0, keepdims=True)
            like_send2[h:h + 1, :] = row
        like_recv2[me] = like_send2[...]
        exchange(lambda other: like_send2, lambda mine: like_recv2.at[mine], sem_small_out.at[1], sem_small_in.at[1])

    def weigh2():
        await_bytes(like_recv2.at[pl.ds(0, GROUPS - 1)], sem_small_in.at[1])
        total = like_recv2[0]
        for g in range(1, GROUPS):
            total = total + like_recv2[g]
        peak = jnp.max(jnp.max(total, axis=0, keepdims=True), axis=1, keepdims=True)
        shifted = jnp.exp(total - peak)
        weight = shifted / jnp.sum(jnp.sum(shifted, axis=0, keepdims=True), axis=1, keepdims=True)
        sides = [jnp.sum(jnp.where(place2 == line2, weight[h:h + 1], 0.0), axis=1, keepdims=True) for h in range(2)]
        weights2[...] = jnp.where(place2 < HALF, sides[0], sides[1])

    def average2(chunk):
        for r in range(ROWS):
            part = weights2[...] * lone[chunk, ALL * r:ALL * r + PAIRS, :]
            mean_send2[chunk, r:r + 1, :] = jnp.sum(part, axis=0, keepdims=True)
        total = mean_send2[chunk]
        total = total + pltpu.roll(total, HALF, axis=1)
        total = jnp.where(lane8 < HALF, mean_own[chunk], total)
        mean_send2[chunk] = total
        mean_recv2[chunk, core, chip] = total

        def one(step, carry):
            pltpu.make_async_remote_copy(
                src_ref=mean_send2.at[chunk], dst_ref=mean_recv2.at[chunk, core, chip],
                send_sem=sem_small_out.at[2 + chunk], recv_sem=sem_small_in.at[2 + chunk],
                device_id={"dom": 2 * lax.rem(chip + step, CHIPS) + core}, device_id_type=MESH,
            ).start()
            return carry

        lax.fori_loop(1, CHIPS, one, 0)

    def means_across(chunk):
        return pltpu.make_async_remote_copy(
            src_ref=mean_recv2.at[chunk, core], dst_ref=mean_recv2.at[chunk, core],
            send_sem=sem_small_out.at[4 + chunk], recv_sem=sem_small_in.at[4 + chunk],
            device_id={"dom": 2 * chip + 1 - core}, device_id_type=MESH,
        )

    def pass_means(chunk):
        await_bytes(mean_recv2.at[chunk, 0, pl.ds(0, CHIPS - 1)], sem_small_in.at[2 + chunk])
        means_across(chunk).start()

    def write_means(chunk):
        means_across(chunk).wait_recv()
        for c in range(CYCLES):
            for f in range(PAIR):
                def loader(g):
                    return lambda u: mean_recv2[chunk, g % 2, (STRIPS * f + g) // 2]

                spans = [(WIDE * g, HALF * c + EDGE, WIDE, loader(g), LANES) for g in range(STRIPS)]
                for u in range(COLS // LANES):
                    averages_v[c, PAIR * chunk + f, :, LANES * u:LANES * (u + 1)] = place(u, spans)

    def edge_coefficients():
        for m in range(2):
            raw[m] = half_turn(courant_v[m])
        for f in range(FIELDS):
            raw[2 + f] = half_turn(diffusion_v[f])

    def coefficients(field):
        def sixteen(m):
            mid = raw[m]
            return jnp.concatenate([jnp.where(upper, raw_north[m], mid), jnp.where(upper, mid, raw_south[m])], axis=0)

        inside = jnp.concatenate([jnp.where(upper, has_north, 1.0), jnp.where(upper, 1.0, has_south)], axis=0)
        column2 = jnp.concatenate([column, column], axis=0)
        cx, cy, d = sixteen(0), sixteen(1), sixteen(2 + field)
        coef[field, 0] = inside * (1.0 - jnp.abs(cx) - jnp.abs(cy) - 4.0 * d)
        coef[field, 1] = inside * (jnp.maximum(cx, 0.0) + d)
        coef[field, 2] = inside * (d - jnp.minimum(cx, 0.0))
        coef[field, 3] = jnp.where(column2 > 0, inside * (jnp.maximum(cy, 0.0) + d), 0.0)
        coef[field, 4] = jnp.where(column2 < COLS - 1, inside * (d - jnp.minimum(cy, 0.0)), 0.0)

    def window(get, rows):
        for g in range(STRIPS):
            spans = [(HALF * h, WIDE * g - EDGE, SPAN, lambda u: get(pl.ds(LANES * u, LANES)), COLS) for h in range(2)]
            windows[g, :rows] = place(0, spans, rows)
        return windows[strip, :rows]

    def coefficients2(chunk):
        lane16 = lax.broadcasted_iota(jnp.int32, (2 * ROWS, LANES), 1)
        used = lax.rem(lane16, HALF) < SPAN
        for n in range(5):
            here = window(lambda cols: coef[PAIR * chunk + in_pair, n, :, cols], 2 * ROWS)
            here = jnp.where(used, here, 0.0)
            for r in range(2 * ROWS):
                coef2[chunk, n, r] = jnp.broadcast_to(here[r:r + 1], (ROWS, LANES))

    def observations():
        cell = lax.broadcasted_iota(jnp.int32, (ROWS, COLS), 0) * COLS + column
        zero = jnp.zeros((ROWS, COLS), jnp.float32)

        def gather(k, sums):
            here = cell == obs_loc_s[0, k]
            precision = jnp.where(here, 1.0 / jnp.full((1, COLS), obs_var_s[0, k], jnp.float32), 0.0)
            return (sums[0] + precision,) + tuple(sums[1 + c] + precision * observed_s[c, 0, k] for c in range(CYCLES))

        sums = lax.fori_loop(0, NOBS, gather, (zero,) * (1 + CYCLES), unroll=8)
        obs_weight[...] = sums[0]
        seen = sums[0] > 0.0
        means = []
        for c in range(CYCLES):
            means.append(jnp.where(seen, sums[1 + c] / jnp.where(seen, sums[0], 1.0), 0.0))
            obs_mean[c] = means[c]

        def rest(k, sums):
            here = cell == obs_loc_s[0, k]
            precision = jnp.where(here, 1.0 / jnp.full((1, COLS), obs_var_s[0, k], jnp.float32), 0.0)
            return tuple(sums[c] + precision * (observed_s[c, 0, k] - means[c]) * (observed_s[c, 0, k] - means[c])
                         for c in range(CYCLES))

        sums = lax.fori_loop(0, NOBS, rest, (zero,) * CYCLES, unroll=8)
        for c in range(CYCLES):
            obs_rest[c] = sums[c]

    def observations2():
        inner = lax.rem(lane8, HALF)
        own = (inner >= EDGE) & (inner < EDGE + WIDE)
        first = jnp.where(in_pair == 0, 1.0, 0.0).astype(jnp.float32)
        obs2[0] = jnp.where(own, window(lambda cols: obs_weight[:, cols], ROWS), 0.0) * first
        obs2[1] = window(lambda cols: obs_mean[1, :, cols], ROWS)
        obs2[2] = jnp.where(own, window(lambda cols: obs_rest[1, :, cols], ROWS), 0.0) * first

    def noise_of(k, field, cols):
        return noise_v[1, k, field, :, cols]

    def state_of(k, field, cols):
        return result[field, k, :, cols]

    loads[0].wait()
    pack(0, noise_of, noise_send, noise_recv)
    for n in (1, 2, 6, 7):
        loads[n].wait()
    edge_coefficients()
    begin(0)
    pl.semaphore_wait(barrier, GROUPS + 1)

    def edges(ready):
        for way in (True, False):
            halo_copy(ready, way).wait_recv()

    def send_edges(field):
        for way in (True, False):
            halo_copy(field, way).start()

    for way in (True, False):
        raw_copy(0, way).start()
    send_edges(0)
    swap(noise_send, noise_recv, 0, 0)
    begin(1)
    send_edges(1)
    for way in (True, False):
        raw_copy(1, way).start()
    for n in (3, 4, 5, 8, 9, 10, 11):
        loads[n].wait()
    for f in range(2, FIELDS):
        begin(f)
    observations()
    for way in (True, False):
        raw_copy(0, way).wait_recv()
    coefficients(0)
    edges(0)
    send_edges(2)
    forecast(0)
    likelihood()
    for way in (True, False):
        raw_copy(1, way).wait_recv()
    coefficients(1)
    edges(1)
    send_edges(3)
    forecast(1)
    pack(0, state_of, state_send, state_recv)
    swap(state_send, state_recv, 0, 1)
    for f in range(2, FIELDS):
        coefficients(f)
        edges(f)
        begin(f + PAIR)
        send_edges(f + PAIR)
        forecast(f)
    pack(1, state_of, state_send, state_recv)
    swap(state_send, state_recv, 1, 1)
    for chunk in range(CHUNKS):
        coefficients2(chunk)
    observations2()
    unpack_noise(0)
    for f in range(FIELDS, SLOTS):
        edges(f)
        forecast(f)
    pack_late()
    swap_late()
    weigh()
    await_bytes(others(state_recv, 0), sem_in.at[0, 1])
    unpack_state(0)
    for block in range(BLOCKS):
        begin2(0, block)
    average(0)
    for block in range(BLOCKS):
        forecast2(0, block)
    likelihood2()
    pack_back(0)
    swap(back_send, back_recv, 0, 2)
    await_bytes(others(state_recv, 1), sem_in.at[1, 1])
    unpack_state(1)
    for block in range(BLOCKS):
        begin2(1, block)
    weigh2()
    average2(0)
    average(1)
    for block in range(BLOCKS):
        forecast2(1, block)
    add_late()
    sum_late()
    average2(1)
    pack_back(1)
    swap(back_send, back_recv, 1, 2)
    pass_means(0)
    finish(0)
    write_means(0)
    for copy in stores(0):
        copy.start()
    pass_means(1)
    finish(1)
    stores(1)[0].start()
    write_means(1)
    stores(1)[1].start()
    await_bytes(others(noise_recv, 0), sem_out.at[0, 0])
    await_bytes(late_recv.at[pl.ds(0, GROUPS - 1)], sem_out.at[1, 0])
    for chunk in range(CHUNKS):
        await_bytes(others(state_recv, chunk), sem_out.at[chunk, 1])
    for chunk in range(CHUNKS):
        await_bytes(others(back_recv, chunk), sem_out.at[chunk, 2])
        await_bytes(mean_recv2.at[chunk, 0, pl.ds(0, CHIPS - 1)], sem_small_out.at[2 + chunk])
        means_across(chunk).wait_send()
        for copy in stores(chunk):
            copy.wait()
    for way in (True, False):
        for f in range(SLOTS):
            halo_copy(f, way).wait_send()
        for part in range(2):
            raw_copy(part, way).wait_send()
        for chunk in range(CHUNKS):
            for block in range(BLOCKS):
                halo_copy2(chunk, block, way).wait_send()
    for n, ref in enumerate((like_recv, like_recv2)):
        await_bytes(ref.at[pl.ds(0, GROUPS - 1)], sem_small_out.at[n])


def hand_over(ensemble, averages, ensemble_out, averages_out, ensemble_v, averages_v, sem_in, sem_out):
    size = PER // PARTS
    ways = [(ensemble.at[pl.ds(size * n, size)], ensemble_v.at[pl.ds(size * n, size)],
             ensemble_out.at[pl.ds(size * n, size)]) for n in range(PARTS)]
    ways.append((averages, averages_v, averages_out))
    into = [pltpu.make_async_copy(source, middle, sem_in.at[n]) for n, (source, middle, _) in enumerate(ways)]
    away = [pltpu.make_async_copy(middle, target, sem_out.at[n]) for n, (_, middle, target) in enumerate(ways)]
    for copy in into:
        copy.start()
    for first, second in zip(into, away):
        first.wait()
        second.start()
    for copy in away:
        copy.wait()


def per_device(members, noise, courant, diffusion, obs_loc, observed, obs_var, ancestors):
    f32 = jnp.float32
    anywhere = pl.BlockSpec(memory_space=pl.ANY)
    plane = (ROWS, COLS)
    one = (ROWS, LANES)
    operands = (members, noise, courant, diffusion, obs_loc, observed, obs_var, ancestors)

    def vmem(*shape):
        return pltpu.VMEM(shape, f32)

    scratch = [vmem(PER, FIELDS, *plane), vmem(CYCLES, FIELDS, *plane)]
    scratch += [vmem(*a.shape) for a in operands[:4]] + [pltpu.SMEM(a.shape, a.dtype) for a in operands[4:]]
    scratch += [vmem(1, GROUPS, ROWS, PER * SPAN) for _ in range(2)]
    scratch += [vmem(GROUPS, ROWS, PER * WIDE) for _ in range(2)] + [vmem((ROWS + 1) * PAIRS, LANES)]
    scratch += [vmem(CHUNKS, GROUPS, ROWS, PER * SPAN) for _ in range(2)]
    scratch += [vmem(CHUNKS, GROUPS, ROWS, PER * WIDE) for _ in range(2)]
    scratch += [vmem(SLOTS, PER // 2, *plane) for _ in range(4)]
    scratch += [
        vmem(SLOTS, PER, *plane),
        vmem(SLOTS, PER, *plane),
        vmem(2 + FIELDS, *plane),
        vmem(2 + FIELDS, *plane),
        vmem(2 + FIELDS, *plane),
        vmem(FIELDS, 5, 2 * ROWS, COLS),
        vmem(*plane),
        vmem(CYCLES, *plane),
        vmem(CYCLES, *plane),
        vmem(PER, LANES),
        vmem(ALL, LANES),
        vmem(1, LANES),
        vmem(GROUPS, 1, LANES),
        vmem(CHUNKS, *one),
        vmem(1, PAIRS, *one),
        vmem(CHUNKS, ALL, *one),
        vmem(CHUNKS, BLOCKS, (ROWS + 2 * EDGE) * BLOCK, LANES),
        vmem(CHUNKS, (ROWS + 1) * ALL, LANES),
        vmem(CHUNKS, 5, 2 * ROWS, *one),
        vmem(STRIPS, 2 * ROWS, LANES),
        vmem(3, *one),
        vmem(PAIRS, LANES),
        vmem(2, LANES),
        vmem(GROUPS, 2, LANES),
        vmem(CHUNKS, *one),
        vmem(CHUNKS, 2, CHIPS, *one),
        pltpu.SemaphoreType.DMA((12,)),
        pltpu.SemaphoreType.DMA((CHUNKS, 2)),
        pltpu.SemaphoreType.DMA((CHUNKS, 3)),
        pltpu.SemaphoreType.DMA((CHUNKS, 3)),
        pltpu.SemaphoreType.DMA((SLOTS, 2)),
        pltpu.SemaphoreType.DMA((SLOTS, 2)),
        pltpu.SemaphoreType.DMA((CHUNKS, BLOCKS, 2)),
        pltpu.SemaphoreType.DMA((CHUNKS, BLOCKS, 2)),
        pltpu.SemaphoreType.DMA((2, 2)),
        pltpu.SemaphoreType.DMA((2, 2)),
        pltpu.SemaphoreType.DMA((6,)),
        pltpu.SemaphoreType.DMA((6,)),
    ]
    results = pl.pallas_call(
        kernel,
        out_shape=(
            jax.ShapeDtypeStruct((PER, FIELDS) + plane, f32),
            jax.ShapeDtypeStruct((CYCLES, FIELDS) + plane, f32),
        ),
        in_specs=[anywhere] * 8,
        out_specs=(anywhere, anywhere),
        scratch_shapes=scratch,
        compiler_params=pltpu.CompilerParams(
            collective_id=0, has_side_effects=True, vmem_limit_bytes=60 * 1024 * 1024
        ),
        name="assimilate",
    )(*operands)
    return pl.pallas_call(
        hand_over,
        out_shape=tuple(jax.ShapeDtypeStruct(r.shape, f32) for r in results),
        in_specs=[anywhere] * 2,
        out_specs=(anywhere, anywhere),
        scratch_shapes=[vmem(*r.shape) for r in results] + [pltpu.SemaphoreType.DMA((PARTS + 1,))] * 2,
        compiler_params=pltpu.CompilerParams(vmem_limit_bytes=60 * 1024 * 1024),
        name="hand_over",
    )(*results)


def solution(mesh):
    return jax.shard_map(
        per_device,
        mesh=mesh,
        in_specs=(
            P("dom", None, "tile", None),
            P(None, "dom", None, "tile", None),
            P(None, "tile", None),
            P(None, "tile", None),
            P("tile", None),
            P(None, "tile", None),
            P("tile", None),
            P(None, "tile", None),
        ),
        out_specs=(P("dom", None, "tile", None), P(None, None, "tile", None)),
        check_vma=False,
    )
```

```python
import jax
import jax.numpy as jnp
from jax import lax
from jax.experimental import pallas as pl
from jax.experimental.pallas import tpu as pltpu
from jax.sharding import PartitionSpec as P

MESH = pl.DeviceIdType.MESH
STEPS = 4
CYCLES = 2
FIELDS = 4
PER = 16
GROUPS = 16
CHIPS = 8
ALL = PER * GROUPS
PAIRS = ALL // 2
TILES = 16
ROWS = 8
COLS = 384
LANES = 128
HALF = LANES // 2
NOBS = 64
CHUNKS = 2
PAIR = 2
SLOTS = FIELDS + PAIR
STRIPS = 8
WIDE = COLS // STRIPS
EDGE = STEPS
SPAN = WIDE + 2 * EDGE
BLOCKS = 4
BLOCK = PAIRS // BLOCKS


def half_turn(x):
    return pltpu.roll(x, 4, axis=0)


def place(vector, spans, rows=ROWS):
    lane = lax.broadcasted_iota(jnp.int32, (rows, LANES), 1)
    result = None
    for begin, column, length, load, limit in spans:
        low, high = max(begin, vector * LANES), min(begin + length, (vector + 1) * LANES)
        if low >= high:
            continue
        column = column + low - begin
        low, high = low - vector * LANES, high - vector * LANES
        first = max(column, 0) // LANES
        last = min(column + high - low, limit) - 1
        for u in range(first, last // LANES + 1):
            piece = load(u)
            shift = (low - column + LANES * u) % LANES
            if shift:
                piece = pltpu.roll(piece, shift, axis=1)
            start = max(low, low - column + LANES * u)
            result = piece if result is None else jnp.where(lane >= start, piece, result)
    return result


def kernel(members, noise, courant, diffusion, obs_loc, observed, obs_var, ancestors, out, last, averages,
           out_v, averages_v,
           members_v, noise_v, courant_v, diffusion_v, obs_loc_s, observed_s, obs_var_s, ancestors_s,
           noise_send, noise_recv, late_send, late_recv, late_rows, state_send, state_recv, back_send, back_recv,
           to_north, to_south, from_north, from_south,
           state, result, raw, raw_north, raw_south, coef, obs_weight, obs_mean, obs_rest, partial, weights,
           like_send, like_recv, mean_own,
           noise_pairs, twins, grid2, lone, coef2, windows, obs2, weights2, like_send2, like_recv2,
           mean_send2, mean_recv2,
           sem_load, sem_store, sem_own, sem_out, sem_in, sem_halo_out, sem_halo_in, sem_halo2_out, sem_halo2_in, sem_raw_out,
           sem_raw_in, sem_small_out, sem_small_in):
    me = lax.axis_index("dom")
    tile = lax.axis_index("tile")
    north = lax.rem(tile + TILES - 1, TILES)
    south = lax.rem(tile + 1, TILES)
    strip = lax.rem(me, STRIPS)
    in_pair = lax.div(me, STRIPS)
    chip = lax.div(me, 2)
    core = lax.rem(me, 2)

    def peer(step):
        return lax.rem(me + step, GROUPS)

    barrier = pltpu.get_barrier_semaphore()

    def greet(step, carry):
        pl.semaphore_signal(barrier, inc=1, device_id={"dom": peer(step)}, device_id_type=MESH)
        return carry

    for neighbour in (north, south):
        pl.semaphore_signal(barrier, inc=1, device_id={"tile": neighbour}, device_id_type=MESH)
    lax.fori_loop(1, GROUPS, greet, 0)

    loads = []

    def load(source, target):
        loads.append(pltpu.make_async_copy(source, target, sem_load.at[len(loads)]))
        loads[-1].start()

    for chunk in range(CHUNKS):
        two = pl.ds(PAIR * chunk, PAIR)
        load(noise.at[1, :, two], noise_v.at[1, :, two])
        load(members.at[:, two], members_v.at[:, two])
        load(noise.at[0, :, two], noise_v.at[0, :, two])
    for source, target in ((courant, courant_v), (diffusion, diffusion_v), (obs_loc, obs_loc_s),
                           (observed, observed_s), (obs_var, obs_var_s), (ancestors, ancestors_s)):
        load(source, target)

    upper = lax.broadcasted_iota(jnp.int32, (ROWS, COLS), 0) < 4
    upper1 = lax.broadcasted_iota(jnp.int32, (ROWS, LANES), 0) < 4
    column = lax.broadcasted_iota(jnp.int32, (ROWS, COLS), 1)
    lane8 = lax.broadcasted_iota(jnp.int32, (ROWS, LANES), 1)
    has_north = jnp.where(tile > 0, 1.0, 0.0).astype(jnp.float32)
    has_south = jnp.where(tile < TILES - 1, 1.0, 0.0).astype(jnp.float32)

    def exchange(source_of, target_of, out_sem, in_sem):
        def one(step, carry):
            near = lax.div(step + 1, 2)
            other = peer(jnp.where(lax.rem(step, 2) == 1, near, GROUPS - near))
            pltpu.make_async_remote_copy(
                src_ref=source_of(other), dst_ref=target_of(me), send_sem=out_sem, recv_sem=in_sem,
                device_id={"dom": other}, device_id_type=MESH,
            ).start()
            return carry

        lax.fori_loop(1, GROUPS, one, 0)

    def await_bytes(ref, sem):
        pltpu.make_async_copy(ref, ref, sem).wait()

    def others(ref, chunk):
        return ref.at[chunk, pl.ds(0, GROUPS - 1)]

    def tile_copy(source, target, out_sem, in_sem, southward):
        return pltpu.make_async_remote_copy(
            src_ref=source, dst_ref=target, send_sem=out_sem, recv_sem=in_sem,
            device_id={"tile": south if southward else north}, device_id_type=MESH,
        )

    def halo_copy(field, southward):
        source, target = (to_south, from_north) if southward else (to_north, from_south)
        way = 1 if southward else 0
        return tile_copy(source.at[field], target.at[field], sem_halo_out.at[field, way], sem_halo_in.at[field, way],
                         southward)

    def halo_copy2(chunk, block, southward):
        source, target = (ROWS, 0) if southward else (EDGE, ROWS + EDGE)
        way = 1 if southward else 0
        rows = EDGE * BLOCK
        return tile_copy(grid2.at[chunk, block, pl.ds(source * BLOCK, rows)],
                         grid2.at[chunk, block, pl.ds(target * BLOCK, rows)], sem_halo2_out.at[chunk, block, way],
                         sem_halo2_in.at[chunk, block, way], southward)

    def raw_copy(part, southward):
        rows = pl.ds(3 * part, 3)
        target = raw_north if southward else raw_south
        way = 1 if southward else 0
        return tile_copy(raw.at[rows], target.at[rows], sem_raw_out.at[part, way], sem_raw_in.at[part, way], southward)

    def begin(field):
        def start_of(particle):
            if field < FIELDS:
                return members_v[particle, field] + noise_v[0, particle, field]
            return noise_v[1, particle, field - PAIR]

        def pair(i, carry):
            first, second = 2 * i, 2 * i + 1
            v0, v1 = start_of(first), start_of(second)
            r0, r1 = half_turn(v0), half_turn(v1)
            state[field, first] = r0
            state[field, second] = r1
            to_south[field, i] = jnp.where(upper, r0, v1)
            to_north[field, i] = jnp.where(upper, v0, r1)
            return carry

        lax.fori_loop(0, PER // 2, pair, 0, unroll=2)

    def forecast(field):
        by = field if field < FIELDS else field - PAIR

        def four(q, carry):
            for i in (2 * q, 2 * q + 1):
                top = from_north[field, i] * has_north
                bottom = from_south[field, i] * has_south
                for k, (above, below) in enumerate(((top, half_turn(bottom)), (half_turn(top), bottom))):
                    particle = 2 * i + k
                    r = state[field, particle]
                    x = jnp.concatenate([jnp.where(upper, above, r), jnp.where(upper, r, below)], axis=0)
                    for _ in range(STEPS):
                        x = (coef[by, 0] * x + coef[by, 1] * pltpu.roll(x, 1, axis=0)
                             + coef[by, 2] * pltpu.roll(x, 2 * ROWS - 1, axis=0)
                             + coef[by, 3] * pltpu.roll(x, 1, axis=1)
                             + coef[by, 4] * pltpu.roll(x, COLS - 1, axis=1))
                    v = half_turn(jnp.where(upper, x[ROWS:], x[:ROWS]))
                    result[field, particle] = v
                    if field == 0:
                        miss = v - obs_mean[0]
                        cost = obs_weight[...] * miss * miss + obs_rest[0]
                        cost = cost[:, :LANES] + cost[:, LANES:2 * LANES] + cost[:, 2 * LANES:]
                        partial[pl.ds(particle, 1), :] = jnp.sum(cost, axis=0, keepdims=True)
            return carry

        lax.fori_loop(0, PER // 4, four, 0)

    def pack(chunk, get, outgoing, incoming):
        def one(f, carry):
            for g in range(STRIPS):
                def loader(k):
                    return lambda u: get(k, PAIR * chunk + f, pl.ds(LANES * u, LANES))

                spans = [(SPAN * k, WIDE * g - EDGE, SPAN, loader(k), COLS) for k in range(PER)]
                for j in range(PER * SPAN // LANES):
                    outgoing[chunk, STRIPS * f + g, :, LANES * j:LANES * (j + 1)] = place(j, spans)
            return carry

        lax.fori_loop(0, PAIR, one, 0)
        incoming[chunk, me] = outgoing[chunk, me]

    def swap(outgoing, incoming, chunk, which):
        exchange(lambda other: outgoing.at[chunk, other], lambda mine: incoming.at[chunk, mine],
                 sem_out.at[chunk, which], sem_in.at[chunk, which])

    def pack_late():
        def one(f, carry):
            for g in range(STRIPS):
                def loader(k):
                    return lambda u: result[FIELDS + f, k, :, pl.ds(LANES * u, LANES)]

                spans = [(WIDE * k, WIDE * g, WIDE, loader(k), COLS) for k in range(PER)]
                for j in range(PER * WIDE // LANES):
                    late_send[STRIPS * f + g, :, LANES * j:LANES * (j + 1)] = place(j, spans)
            return carry

        lax.fori_loop(0, PAIR, one, 0)
        late_recv[me] = late_send[me]

    def swap_late():
        exchange(lambda other: late_send.at[other], lambda mine: late_recv.at[mine], sem_out.at[1, 0], sem_in.at[1, 0])

    def add_late():
        await_bytes(late_recv.at[pl.ds(0, GROUPS - 1)], sem_in.at[1, 0])

        def one(s, carry):
            def load_from(u):
                return late_recv[s, :, LANES * u:LANES * (u + 1)]

            for m in range(PER // 2):
                late_rows[pl.ds(PER // 2 * s + m, ROWS, stride=PAIRS), :] = place(
                    0, [(HALF * h + EDGE, WIDE * (2 * m + h), WIDE, load_from, PER * WIDE) for h in range(2)])
            return carry

        lax.fori_loop(0, GROUPS, one, 0, unroll=4)

    def sum_late():
        for r in range(ROWS):
            x = lone[1, ALL * r:ALL * r + PAIRS, :] + late_rows[PAIRS * r:PAIRS * (r + 1), :]
            lone[1, ALL * r:ALL * r + PAIRS, :] = x
            lone[1, ALL * r + PAIRS:ALL * (r + 1), :] = pltpu.roll(x, HALF, axis=1)

    def unpack_noise(chunk):
        await_bytes(others(noise_recv, chunk), sem_in.at[chunk, 0])

        def one(s, carry):
            def load_from(u):
                return noise_recv[chunk, s, :, LANES * u:LANES * (u + 1)]

            for m in range(PER // 2):
                noise_pairs[chunk, PER // 2 * s + m] = place(
                    0, [(HALF * h, SPAN * (2 * m + h), SPAN, load_from, PER * SPAN) for h in range(2)])
            return carry

        lax.fori_loop(0, GROUPS, one, 0, unroll=4)

    def unpack_state(chunk):

        def one(s, carry):
            def load_from(u):
                return state_recv[chunk, s, :, LANES * u:LANES * (u + 1)]

            for k in range(PER):
                twins[chunk, PER * s + k] = place(
                    0, [(HALF * h, SPAN * k, SPAN, load_from, PER * SPAN) for h in range(2)])
            return carry

        lax.fori_loop(0, GROUPS, one, 0, unroll=2)

    def begin2(chunk, block):
        left = lane8 < HALF

        def one(i, carry):
            m = BLOCK * block + i
            old0, old1 = ancestors_s[0, 0, 2 * m], ancestors_s[0, 0, 2 * m + 1]
            v = jnp.where(left, twins[chunk, old0], twins[chunk, old1])
            if chunk == 0:
                v = v + noise_pairs[chunk, m]
            grid2[chunk, block, pl.ds(EDGE * BLOCK + i, ROWS, stride=BLOCK), :] = v
            return carry

        lax.fori_loop(0, BLOCK, one, 0, unroll=8)
        halo_copy2(chunk, block, True).start()
        halo_copy2(chunk, block, False).start()

    def forecast2(chunk, block):
        halo_copy2(chunk, block, True).wait_recv()
        halo_copy2(chunk, block, False).wait_recv()
        high = ROWS + 2 * EDGE

        def tall(n, r):
            return jnp.concatenate([coef2[chunk, n, r]] * (BLOCK // ROWS), axis=0)

        x = [grid2[chunk, block, BLOCK * r:BLOCK * (r + 1), :] for r in range(high)]
        x = [v * has_north if r < EDGE else v * has_south if r >= EDGE + ROWS else v for r, v in enumerate(x)]
        for s in range(1, STEPS + 1):
            new = list(x)
            for r in range(s, high - s):
                new[r] = (tall(0, r) * x[r] + tall(1, r) * x[r - 1] + tall(2, r) * x[r + 1]
                          + tall(3, r) * pltpu.roll(x[r], 1, axis=1) + tall(4, r) * pltpu.roll(x[r], LANES - 1, axis=1))
            x = new
        for r in range(ROWS):
            lone[chunk, ALL * r + BLOCK * block:ALL * r + BLOCK * (block + 1), :] = x[EDGE + r]
            if chunk == 0:
                low = ALL * r + PAIRS + BLOCK * block
                lone[chunk, low:low + BLOCK, :] = pltpu.roll(x[EDGE + r], HALF, axis=1)

    def pack_back(chunk):
        def one(group, carry):
            def loader(j):
                old = ancestors_s[1, 0, PER * group + j]
                tall = lone[chunk, pl.ds((old & 1) * PAIRS + (old >> 1), ROWS, stride=ALL), :]
                return lambda u: tall

            spans = [(WIDE * j, EDGE, WIDE, loader(j), LANES) for j in range(PER)]
            for n in range(PER * WIDE // LANES):
                back_send[chunk, group, :, LANES * n:LANES * (n + 1)] = place(n, spans)
            return carry

        lax.fori_loop(0, GROUPS, one, 0, unroll=4)
        if chunk == 0:
            back_recv[chunk, me] = back_send[chunk, me]
        else:
            own_back().start()

    def own_back():
        return pltpu.make_async_copy(back_send.at[1, me], last.at[me], sem_own)

    def swap_last():
        exchange(lambda other: back_send.at[1, other], lambda mine: last.at[mine], sem_out.at[1, 2], sem_in.at[1, 2])

    def stores(chunk):
        two = pl.ds(PAIR * chunk, PAIR)
        copies = [pltpu.make_async_copy(averages_v.at[:, two], averages.at[:, two], sem_store.at[chunk, 1])]
        if chunk == 0:
            copies.append(pltpu.make_async_copy(out_v, out, sem_store.at[chunk, 0]))
        return copies

    def finish(chunk):
        await_bytes(others(back_recv, chunk), sem_in.at[chunk, 2])

        def one(f, carry):
            def loader(g):
                return lambda u: back_recv[chunk, STRIPS * f + g, :, LANES * u:LANES * (u + 1)]

            for j in range(PER):
                spans = [(WIDE * g, WIDE * j, WIDE, loader(g), PER * WIDE) for g in range(STRIPS)]
                for u in range(COLS // LANES):
                    out_v[j, f, :, LANES * u:LANES * (u + 1)] = place(u, spans)
            return carry

        lax.fori_loop(0, PAIR, one, 0)

    lane = lax.broadcasted_iota(jnp.int32, (PER, LANES), 1)
    line = lax.broadcasted_iota(jnp.int32, (PER, LANES), 0)

    def likelihood():
        total = -0.5 * jnp.sum(partial[...], axis=1, keepdims=True)
        row = jnp.sum(jnp.where(lane == line, total, 0.0), axis=0, keepdims=True)
        like_send[...] = row
        like_recv[me] = row
        exchange(lambda other: like_send, lambda mine: like_recv.at[mine], sem_small_out.at[0], sem_small_in.at[0])

    def weigh():
        await_bytes(like_recv.at[pl.ds(0, GROUPS - 1)], sem_small_in.at[0])
        everyone = like_recv[...]
        known = lax.broadcasted_iota(jnp.int32, (GROUPS, 1, LANES), 2) < PER
        peak = jnp.max(jnp.where(known, everyone, -3.0e38), axis=0)
        peak = jnp.max(peak, axis=1, keepdims=True)
        shifted = jnp.where(known, jnp.exp(jnp.where(known, everyone - peak[None], 0.0)), 0.0)
        total = jnp.sum(jnp.sum(shifted, axis=0), axis=1, keepdims=True)
        weight = shifted / total[None]
        for g in range(GROUPS):
            own = jnp.sum(jnp.where(lane == line, weight[g], 0.0), axis=1, keepdims=True)
            weights[PER * g:PER * (g + 1), :] = jnp.broadcast_to(own, (PER, LANES))

    def average(chunk):
        def add(q, sums):
            return tuple(s + weights[pl.ds(4 * q + k, 1), :] * twins[chunk, 4 * q + k] for k, s in enumerate(sums))

        sums = lax.fori_loop(0, ALL // 4, add, (jnp.zeros((ROWS, LANES), jnp.float32),) * 4, unroll=4)
        mean_own[chunk] = (sums[0] + sums[1]) + (sums[2] + sums[3])

    place2 = lax.broadcasted_iota(jnp.int32, (PAIRS, LANES), 1)
    line2 = lax.broadcasted_iota(jnp.int32, (PAIRS, LANES), 0)

    def likelihood2():
        cost = jnp.zeros((PAIRS, LANES), jnp.float32)
        for r in range(ROWS):
            miss = lone[0, ALL * r:ALL * r + PAIRS, :] - obs2[1, r:r + 1]
            cost = cost + obs2[0, r:r + 1] * miss * miss + obs2[2, r:r + 1]
        for h in range(2):
            side = (place2 < HALF) if h == 0 else (place2 >= HALF)
            total = -0.5 * jnp.sum(jnp.where(side, cost, 0.0), axis=1, keepdims=True)
            row = jnp.sum(jnp.where(place2 == line2, total, 0.0), axis=0, keepdims=True)
            like_send2[h:h + 1, :] = row
        like_recv2[me] = like_send2[...]
        exchange(lambda other: like_send2, lambda mine: like_recv2.at[mine], sem_small_out.at[1], sem_small_in.at[1])

    def weigh2():
        await_bytes(like_recv2.at[pl.ds(0, GROUPS - 1)], sem_small_in.at[1])
        total = like_recv2[0]
        for g in range(1, GROUPS):
            total = total + like_recv2[g]
        peak = jnp.max(jnp.max(total, axis=0, keepdims=True), axis=1, keepdims=True)
        shifted = jnp.exp(total - peak)
        weight = shifted / jnp.sum(jnp.sum(shifted, axis=0, keepdims=True), axis=1, keepdims=True)
        sides = [jnp.sum(jnp.where(place2 == line2, weight[h:h + 1], 0.0), axis=1, keepdims=True) for h in range(2)]
        weights2[...] = jnp.where(place2 < HALF, sides[0], sides[1])

    def average2(chunk):
        for r in range(ROWS):
            part = weights2[...] * lone[chunk, ALL * r:ALL * r + PAIRS, :]
            mean_send2[chunk, r:r + 1, :] = jnp.sum(part, axis=0, keepdims=True)
        total = mean_send2[chunk]
        total = total + pltpu.roll(total, HALF, axis=1)
        total = jnp.where(lane8 < HALF, mean_own[chunk], total)
        mean_send2[chunk] = total
        mean_recv2[chunk, core, chip] = total

        def one(step, carry):
            pltpu.make_async_remote_copy(
                src_ref=mean_send2.at[chunk], dst_ref=mean_recv2.at[chunk, core, chip],
                send_sem=sem_small_out.at[2 + chunk], recv_sem=sem_small_in.at[2 + chunk],
                device_id={"dom": 2 * lax.rem(chip + step, CHIPS) + core}, device_id_type=MESH,
            ).start()
            return carry

        lax.fori_loop(1, CHIPS, one, 0)

    def means_across(chunk):
        return pltpu.make_async_remote_copy(
            src_ref=mean_recv2.at[chunk, core], dst_ref=mean_recv2.at[chunk, core],
            send_sem=sem_small_out.at[4 + chunk], recv_sem=sem_small_in.at[4 + chunk],
            device_id={"dom": 2 * chip + 1 - core}, device_id_type=MESH,
        )

    def pass_means(chunk):
        await_bytes(mean_recv2.at[chunk, 0, pl.ds(0, CHIPS - 1)], sem_small_in.at[2 + chunk])
        means_across(chunk).start()

    def write_means(chunk):
        means_across(chunk).wait_recv()
        for c in range(CYCLES):
            for f in range(PAIR):
                def loader(g):
                    return lambda u: mean_recv2[chunk, g % 2, (STRIPS * f + g) // 2]

                spans = [(WIDE * g, HALF * c + EDGE, WIDE, loader(g), LANES) for g in range(STRIPS)]
                for u in range(COLS // LANES):
                    averages_v[c, PAIR * chunk + f, :, LANES * u:LANES * (u + 1)] = place(u, spans)

    def edge_coefficients():
        for m in range(2):
            raw[m] = half_turn(courant_v[m])
        for f in range(FIELDS):
            raw[2 + f] = half_turn(diffusion_v[f])

    def coefficients(field):
        def sixteen(m):
            mid = raw[m]
            return jnp.concatenate([jnp.where(upper, raw_north[m], mid), jnp.where(upper, mid, raw_south[m])], axis=0)

        inside = jnp.concatenate([jnp.where(upper, has_north, 1.0), jnp.where(upper, 1.0, has_south)], axis=0)
        column2 = jnp.concatenate([column, column], axis=0)
        cx, cy, d = sixteen(0), sixteen(1), sixteen(2 + field)
        coef[field, 0] = inside * (1.0 - jnp.abs(cx) - jnp.abs(cy) - 4.0 * d)
        coef[field, 1] = inside * (jnp.maximum(cx, 0.0) + d)
        coef[field, 2] = inside * (d - jnp.minimum(cx, 0.0))
        coef[field, 3] = jnp.where(column2 > 0, inside * (jnp.maximum(cy, 0.0) + d), 0.0)
        coef[field, 4] = jnp.where(column2 < COLS - 1, inside * (d - jnp.minimum(cy, 0.0)), 0.0)

    def window(get, rows):
        for g in range(STRIPS):
            spans = [(HALF * h, WIDE * g - EDGE, SPAN, lambda u: get(pl.ds(LANES * u, LANES)), COLS) for h in range(2)]
            windows[g, :rows] = place(0, spans, rows)
        return windows[strip, :rows]

    def coefficients2(chunk):
        lane16 = lax.broadcasted_iota(jnp.int32, (2 * ROWS, LANES), 1)
        used = lax.rem(lane16, HALF) < SPAN
        for n in range(5):
            here = window(lambda cols: coef[PAIR * chunk + in_pair, n, :, cols], 2 * ROWS)
            here = jnp.where(used, here, 0.0)
            for r in range(2 * ROWS):
                coef2[chunk, n, r] = jnp.broadcast_to(here[r:r + 1], (ROWS, LANES))

    def observations():
        cell = lax.broadcasted_iota(jnp.int32, (ROWS, COLS), 0) * COLS + column
        zero = jnp.zeros((ROWS, COLS), jnp.float32)

        def gather(k, sums):
            here = cell == obs_loc_s[0, k]
            precision = jnp.where(here, 1.0 / jnp.full((1, COLS), obs_var_s[0, k], jnp.float32), 0.0)
            return (sums[0] + precision,) + tuple(sums[1 + c] + precision * observed_s[c, 0, k] for c in range(CYCLES))

        sums = lax.fori_loop(0, NOBS, gather, (zero,) * (1 + CYCLES), unroll=8)
        obs_weight[...] = sums[0]
        seen = sums[0] > 0.0
        means = []
        for c in range(CYCLES):
            means.append(jnp.where(seen, sums[1 + c] / jnp.where(seen, sums[0], 1.0), 0.0))
            obs_mean[c] = means[c]

        def rest(k, sums):
            here = cell == obs_loc_s[0, k]
            precision = jnp.where(here, 1.0 / jnp.full((1, COLS), obs_var_s[0, k], jnp.float32), 0.0)
            return tuple(sums[c] + precision * (observed_s[c, 0, k] - means[c]) * (observed_s[c, 0, k] - means[c])
                         for c in range(CYCLES))

        sums = lax.fori_loop(0, NOBS, rest, (zero,) * CYCLES, unroll=8)
        for c in range(CYCLES):
            obs_rest[c] = sums[c]

    def observations2():
        inner = lax.rem(lane8, HALF)
        own = (inner >= EDGE) & (inner < EDGE + WIDE)
        first = jnp.where(in_pair == 0, 1.0, 0.0).astype(jnp.float32)
        obs2[0] = jnp.where(own, window(lambda cols: obs_weight[:, cols], ROWS), 0.0) * first
        obs2[1] = window(lambda cols: obs_mean[1, :, cols], ROWS)
        obs2[2] = jnp.where(own, window(lambda cols: obs_rest[1, :, cols], ROWS), 0.0) * first

    def noise_of(k, field, cols):
        return noise_v[1, k, field, :, cols]

    def state_of(k, field, cols):
        return result[field, k, :, cols]

    loads[0].wait()
    pack(0, noise_of, noise_send, noise_recv)
    for n in (1, 2, 6, 7):
        loads[n].wait()
    edge_coefficients()
    begin(0)
    pl.semaphore_wait(barrier, GROUPS + 1)

    def edges(ready):
        for way in (True, False):
            halo_copy(ready, way).wait_recv()

    def send_edges(field):
        for way in (True, False):
            halo_copy(field, way).start()

    for way in (True, False):
        raw_copy(0, way).start()
    send_edges(0)
    swap(noise_send, noise_recv, 0, 0)
    begin(1)
    send_edges(1)
    for way in (True, False):
        raw_copy(1, way).start()
    for n in (3, 4, 5, 8, 9, 10, 11):
        loads[n].wait()
    for f in range(2, FIELDS):
        begin(f)
    observations()
    for way in (True, False):
        raw_copy(0, way).wait_recv()
    coefficients(0)
    edges(0)
    send_edges(2)
    forecast(0)
    likelihood()
    for way in (True, False):
        raw_copy(1, way).wait_recv()
    coefficients(1)
    edges(1)
    send_edges(3)
    forecast(1)
    pack(0, state_of, state_send, state_recv)
    swap(state_send, state_recv, 0, 1)
    for f in range(2, FIELDS):
        coefficients(f)
        edges(f)
        begin(f + PAIR)
        send_edges(f + PAIR)
        forecast(f)
    pack(1, state_of, state_send, state_recv)
    swap(state_send, state_recv, 1, 1)
    for chunk in range(CHUNKS):
        coefficients2(chunk)
    observations2()
    unpack_noise(0)
    for f in range(FIELDS, SLOTS):
        edges(f)
        forecast(f)
    pack_late()
    swap_late()
    weigh()
    await_bytes(others(state_recv, 0), sem_in.at[0, 1])
    unpack_state(0)
    for block in range(BLOCKS):
        begin2(0, block)
    average(0)
    for block in range(BLOCKS):
        forecast2(0, block)
    likelihood2()
    pack_back(0)
    swap(back_send, back_recv, 0, 2)
    await_bytes(others(state_recv, 1), sem_in.at[1, 1])
    unpack_state(1)
    for block in range(BLOCKS):
        begin2(1, block)
    weigh2()
    average2(0)
    average(1)
    for block in range(BLOCKS):
        forecast2(1, block)
    add_late()
    sum_late()
    average2(1)
    pack_back(1)
    swap_last()
    pass_means(0)
    finish(0)
    write_means(0)
    for copy in stores(0):
        copy.start()
    pass_means(1)
    write_means(1)
    stores(1)[0].start()
    await_bytes(last.at[pl.ds(0, GROUPS - 1)], sem_in.at[1, 2])
    own_back().wait()
    await_bytes(others(noise_recv, 0), sem_out.at[0, 0])
    await_bytes(late_recv.at[pl.ds(0, GROUPS - 1)], sem_out.at[1, 0])
    for chunk in range(CHUNKS):
        await_bytes(others(state_recv, chunk), sem_out.at[chunk, 1])
    for chunk in range(CHUNKS):
        await_bytes(others(back_send, chunk), sem_out.at[chunk, 2])
        await_bytes(mean_recv2.at[chunk, 0, pl.ds(0, CHIPS - 1)], sem_small_out.at[2 + chunk])
        means_across(chunk).wait_send()
        for copy in stores(chunk):
            copy.wait()
    for way in (True, False):
        for f in range(SLOTS):
            halo_copy(f, way).wait_send()
        for part in range(2):
            raw_copy(part, way).wait_send()
        for chunk in range(CHUNKS):
            for block in range(BLOCKS):
                halo_copy2(chunk, block, way).wait_send()
    for n, ref in enumerate((like_recv, like_recv2)):
        await_bytes(ref.at[pl.ds(0, GROUPS - 1)], sem_small_out.at[n])


def hand_over(ensemble, last, averages, ensemble_out, averages_out, ensemble_v, last_v, averages_v, new_v, sem_in,
              sem_out):
    strips = [pl.ds(STRIPS * f, STRIPS) for f in range(PAIR)]
    into = [pltpu.make_async_copy(last.at[s], last_v.at[s], sem_in.at[f]) for f, s in enumerate(strips)]
    into.append(pltpu.make_async_copy(ensemble, ensemble_v, sem_in.at[PAIR]))
    into.append(pltpu.make_async_copy(averages, averages_v, sem_in.at[PAIR + 1]))
    away = [pltpu.make_async_copy(new_v.at[f], ensemble_out.at[:, PAIR + f], sem_out.at[f]) for f in range(PAIR)]
    away.append(pltpu.make_async_copy(ensemble_v, ensemble_out.at[:, pl.ds(0, PAIR)], sem_out.at[PAIR]))
    away.append(pltpu.make_async_copy(averages_v, averages_out, sem_out.at[PAIR + 1]))
    for copy in into:
        copy.start()
    for f in range(PAIR):
        into[f].wait()

        def loader(g):
            return lambda u: last_v[STRIPS * f + g, :, LANES * u:LANES * (u + 1)]

        for j in range(PER):
            spans = [(WIDE * g, WIDE * j, WIDE, loader(g), PER * WIDE) for g in range(STRIPS)]
            for u in range(COLS // LANES):
                new_v[f, j, :, LANES * u:LANES * (u + 1)] = place(u, spans)
        away[f].start()
        if f == 0:
            for n in (PAIR, PAIR + 1):
                into[n].wait()
                away[n].start()
    for copy in away:
        copy.wait()


def per_device(members, noise, courant, diffusion, obs_loc, observed, obs_var, ancestors):
    f32 = jnp.float32
    anywhere = pl.BlockSpec(memory_space=pl.ANY)
    plane = (ROWS, COLS)
    one = (ROWS, LANES)
    operands = (members, noise, courant, diffusion, obs_loc, observed, obs_var, ancestors)

    def vmem(*shape):
        return pltpu.VMEM(shape, f32)

    scratch = [vmem(PER, PAIR, *plane), vmem(CYCLES, FIELDS, *plane)]
    scratch += [vmem(*a.shape) for a in operands[:4]] + [pltpu.SMEM(a.shape, a.dtype) for a in operands[4:]]
    scratch += [vmem(1, GROUPS, ROWS, PER * SPAN) for _ in range(2)]
    scratch += [vmem(GROUPS, ROWS, PER * WIDE) for _ in range(2)] + [vmem((ROWS + 1) * PAIRS, LANES)]
    scratch += [vmem(CHUNKS, GROUPS, ROWS, PER * SPAN) for _ in range(2)]
    scratch += [vmem(n, GROUPS, ROWS, PER * WIDE) for n in (CHUNKS, 1)]
    scratch += [vmem(SLOTS, PER // 2, *plane) for _ in range(4)]
    scratch += [
        vmem(SLOTS, PER, *plane),
        vmem(SLOTS, PER, *plane),
        vmem(2 + FIELDS, *plane),
        vmem(2 + FIELDS, *plane),
        vmem(2 + FIELDS, *plane),
        vmem(FIELDS, 5, 2 * ROWS, COLS),
        vmem(*plane),
        vmem(CYCLES, *plane),
        vmem(CYCLES, *plane),
        vmem(PER, LANES),
        vmem(ALL, LANES),
        vmem(1, LANES),
        vmem(GROUPS, 1, LANES),
        vmem(CHUNKS, *one),
        vmem(1, PAIRS, *one),
        vmem(CHUNKS, ALL, *one),
        vmem(CHUNKS, BLOCKS, (ROWS + 2 * EDGE) * BLOCK, LANES),
        vmem(CHUNKS, (ROWS + 1) * ALL, LANES),
        vmem(CHUNKS, 5, 2 * ROWS, *one),
        vmem(STRIPS, 2 * ROWS, LANES),
        vmem(3, *one),
        vmem(PAIRS, LANES),
        vmem(2, LANES),
        vmem(GROUPS, 2, LANES),
        vmem(CHUNKS, *one),
        vmem(CHUNKS, 2, CHIPS, *one),
        pltpu.SemaphoreType.DMA((12,)),
        pltpu.SemaphoreType.DMA((CHUNKS, 2)),
        pltpu.SemaphoreType.DMA,
        pltpu.SemaphoreType.DMA((CHUNKS, 3)),
        pltpu.SemaphoreType.DMA((CHUNKS, 3)),
        pltpu.SemaphoreType.DMA((SLOTS, 2)),
        pltpu.SemaphoreType.DMA((SLOTS, 2)),
        pltpu.SemaphoreType.DMA((CHUNKS, BLOCKS, 2)),
        pltpu.SemaphoreType.DMA((CHUNKS, BLOCKS, 2)),
        pltpu.SemaphoreType.DMA((2, 2)),
        pltpu.SemaphoreType.DMA((2, 2)),
        pltpu.SemaphoreType.DMA((6,)),
        pltpu.SemaphoreType.DMA((6,)),
    ]
    results = pl.pallas_call(
        kernel,
        out_shape=(
            jax.ShapeDtypeStruct((PER, PAIR) + plane, f32),
            jax.ShapeDtypeStruct((GROUPS, ROWS, PER * WIDE), f32),
            jax.ShapeDtypeStruct((CYCLES, FIELDS) + plane, f32),
        ),
        in_specs=[anywhere] * 8,
        out_specs=(anywhere,) * 3,
        scratch_shapes=scratch,
        compiler_params=pltpu.CompilerParams(
            collective_id=0, has_side_effects=True, vmem_limit_bytes=60 * 1024 * 1024
        ),
        name="assimilate",
    )(*operands)
    return pl.pallas_call(
        hand_over,
        out_shape=(
            jax.ShapeDtypeStruct((PER, FIELDS) + plane, f32),
            jax.ShapeDtypeStruct((CYCLES, FIELDS) + plane, f32),
        ),
        in_specs=[anywhere] * 3,
        out_specs=(anywhere, anywhere),
        scratch_shapes=[vmem(*r.shape) for r in results] + [vmem(PAIR, PER, *plane)]
        + [pltpu.SemaphoreType.DMA((PAIR + 2,))] * 2,
        compiler_params=pltpu.CompilerParams(vmem_limit_bytes=60 * 1024 * 1024),
        name="hand_over",
    )(*results)


def solution(mesh):
    return jax.shard_map(
        per_device,
        mesh=mesh,
        in_specs=(
            P("dom", None, "tile", None),
            P(None, "dom", None, "tile", None),
            P(None, "tile", None),
            P(None, "tile", None),
            P("tile", None),
            P(None, "tile", None),
            P("tile", None),
            P(None, "tile", None),
        ),
        out_specs=(P("dom", None, "tile", None), P(None, None, "tile", None)),
        check_vma=False,
    )
```

```python
import jax
import jax.numpy as jnp
from jax import lax
from jax.experimental import pallas as pl
from jax.experimental.pallas import tpu as pltpu
from jax.sharding import PartitionSpec as P

MESH = pl.DeviceIdType.MESH
STEPS = 4
CYCLES = 2
FIELDS = 4
PER = 16
GROUPS = 16
CHIPS = 8
ALL = PER * GROUPS
PAIRS = ALL // 2
TILES = 16
ROWS = 8
COLS = 384
LANES = 128
HALF = LANES // 2
NOBS = 64
CHUNKS = 2
PAIR = 2
SLOTS = FIELDS + PAIR
STRIPS = 8
WIDE = COLS // STRIPS
EDGE = STEPS
SPAN = WIDE + 2 * EDGE
BLOCKS = 4
BLOCK = PAIRS // BLOCKS


def half_turn(x):
    return pltpu.roll(x, 4, axis=0)


def place(vector, spans, rows=ROWS):
    lane = lax.broadcasted_iota(jnp.int32, (rows, LANES), 1)
    result = None
    for begin, column, length, load, limit in spans:
        low, high = max(begin, vector * LANES), min(begin + length, (vector + 1) * LANES)
        if low >= high:
            continue
        column = column + low - begin
        low, high = low - vector * LANES, high - vector * LANES
        first = max(column, 0) // LANES
        last = min(column + high - low, limit) - 1
        for u in range(first, last // LANES + 1):
            piece = load(u)
            shift = (low - column + LANES * u) % LANES
            if shift:
                piece = pltpu.roll(piece, shift, axis=1)
            start = max(low, low - column + LANES * u)
            result = piece if result is None else jnp.where(lane >= start, piece, result)
    return result


def kernel(members, noise, courant, diffusion, obs_loc, observed, obs_var, ancestors, out, last, averages,
           out_v, averages_v,
           members_v, noise_v, courant_v, diffusion_v, obs_loc_s, observed_s, obs_var_s, ancestors_s,
           noise_send, noise_recv, late_send, late_recv, late_rows, state_send, state_recv, back_send, back_recv,
           to_north, to_south, from_north, from_south,
           state, result, raw, raw_north, raw_south, coef, obs_weight, obs_mean, obs_rest, partial, weights,
           like_send, like_recv, mean_own,
           noise_pairs, twins, grid2, lone, coef2, windows, obs2, weights2, like_send2, like_recv2,
           mean_send2, mean_recv2,
           sem_load, sem_store, sem_own, sem_out, sem_in, sem_halo_out, sem_halo_in, sem_halo2_out, sem_halo2_in, sem_raw_out,
           sem_raw_in, sem_small_out, sem_small_in):
    me = lax.axis_index("dom")
    tile = lax.axis_index("tile")
    north = lax.rem(tile + TILES - 1, TILES)
    south = lax.rem(tile + 1, TILES)
    strip = lax.rem(me, STRIPS)
    in_pair = lax.div(me, STRIPS)
    chip = lax.div(me, 2)
    core = lax.rem(me, 2)

    def peer(step):
        return lax.rem(me + step, GROUPS)

    barrier = pltpu.get_barrier_semaphore()

    def greet(step, carry):
        pl.semaphore_signal(barrier, inc=1, device_id={"dom": peer(step)}, device_id_type=MESH)
        return carry

    for neighbour in (north, south):
        pl.semaphore_signal(barrier, inc=1, device_id={"tile": neighbour}, device_id_type=MESH)
    lax.fori_loop(1, GROUPS, greet, 0)

    loads = []

    def load(source, target):
        loads.append(pltpu.make_async_copy(source, target, sem_load.at[len(loads)]))
        loads[-1].start()

    for chunk in range(CHUNKS):
        two = pl.ds(PAIR * chunk, PAIR)
        load(noise.at[1, :, two], noise_v.at[1, :, two])
        load(members.at[:, two], members_v.at[:, two])
        load(noise.at[0, :, two], noise_v.at[0, :, two])
    for source, target in ((courant, courant_v), (diffusion, diffusion_v), (obs_loc, obs_loc_s),
                           (observed, observed_s), (obs_var, obs_var_s), (ancestors, ancestors_s)):
        load(source, target)

    upper = lax.broadcasted_iota(jnp.int32, (ROWS, COLS), 0) < 4
    upper1 = lax.broadcasted_iota(jnp.int32, (ROWS, LANES), 0) < 4
    column = lax.broadcasted_iota(jnp.int32, (ROWS, COLS), 1)
    lane8 = lax.broadcasted_iota(jnp.int32, (ROWS, LANES), 1)
    has_north = jnp.where(tile > 0, 1.0, 0.0).astype(jnp.float32)
    has_south = jnp.where(tile < TILES - 1, 1.0, 0.0).astype(jnp.float32)

    def exchange(source_of, target_of, out_sem, in_sem):
        def one(step, carry):
            near = lax.div(step + 1, 2)
            other = peer(jnp.where(lax.rem(step, 2) == 1, near, GROUPS - near))
            pltpu.make_async_remote_copy(
                src_ref=source_of(other), dst_ref=target_of(me), send_sem=out_sem, recv_sem=in_sem,
                device_id={"dom": other}, device_id_type=MESH,
            ).start()
            return carry

        lax.fori_loop(1, GROUPS, one, 0)

    def await_bytes(ref, sem):
        pltpu.make_async_copy(ref, ref, sem).wait()

    def others(ref, chunk):
        return ref.at[chunk, pl.ds(0, GROUPS - 1)]

    def tile_copy(source, target, out_sem, in_sem, southward):
        return pltpu.make_async_remote_copy(
            src_ref=source, dst_ref=target, send_sem=out_sem, recv_sem=in_sem,
            device_id={"tile": south if southward else north}, device_id_type=MESH,
        )

    def halo_copy(field, southward):
        source, target = (to_south, from_north) if southward else (to_north, from_south)
        way = 1 if southward else 0
        return tile_copy(source.at[field], target.at[field], sem_halo_out.at[field, way], sem_halo_in.at[field, way],
                         southward)

    def halo_copy2(chunk, block, southward):
        source, target = (ROWS, 0) if southward else (EDGE, ROWS + EDGE)
        way = 1 if southward else 0
        rows = EDGE * BLOCK
        return tile_copy(grid2.at[chunk, block, pl.ds(source * BLOCK, rows)],
                         grid2.at[chunk, block, pl.ds(target * BLOCK, rows)], sem_halo2_out.at[chunk, block, way],
                         sem_halo2_in.at[chunk, block, way], southward)

    def raw_copy(part, southward):
        rows = pl.ds(3 * part, 3)
        target = raw_north if southward else raw_south
        way = 1 if southward else 0
        return tile_copy(raw.at[rows], target.at[rows], sem_raw_out.at[part, way], sem_raw_in.at[part, way], southward)

    def begin(field):
        def start_of(particle):
            if field < FIELDS:
                return members_v[particle, field] + noise_v[0, particle, field]
            return noise_v[1, particle, field - PAIR]

        def pair(i, carry):
            first, second = 2 * i, 2 * i + 1
            v0, v1 = start_of(first), start_of(second)
            r0, r1 = half_turn(v0), half_turn(v1)
            state[field, first] = r0
            state[field, second] = r1
            to_south[field, i] = jnp.where(upper, r0, v1)
            to_north[field, i] = jnp.where(upper, v0, r1)
            return carry

        lax.fori_loop(0, PER // 2, pair, 0, unroll=2)

    def forecast(field):
        by = field if field < FIELDS else field - PAIR

        def four(q, carry):
            for i in (2 * q, 2 * q + 1):
                top = from_north[field, i] * has_north
                bottom = from_south[field, i] * has_south
                for k, (above, below) in enumerate(((top, half_turn(bottom)), (half_turn(top), bottom))):
                    particle = 2 * i + k
                    r = state[field, particle]
                    x = jnp.concatenate([jnp.where(upper, above, r), jnp.where(upper, r, below)], axis=0)
                    for _ in range(STEPS):
                        x = (coef[by, 0] * x + coef[by, 1] * pltpu.roll(x, 1, axis=0)
                             + coef[by, 2] * pltpu.roll(x, 2 * ROWS - 1, axis=0)
                             + coef[by, 3] * pltpu.roll(x, 1, axis=1)
                             + coef[by, 4] * pltpu.roll(x, COLS - 1, axis=1))
                    v = half_turn(jnp.where(upper, x[ROWS:], x[:ROWS]))
                    result[field, particle] = v
                    if field == 0:
                        miss = v - obs_mean[0]
                        cost = obs_weight[...] * miss * miss + obs_rest[0]
                        cost = cost[:, :LANES] + cost[:, LANES:2 * LANES] + cost[:, 2 * LANES:]
                        partial[pl.ds(particle, 1), :] = jnp.sum(cost, axis=0, keepdims=True)
            return carry

        lax.fori_loop(0, PER // 4, four, 0)

    def pack(chunk, get, outgoing, incoming):
        def one(f, carry):
            for g in range(STRIPS):
                def loader(k):
                    return lambda u: get(k, PAIR * chunk + f, pl.ds(LANES * u, LANES))

                spans = [(SPAN * k, WIDE * g - EDGE, SPAN, loader(k), COLS) for k in range(PER)]
                for j in range(PER * SPAN // LANES):
                    outgoing[chunk, STRIPS * f + g, :, LANES * j:LANES * (j + 1)] = place(j, spans)
            return carry

        lax.fori_loop(0, PAIR, one, 0)
        incoming[chunk, me] = outgoing[chunk, me]

    def swap(outgoing, incoming, chunk, which):
        exchange(lambda other: outgoing.at[chunk, other], lambda mine: incoming.at[chunk, mine],
                 sem_out.at[chunk, which], sem_in.at[chunk, which])

    def pack_late():
        def one(f, carry):
            for g in range(STRIPS):
                def loader(k):
                    return lambda u: result[FIELDS + f, k, :, pl.ds(LANES * u, LANES)]

                spans = [(WIDE * k, WIDE * g, WIDE, loader(k), COLS) for k in range(PER)]
                for j in range(PER * WIDE // LANES):
                    late_send[STRIPS * f + g, :, LANES * j:LANES * (j + 1)] = place(j, spans)
            return carry

        lax.fori_loop(0, PAIR, one, 0)
        late_recv[me] = late_send[me]

    def swap_late():
        exchange(lambda other: late_send.at[other], lambda mine: late_recv.at[mine], sem_out.at[1, 0], sem_in.at[1, 0])

    def add_late():
        await_bytes(late_recv.at[pl.ds(0, GROUPS - 1)], sem_in.at[1, 0])

        def one(s, carry):
            def load_from(u):
                return late_recv[s, :, LANES * u:LANES * (u + 1)]

            for m in range(PER // 2):
                late_rows[pl.ds(PER // 2 * s + m, ROWS, stride=PAIRS), :] = place(
                    0, [(HALF * h + EDGE, WIDE * (2 * m + h), WIDE, load_from, PER * WIDE) for h in range(2)])
            return carry

        lax.fori_loop(0, GROUPS, one, 0, unroll=4)

    def sum_late():
        for r in range(ROWS):
            x = lone[1, ALL * r:ALL * r + PAIRS, :] + late_rows[PAIRS * r:PAIRS * (r + 1), :]
            lone[1, ALL * r:ALL * r + PAIRS, :] = x
            lone[1, ALL * r + PAIRS:ALL * (r + 1), :] = pltpu.roll(x, HALF, axis=1)

    def unpack_noise(chunk):
        await_bytes(others(noise_recv, chunk), sem_in.at[chunk, 0])

        def one(s, carry):
            def load_from(u):
                return noise_recv[chunk, s, :, LANES * u:LANES * (u + 1)]

            for m in range(PER // 2):
                noise_pairs[chunk, PER // 2 * s + m] = place(
                    0, [(HALF * h, SPAN * (2 * m + h), SPAN, load_from, PER * SPAN) for h in range(2)])
            return carry

        lax.fori_loop(0, GROUPS, one, 0, unroll=4)

    def unpack_state(chunk):

        def one(s, carry):
            def load_from(u):
                return state_recv[chunk, s, :, LANES * u:LANES * (u + 1)]

            for k in range(PER):
                twins[chunk, PER * s + k] = place(
                    0, [(HALF * h, SPAN * k, SPAN, load_from, PER * SPAN) for h in range(2)])
            return carry

        lax.fori_loop(0, GROUPS, one, 0, unroll=2)

    def begin2(chunk, block):
        left = lane8 < HALF

        def one(i, carry):
            m = BLOCK * block + i
            old0, old1 = ancestors_s[0, 0, 2 * m], ancestors_s[0, 0, 2 * m + 1]
            v = jnp.where(left, twins[chunk, old0], twins[chunk, old1])
            if chunk == 0:
                v = v + noise_pairs[chunk, m]
            grid2[chunk, block, pl.ds(EDGE * BLOCK + i, ROWS, stride=BLOCK), :] = v
            return carry

        lax.fori_loop(0, BLOCK, one, 0, unroll=8)
        halo_copy2(chunk, block, True).start()
        halo_copy2(chunk, block, False).start()

    def forecast2(chunk, block):
        halo_copy2(chunk, block, True).wait_recv()
        halo_copy2(chunk, block, False).wait_recv()
        high = ROWS + 2 * EDGE

        def tall(n, r):
            return jnp.concatenate([coef2[chunk, n, r]] * (BLOCK // ROWS), axis=0)

        x = [grid2[chunk, block, BLOCK * r:BLOCK * (r + 1), :] for r in range(high)]
        x = [v * has_north if r < EDGE else v * has_south if r >= EDGE + ROWS else v for r, v in enumerate(x)]
        for s in range(1, STEPS + 1):
            new = list(x)
            for r in range(s, high - s):
                new[r] = (tall(0, r) * x[r] + tall(1, r) * x[r - 1] + tall(2, r) * x[r + 1]
                          + tall(3, r) * pltpu.roll(x[r], 1, axis=1) + tall(4, r) * pltpu.roll(x[r], LANES - 1, axis=1))
            x = new
        for r in range(ROWS):
            lone[chunk, ALL * r + BLOCK * block:ALL * r + BLOCK * (block + 1), :] = x[EDGE + r]
            if chunk == 0:
                low = ALL * r + PAIRS + BLOCK * block
                lone[chunk, low:low + BLOCK, :] = pltpu.roll(x[EDGE + r], HALF, axis=1)

    def pack_back(chunk):
        def one(group, carry):
            def loader(j):
                old = ancestors_s[1, 0, PER * group + j]
                tall = lone[chunk, pl.ds((old & 1) * PAIRS + (old >> 1), ROWS, stride=ALL), :]
                return lambda u: tall

            spans = [(WIDE * j, EDGE, WIDE, loader(j), LANES) for j in range(PER)]
            for n in range(PER * WIDE // LANES):
                back_send[chunk, group, :, LANES * n:LANES * (n + 1)] = place(n, spans)
            return carry

        lax.fori_loop(0, GROUPS, one, 0, unroll=4)
        if chunk == 0:
            back_recv[chunk, me] = back_send[chunk, me]
        else:
            own_back().start()

    def own_back():
        return pltpu.make_async_copy(back_send.at[1, me], last.at[me], sem_own)

    def swap_last():
        exchange(lambda other: back_send.at[1, other], lambda mine: last.at[mine], sem_out.at[1, 2], sem_in.at[1, 2])

    def stores(chunk):
        two = pl.ds(PAIR * chunk, PAIR)
        copies = [pltpu.make_async_copy(averages_v.at[:, two], averages.at[:, two], sem_store.at[chunk, 1])]
        if chunk == 0:
            copies.append(pltpu.make_async_copy(out_v, out, sem_store.at[chunk, 0]))
        return copies

    def finish(chunk):
        await_bytes(others(back_recv, chunk), sem_in.at[chunk, 2])

        def one(f, carry):
            def loader(g):
                return lambda u: back_recv[chunk, STRIPS * f + g, :, LANES * u:LANES * (u + 1)]

            for j in range(PER):
                spans = [(WIDE * g, WIDE * j, WIDE, loader(g), PER * WIDE) for g in range(STRIPS)]
                for u in range(COLS // LANES):
                    out_v[j, f, :, LANES * u:LANES * (u + 1)] = place(u, spans)
            return carry

        lax.fori_loop(0, PAIR, one, 0)

    lane = lax.broadcasted_iota(jnp.int32, (PER, LANES), 1)
    line = lax.broadcasted_iota(jnp.int32, (PER, LANES), 0)

    def likelihood():
        total = -0.5 * jnp.sum(partial[...], axis=1, keepdims=True)
        row = jnp.sum(jnp.where(lane == line, total, 0.0), axis=0, keepdims=True)
        like_send[...] = row
        like_recv[me] = row
        exchange(lambda other: like_send, lambda mine: like_recv.at[mine], sem_small_out.at[0], sem_small_in.at[0])

    def weigh():
        await_bytes(like_recv.at[pl.ds(0, GROUPS - 1)], sem_small_in.at[0])
        everyone = like_recv[...]
        known = lax.broadcasted_iota(jnp.int32, (GROUPS, 1, LANES), 2) < PER
        peak = jnp.max(jnp.where(known, everyone, -3.0e38), axis=0)
        peak = jnp.max(peak, axis=1, keepdims=True)
        shifted = jnp.where(known, jnp.exp(jnp.where(known, everyone - peak[None], 0.0)), 0.0)
        total = jnp.sum(jnp.sum(shifted, axis=0), axis=1, keepdims=True)
        weight = shifted / total[None]
        for g in range(GROUPS):
            own = jnp.sum(jnp.where(lane == line, weight[g], 0.0), axis=1, keepdims=True)
            weights[PER * g:PER * (g + 1), :] = jnp.broadcast_to(own, (PER, LANES))

    def average(chunk):
        def add(q, sums):
            return tuple(s + weights[pl.ds(4 * q + k, 1), :] * twins[chunk, 4 * q + k] for k, s in enumerate(sums))

        sums = lax.fori_loop(0, ALL // 4, add, (jnp.zeros((ROWS, LANES), jnp.float32),) * 4, unroll=4)
        mean_own[chunk] = (sums[0] + sums[1]) + (sums[2] + sums[3])

    place2 = lax.broadcasted_iota(jnp.int32, (PAIRS, LANES), 1)
    line2 = lax.broadcasted_iota(jnp.int32, (PAIRS, LANES), 0)

    def likelihood2():
        cost = jnp.zeros((PAIRS, LANES), jnp.float32)
        for r in range(ROWS):
            miss = lone[0, ALL * r:ALL * r + PAIRS, :] - obs2[1, r:r + 1]
            cost = cost + obs2[0, r:r + 1] * miss * miss + obs2[2, r:r + 1]
        for h in range(2):
            side = (place2 < HALF) if h == 0 else (place2 >= HALF)
            total = -0.5 * jnp.sum(jnp.where(side, cost, 0.0), axis=1, keepdims=True)
            row = jnp.sum(jnp.where(place2 == line2, total, 0.0), axis=0, keepdims=True)
            like_send2[h:h + 1, :] = row
        like_recv2[me] = like_send2[...]
        exchange(lambda other: like_send2, lambda mine: like_recv2.at[mine], sem_small_out.at[1], sem_small_in.at[1])

    def weigh2():
        await_bytes(like_recv2.at[pl.ds(0, GROUPS - 1)], sem_small_in.at[1])
        total = like_recv2[0]
        for g in range(1, GROUPS):
            total = total + like_recv2[g]
        peak = jnp.max(jnp.max(total, axis=0, keepdims=True), axis=1, keepdims=True)
        shifted = jnp.exp(total - peak)
        weight = shifted / jnp.sum(jnp.sum(shifted, axis=0, keepdims=True), axis=1, keepdims=True)
        sides = [jnp.sum(jnp.where(place2 == line2, weight[h:h + 1], 0.0), axis=1, keepdims=True) for h in range(2)]
        weights2[...] = jnp.where(place2 < HALF, sides[0], sides[1])

    def average2(chunk):
        for r in range(ROWS):
            part = weights2[...] * lone[chunk, ALL * r:ALL * r + PAIRS, :]
            mean_send2[chunk, r:r + 1, :] = jnp.sum(part, axis=0, keepdims=True)
        total = mean_send2[chunk]
        total = total + pltpu.roll(total, HALF, axis=1)
        total = jnp.where(lane8 < HALF, mean_own[chunk], total)
        mean_send2[chunk] = total
        mean_recv2[chunk, core, chip] = total

        def one(step, carry):
            pltpu.make_async_remote_copy(
                src_ref=mean_send2.at[chunk], dst_ref=mean_recv2.at[chunk, core, chip],
                send_sem=sem_small_out.at[2 + chunk], recv_sem=sem_small_in.at[2 + chunk],
                device_id={"dom": 2 * lax.rem(chip + step, CHIPS) + core}, device_id_type=MESH,
            ).start()
            return carry

        lax.fori_loop(1, CHIPS, one, 0)

    def means_across(chunk):
        return pltpu.make_async_remote_copy(
            src_ref=mean_recv2.at[chunk, core], dst_ref=mean_recv2.at[chunk, core],
            send_sem=sem_small_out.at[4 + chunk], recv_sem=sem_small_in.at[4 + chunk],
            device_id={"dom": 2 * chip + 1 - core}, device_id_type=MESH,
        )

    def pass_means(chunk):
        await_bytes(mean_recv2.at[chunk, 0, pl.ds(0, CHIPS - 1)], sem_small_in.at[2 + chunk])
        means_across(chunk).start()

    def write_means(chunk):
        means_across(chunk).wait_recv()
        for c in range(CYCLES):
            for f in range(PAIR):
                def loader(g):
                    return lambda u: mean_recv2[chunk, g % 2, (STRIPS * f + g) // 2]

                spans = [(WIDE * g, HALF * c + EDGE, WIDE, loader(g), LANES) for g in range(STRIPS)]
                for u in range(COLS // LANES):
                    averages_v[c, PAIR * chunk + f, :, LANES * u:LANES * (u + 1)] = place(u, spans)

    def edge_coefficients():
        for m in range(2):
            raw[m] = half_turn(courant_v[m])
        for f in range(FIELDS):
            raw[2 + f] = half_turn(diffusion_v[f])

    def coefficients(field):
        def sixteen(m):
            mid = raw[m]
            return jnp.concatenate([jnp.where(upper, raw_north[m], mid), jnp.where(upper, mid, raw_south[m])], axis=0)

        inside = jnp.concatenate([jnp.where(upper, has_north, 1.0), jnp.where(upper, 1.0, has_south)], axis=0)
        column2 = jnp.concatenate([column, column], axis=0)
        cx, cy, d = sixteen(0), sixteen(1), sixteen(2 + field)
        coef[field, 0] = inside * (1.0 - jnp.abs(cx) - jnp.abs(cy) - 4.0 * d)
        coef[field, 1] = inside * (jnp.maximum(cx, 0.0) + d)
        coef[field, 2] = inside * (d - jnp.minimum(cx, 0.0))
        coef[field, 3] = jnp.where(column2 > 0, inside * (jnp.maximum(cy, 0.0) + d), 0.0)
        coef[field, 4] = jnp.where(column2 < COLS - 1, inside * (d - jnp.minimum(cy, 0.0)), 0.0)

    def window(get, rows):
        for g in range(STRIPS):
            spans = [(HALF * h, WIDE * g - EDGE, SPAN, lambda u: get(pl.ds(LANES * u, LANES)), COLS) for h in range(2)]
            windows[g, :rows] = place(0, spans, rows)
        return windows[strip, :rows]

    def coefficients2(chunk):
        lane16 = lax.broadcasted_iota(jnp.int32, (2 * ROWS, LANES), 1)
        used = lax.rem(lane16, HALF) < SPAN
        for n in range(5):
            here = window(lambda cols: coef[PAIR * chunk + in_pair, n, :, cols], 2 * ROWS)
            here = jnp.where(used, here, 0.0)
            for r in range(2 * ROWS):
                coef2[chunk, n, r] = jnp.broadcast_to(here[r:r + 1], (ROWS, LANES))

    def observations():
        cell = lax.broadcasted_iota(jnp.int32, (ROWS, COLS), 0) * COLS + column
        zero = jnp.zeros((ROWS, COLS), jnp.float32)

        def gather(k, sums):
            here = cell == obs_loc_s[0, k]
            precision = jnp.where(here, 1.0 / jnp.full((1, COLS), obs_var_s[0, k], jnp.float32), 0.0)
            return (sums[0] + precision,) + tuple(sums[1 + c] + precision * observed_s[c, 0, k] for c in range(CYCLES))

        sums = lax.fori_loop(0, NOBS, gather, (zero,) * (1 + CYCLES), unroll=8)
        obs_weight[...] = sums[0]
        seen = sums[0] > 0.0
        means = []
        for c in range(CYCLES):
            means.append(jnp.where(seen, sums[1 + c] / jnp.where(seen, sums[0], 1.0), 0.0))
            obs_mean[c] = means[c]

        def rest(k, sums):
            here = cell == obs_loc_s[0, k]
            precision = jnp.where(here, 1.0 / jnp.full((1, COLS), obs_var_s[0, k], jnp.float32), 0.0)
            return tuple(sums[c] + precision * (observed_s[c, 0, k] - means[c]) * (observed_s[c, 0, k] - means[c])
                         for c in range(CYCLES))

        sums = lax.fori_loop(0, NOBS, rest, (zero,) * CYCLES, unroll=8)
        for c in range(CYCLES):
            obs_rest[c] = sums[c]

    def observations2():
        inner = lax.rem(lane8, HALF)
        own = (inner >= EDGE) & (inner < EDGE + WIDE)
        first = jnp.where(in_pair == 0, 1.0, 0.0).astype(jnp.float32)
        obs2[0] = jnp.where(own, window(lambda cols: obs_weight[:, cols], ROWS), 0.0) * first
        obs2[1] = window(lambda cols: obs_mean[1, :, cols], ROWS)
        obs2[2] = jnp.where(own, window(lambda cols: obs_rest[1, :, cols], ROWS), 0.0) * first

    def noise_of(k, field, cols):
        return noise_v[1, k, field, :, cols]

    def state_of(k, field, cols):
        return result[field, k, :, cols]

    loads[0].wait()
    pack(0, noise_of, noise_send, noise_recv)
    for n in (1, 2, 6, 7):
        loads[n].wait()
    edge_coefficients()
    begin(0)
    pl.semaphore_wait(barrier, GROUPS + 1)

    def edges(ready):
        for way in (True, False):
            halo_copy(ready, way).wait_recv()

    def send_edges(field):
        for way in (True, False):
            halo_copy(field, way).start()

    for way in (True, False):
        raw_copy(0, way).start()
    send_edges(0)
    swap(noise_send, noise_recv, 0, 0)
    begin(1)
    send_edges(1)
    for way in (True, False):
        raw_copy(1, way).start()
    for n in (3, 4, 5, 8, 9, 10, 11):
        loads[n].wait()
    for f in range(2, FIELDS):
        begin(f)
    observations()
    for way in (True, False):
        raw_copy(0, way).wait_recv()
    coefficients(0)
    edges(0)
    send_edges(2)
    forecast(0)
    likelihood()
    for way in (True, False):
        raw_copy(1, way).wait_recv()
    coefficients(1)
    edges(1)
    send_edges(3)
    forecast(1)
    pack(0, state_of, state_send, state_recv)
    swap(state_send, state_recv, 0, 1)
    for f in range(2, FIELDS):
        coefficients(f)
        edges(f)
        begin(f + PAIR)
        send_edges(f + PAIR)
        forecast(f)
    pack(1, state_of, state_send, state_recv)
    swap(state_send, state_recv, 1, 1)
    for chunk in range(CHUNKS):
        coefficients2(chunk)
    observations2()
    unpack_noise(0)
    for f in range(FIELDS, SLOTS):
        edges(f)
        forecast(f)
    pack_late()
    swap_late()
    weigh()
    await_bytes(others(state_recv, 0), sem_in.at[0, 1])
    unpack_state(0)
    for block in range(BLOCKS):
        begin2(0, block)
    average(0)
    for block in range(BLOCKS):
        forecast2(0, block)
    likelihood2()
    await_bytes(others(state_recv, 1), sem_in.at[1, 1])
    unpack_state(1)
    for block in range(BLOCKS):
        begin2(1, block)
    pack_back(0)
    swap(back_send, back_recv, 0, 2)
    weigh2()
    average2(0)
    average(1)
    for block in range(BLOCKS):
        forecast2(1, block)
    add_late()
    sum_late()
    average2(1)
    pack_back(1)
    swap_last()
    pass_means(0)
    finish(0)
    write_means(0)
    for copy in stores(0):
        copy.start()
    pass_means(1)
    write_means(1)
    stores(1)[0].start()
    await_bytes(last.at[pl.ds(0, GROUPS - 1)], sem_in.at[1, 2])
    own_back().wait()
    await_bytes(others(noise_recv, 0), sem_out.at[0, 0])
    await_bytes(late_recv.at[pl.ds(0, GROUPS - 1)], sem_out.at[1, 0])
    for chunk in range(CHUNKS):
        await_bytes(others(state_recv, chunk), sem_out.at[chunk, 1])
    for chunk in range(CHUNKS):
        await_bytes(others(back_send, chunk), sem_out.at[chunk, 2])
        await_bytes(mean_recv2.at[chunk, 0, pl.ds(0, CHIPS - 1)], sem_small_out.at[2 + chunk])
        means_across(chunk).wait_send()
        for copy in stores(chunk):
            copy.wait()
    for way in (True, False):
        for f in range(SLOTS):
            halo_copy(f, way).wait_send()
        for part in range(2):
            raw_copy(part, way).wait_send()
        for chunk in range(CHUNKS):
            for block in range(BLOCKS):
                halo_copy2(chunk, block, way).wait_send()
    for n, ref in enumerate((like_recv, like_recv2)):
        await_bytes(ref.at[pl.ds(0, GROUPS - 1)], sem_small_out.at[n])


def hand_over(ensemble, last, averages, ensemble_out, averages_out, ensemble_v, last_v, averages_v, new_v, sem_in,
              sem_out):
    strips = [pl.ds(STRIPS * f, STRIPS) for f in range(PAIR)]
    into = [pltpu.make_async_copy(last.at[s], last_v.at[s], sem_in.at[f]) for f, s in enumerate(strips)]
    into.append(pltpu.make_async_copy(ensemble, ensemble_v, sem_in.at[PAIR]))
    into.append(pltpu.make_async_copy(averages, averages_v, sem_in.at[PAIR + 1]))
    away = [pltpu.make_async_copy(new_v.at[f], ensemble_out.at[:, PAIR + f], sem_out.at[f]) for f in range(PAIR)]
    away.append(pltpu.make_async_copy(ensemble_v, ensemble_out.at[:, pl.ds(0, PAIR)], sem_out.at[PAIR]))
    away.append(pltpu.make_async_copy(averages_v, averages_out, sem_out.at[PAIR + 1]))
    for copy in into:
        copy.start()
    for f in range(PAIR):
        into[f].wait()

        def loader(g):
            return lambda u: last_v[STRIPS * f + g, :, LANES * u:LANES * (u + 1)]

        for j in range(PER):
            spans = [(WIDE * g, WIDE * j, WIDE, loader(g), PER * WIDE) for g in range(STRIPS)]
            for u in range(COLS // LANES):
                new_v[f, j, :, LANES * u:LANES * (u + 1)] = place(u, spans)
        away[f].start()
        if f == 0:
            for n in (PAIR, PAIR + 1):
                into[n].wait()
                away[n].start()
    for copy in away:
        copy.wait()


def per_device(members, noise, courant, diffusion, obs_loc, observed, obs_var, ancestors):
    f32 = jnp.float32
    anywhere = pl.BlockSpec(memory_space=pl.ANY)
    plane = (ROWS, COLS)
    one = (ROWS, LANES)
    operands = (members, noise, courant, diffusion, obs_loc, observed, obs_var, ancestors)

    def vmem(*shape):
        return pltpu.VMEM(shape, f32)

    scratch = [vmem(PER, PAIR, *plane), vmem(CYCLES, FIELDS, *plane)]
    scratch += [vmem(*a.shape) for a in operands[:4]] + [pltpu.SMEM(a.shape, a.dtype) for a in operands[4:]]
    scratch += [vmem(1, GROUPS, ROWS, PER * SPAN) for _ in range(2)]
    scratch += [vmem(GROUPS, ROWS, PER * WIDE) for _ in range(2)] + [vmem((ROWS + 1) * PAIRS, LANES)]
    scratch += [vmem(CHUNKS, GROUPS, ROWS, PER * SPAN) for _ in range(2)]
    scratch += [vmem(n, GROUPS, ROWS, PER * WIDE) for n in (CHUNKS, 1)]
    scratch += [vmem(SLOTS, PER // 2, *plane) for _ in range(4)]
    scratch += [
        vmem(SLOTS, PER, *plane),
        vmem(SLOTS, PER, *plane),
        vmem(2 + FIELDS, *plane),
        vmem(2 + FIELDS, *plane),
        vmem(2 + FIELDS, *plane),
        vmem(FIELDS, 5, 2 * ROWS, COLS),
        vmem(*plane),
        vmem(CYCLES, *plane),
        vmem(CYCLES, *plane),
        vmem(PER, LANES),
        vmem(ALL, LANES),
        vmem(1, LANES),
        vmem(GROUPS, 1, LANES),
        vmem(CHUNKS, *one),
        vmem(1, PAIRS, *one),
        vmem(CHUNKS, ALL, *one),
        vmem(CHUNKS, BLOCKS, (ROWS + 2 * EDGE) * BLOCK, LANES),
        vmem(CHUNKS, (ROWS + 1) * ALL, LANES),
        vmem(CHUNKS, 5, 2 * ROWS, *one),
        vmem(STRIPS, 2 * ROWS, LANES),
        vmem(3, *one),
        vmem(PAIRS, LANES),
        vmem(2, LANES),
        vmem(GROUPS, 2, LANES),
        vmem(CHUNKS, *one),
        vmem(CHUNKS, 2, CHIPS, *one),
        pltpu.SemaphoreType.DMA((12,)),
        pltpu.SemaphoreType.DMA((CHUNKS, 2)),
        pltpu.SemaphoreType.DMA,
        pltpu.SemaphoreType.DMA((CHUNKS, 3)),
        pltpu.SemaphoreType.DMA((CHUNKS, 3)),
        pltpu.SemaphoreType.DMA((SLOTS, 2)),
        pltpu.SemaphoreType.DMA((SLOTS, 2)),
        pltpu.SemaphoreType.DMA((CHUNKS, BLOCKS, 2)),
        pltpu.SemaphoreType.DMA((CHUNKS, BLOCKS, 2)),
        pltpu.SemaphoreType.DMA((2, 2)),
        pltpu.SemaphoreType.DMA((2, 2)),
        pltpu.SemaphoreType.DMA((6,)),
        pltpu.SemaphoreType.DMA((6,)),
    ]
    results = pl.pallas_call(
        kernel,
        out_shape=(
            jax.ShapeDtypeStruct((PER, PAIR) + plane, f32),
            jax.ShapeDtypeStruct((GROUPS, ROWS, PER * WIDE), f32),
            jax.ShapeDtypeStruct((CYCLES, FIELDS) + plane, f32),
        ),
        in_specs=[anywhere] * 8,
        out_specs=(anywhere,) * 3,
        scratch_shapes=scratch,
        compiler_params=pltpu.CompilerParams(
            collective_id=0, has_side_effects=True, vmem_limit_bytes=60 * 1024 * 1024
        ),
        name="assimilate",
    )(*operands)
    return pl.pallas_call(
        hand_over,
        out_shape=(
            jax.ShapeDtypeStruct((PER, FIELDS) + plane, f32),
            jax.ShapeDtypeStruct((CYCLES, FIELDS) + plane, f32),
        ),
        in_specs=[anywhere] * 3,
        out_specs=(anywhere, anywhere),
        scratch_shapes=[vmem(*r.shape) for r in results] + [vmem(PAIR, PER, *plane)]
        + [pltpu.SemaphoreType.DMA((PAIR + 2,))] * 2,
        compiler_params=pltpu.CompilerParams(vmem_limit_bytes=60 * 1024 * 1024),
        name="hand_over",
    )(*results)


def solution(mesh):
    return jax.shard_map(
        per_device,
        mesh=mesh,
        in_specs=(
            P("dom", None, "tile", None),
            P(None, "dom", None, "tile", None),
            P(None, "tile", None),
            P(None, "tile", None),
            P("tile", None),
            P(None, "tile", None),
            P("tile", None),
            P(None, "tile", None),
        ),
        out_specs=(P("dom", None, "tile", None), P(None, None, "tile", None)),
        check_vma=False,
    )
```
